32 devices in a mesh: rows: 16 (over z, y, x), heads: 2 (over core).
Axes of the slice: x: 2, y: 2, z: 4, core: 2. Of those that a mesh axis runs over, the one named last changes fastest.
Arguments:
- token_ids: int32 [32, 1024], P('rows'), may hold values from 0 to 30521
- bounds: int32 [32, 2], P('rows'), may hold values from 1 to 1024, as said below
- micro_batch: int32 [32], P('rows'), may hold values from 0 to 1, as said below
- owners: int32 [47], replicated, may hold values from 0 to 15, as said below
- step_count: int32 [1], replicated, may hold values from 1 to 20
- word_table: bfloat16 [30522, 128], replicated, may hold values from -6 to 6
- conv_weight: bfloat16 [384, 512], replicated, may hold values from -0.3125 to 0.3125
- embed_extra: float32 [1026, 512], replicated, may hold values from -3 to 3
- teacher_entry: bfloat16 [512, 1024], replicated, may hold values from -0.25 to 0.25
- teacher_project: bfloat16 [1024, 3, 1024], P(None, None, 'heads'), may hold values from -0.1875 to 0.1875
- teacher_mixer: bfloat16 [1024, 1024], P('heads'), may hold values from -0.75 to 0.75
- teacher_expand: bfloat16 [1024, 4096], P(None, 'heads'), may hold values from -0.1875 to 0.1875
- teacher_shrink: bfloat16 [4096, 1024], P('heads'), may hold values from -0.09375 to 0.09375
- teacher_leave: bfloat16 [1024, 512], replicated, may hold values from -0.1875 to 0.1875
- teacher_norms: float32 [2, 3584], replicated, may hold values from 0.1 to 1.9
- tile_weight: float32 [64, 128, 128], P('rows'), may hold values from -0.375 to 0.375
- tile_first: float32 [64, 128, 128], P('rows'), may hold values from -3.8146973e-05 to 3.8146973e-05
- tile_second: float32 [64, 128, 128], P('rows'), may hold values from 1.6178968e-12 to 2.5886349e-11
- small_weight: float32 [2, 1280], replicated, may hold values from 0.5 to 1.5
- small_first: float32 [2, 1280], replicated, may hold values from -0.00015258789 to 0.00015258789
- small_second: float32 [2, 1280], replicated, may hold values from 2.5886349e-11 to 4.1418158e-10
Outputs:
- total_loss: float32 [], replicated
- gradient_norm: float32 [], replicated
- updated_tiles: float32 [64, 128, 128], P('rows')
- tile_moment: float32 [64, 128, 128], P('rows')
- tile_square: float32 [64, 128, 128], P('rows')
- updated_small: float32 [2, 1280], replicated
- small_moment: float32 [2, 1280], replicated
- small_square: float32 [2, 1280], replicated
- small_gradient: float32 [2, 1280], replicated
The draws below stay inside these ranges and needn't reach their ends.
Inputs may be any that keep to these rules, and one draw needn't show every extreme that they name: bounds[r,1] is row r's valid length, from 512 up to 1024, and row 0 has length 1024; bounds[r,0] is where its second segment starts, 1 or more and below bounds[r,1]. `micro_batch`: rows 0 to 1 belong to micro-batches 0 to 1 in order. `owners`: no owner holds more than 4 tiles, and some owner holds exactly 4.
All inputs are finite; a program needn't handle non-finite values.
Results may differ from the reference program's by a relative error of at most 0.0061.
Values may be sent and summed in bfloat16 or wider, within the bound.
A program may use at most 192 MiB of HBM per device.

```python
import math
import jax
import jax.numpy as jnp
import numpy as np
from jax import lax

VOCAB = 30522
EMB = 128
HID = 512
TW = 1024
THEADS = 4
THD = 256
TFF = 4096
SW = 128
SHEADS = 4
SHD = 32
SFF = 512
NFFN = 4
LEN = 1024
NMB = 2
SLOTS = 4
ROWS = 32
NTILE = 47
SMALL = 1280
P_ALL = 772608
N_ROWS = 16


def draw_bounds(key, part):
    first_key, second_key = jax.random.split(key)
    lengths = jax.random.randint(first_key, (ROWS,), LEN // 2, LEN + 1)
    lengths = lengths.at[0].set(LEN)
    offsets = jax.random.randint(second_key, (ROWS,), 0, 1 << 20)
    starts = 1 + offsets % (lengths - 1)
    return jnp.stack([starts, lengths], 1).astype(jnp.int32)


def draw_micro_batch(key, part):
    batch_ids = jax.random.randint(key, (ROWS,), 0, NMB)
    batch_ids = batch_ids.at[:NMB].set(jnp.arange(NMB))
    return batch_ids.astype(jnp.int32)


def draw_owners(key, part):
    first_key, second_key, third_key = jax.random.split(key, 3)
    busiest = jax.random.randint(first_key, (), 0, N_ROWS)
    places = jax.random.permutation(second_key, (N_ROWS - 1) * SLOTS)[:NTILE - SLOTS]
    others = places // SLOTS
    others = others + (others >= busiest).astype(others.dtype)
    owner_list = jnp.concatenate([jnp.full((SLOTS,), busiest, others.dtype), others])
    return jax.random.permutation(third_key, owner_list).astype(jnp.int32)


def with_ends(values, rng, low, high):
    place = [jax.random.randint(jax.random.fold_in(rng, axis), (), 0, length) for axis, length in enumerate(values.shape)]
    main_axis = values.shape.index(max(values.shape))
    next_to = place[:main_axis] + [(place[main_axis] + 1) % values.shape[main_axis]] + place[main_axis + 1:]
    return values.at[tuple(place)].set(low).at[tuple(next_to)].set(high)


def steps_of(stream_key, extent, cuts, least, top_value):
    gain = 1.0
    for dim, blocks in cuts:
        draws = jax.random.uniform(jax.random.fold_in(jax.random.fold_in(stream_key, 6), dim), (blocks,), jnp.float32, least / len(cuts), top_value / len(cuts))
        gain = gain * jnp.repeat(jnp.exp(draws), extent[dim] // blocks).reshape((-1,) + (1,) * (len(extent) - 1 - dim))
    return gain


def rank_table(number_of, lean):
    weights = [(1 << 20) // math.isqrt(standing ** lean) + 1 for standing in range(1, number_of + 1)]
    scale = 1 + sum(weights) // (1 << 30)
    return np.cumsum(np.array([max(1, weight // scale) for weight in weights]))


def skewed_ids(key, dims, count, slope):
    listing = rank_table(count, slope)
    pick = jax.random.randint(jax.random.fold_in(key, 1), dims, 0, int(listing[count - 1]))
    rank = jnp.searchsorted(jnp.asarray(listing, jnp.int32), pick, side="right")
    return jax.random.permutation(jax.random.fold_in(key, 2), count)[rank].astype(jnp.int32)


def bell_draw(stream_key, extent, scale, limit, cuts=(), kind=jnp.bfloat16):
    gain = steps_of(stream_key, extent, cuts, -0.22, 0.18) if cuts else 1.0
    drawn = jax.random.normal(stream_key, extent, jnp.float32) * scale * gain
    return jnp.minimum(jnp.maximum(drawn, -limit), limit).astype(kind)


def setup_inputs(seed: int = 0) -> dict:
    seeds = jax.random.split(jax.random.key(seed), 22)
    return {
        "token_ids": with_ends(skewed_ids(seeds[0], (ROWS, LEN), VOCAB, 2), jax.random.fold_in(seeds[0], 3), 0, VOCAB - 1).astype(jnp.int32),
        "bounds": draw_bounds(jax.random.fold_in(seeds[21], 71), 0),
        "micro_batch": draw_micro_batch(jax.random.fold_in(seeds[21], 71), 0),
        "owners": draw_owners(jax.random.fold_in(seeds[21], 71), 0),
        "step_count": jax.random.randint(seeds[4], (1,), 1, 21).astype(jnp.int32),
        "word_table": bell_draw(seeds[5], (VOCAB, EMB), 1.0, 6.0),
        "conv_weight": bell_draw(seeds[6], (3 * EMB, HID), (3 * EMB) ** -0.5, 0.3125),
        "embed_extra": bell_draw(seeds[7], (LEN + 2, HID), 0.5, 3.0, (), jnp.float32),
        "teacher_entry": bell_draw(seeds[8], (HID, TW), HID ** -0.5, 0.25),
        "teacher_project": bell_draw(seeds[9], (TW, 3, TW), TW ** -0.5, 0.1875, ((2, 2),)),
        "teacher_mixer": bell_draw(seeds[10], (TW, TW), (TW // 16) ** -0.5, 0.75, ((0, 2),)),
        "teacher_expand": bell_draw(seeds[11], (TW, TFF), TW ** -0.5, 0.1875, ((1, 2),)),
        "teacher_shrink": bell_draw(seeds[12], (TFF, TW), TFF ** -0.5, 0.09375, ((0, 2),)),
        "teacher_leave": bell_draw(seeds[13], (TW, HID), TW ** -0.5, 0.1875),
        "teacher_norms": jnp.clip(1.0 + 0.18 * jax.random.normal(seeds[14], (2, 3 * TW + HID), jnp.float32), 0.1, 1.9),
        "tile_weight": bell_draw(seeds[15], (N_ROWS * SLOTS, SW, SW), (2 * SW) ** -0.5, 0.375, ((0, 16),), jnp.float32),
        "tile_first": bell_draw(seeds[16], (N_ROWS * SLOTS, SW, SW), (0.00555 * P_ALL ** -0.5), 3.814697265625e-05, ((0, 16),), jnp.float32),
        "tile_second": jnp.clip(jnp.exp(math.log(2.588634862021877e-11) - 2.7725887 * jax.random.uniform(seeds[17], (N_ROWS * SLOTS, SW, SW), jnp.float32) ** steps_of(seeds[17], (N_ROWS * SLOTS, SW, SW), ((0, 16),), -0.2, 0.2)), 1.617896788763673e-12, 2.588634862021877e-11),
        "small_weight": jnp.clip(jax.random.uniform(seeds[18], (2, SMALL), jnp.float32, 0.5, 1.5), 0.5, 1.5),
        "small_first": bell_draw(seeds[19], (2, SMALL), (0.0222 * P_ALL ** -0.5), 0.00015258789, (), jnp.float32),
        "small_second": jnp.clip(jnp.exp(jax.random.uniform(seeds[20], (2, SMALL), jnp.float32, math.log(2.588634862021877e-11), math.log(4.141815779235003e-10))), 2.588634862021877e-11, 4.141815779235003e-10),
    }


PRECISE = lax.Precision.HIGHEST
NORM_EPSILON = 1e-05
CLIP_NORM = 0.05
LEARN_RATE = 0.1
BETA_FIRST = 0.9
BETA_SECOND = 0.999
ADAM_EPSILON = 1e-08
WEIGHT_DECAY = 0.01
MASKED_SCORE = -1e+30

@jax.custom_vjp
def low(v):
    return lax.optimization_barrier(v.astype(jnp.bfloat16)).astype(jnp.float32)

@jax.custom_vjp
def low_back(v):
    return v

def low_keep(v):
    return (low(v), None)

def low_pass(kept, grad):
    return (grad,)

def back_keep(v):
    return (v, None)

def back_low(kept, grad):
    return (low(grad),)
low.defvjp(low_keep, low_pass)
low_back.defvjp(back_keep, back_low)

def product(left, right):
    return jnp.dot(left, right, precision=PRECISE)

def rounded_product(left, right):
    return low_back(product(left, right))

def layer_norm(values, gain_row, bias_row):
    center = values - lax.optimization_barrier(jnp.mean(values, -1, keepdims=True))
    spread = lax.optimization_barrier(jnp.mean(center * center, -1, keepdims=True))
    return center * lax.rsqrt(spread + NORM_EPSILON) * gain_row + bias_row

def masked_scores(scores, valid_key):
    return jnp.where(valid_key[None, None, :], scores, MASKED_SCORE)

def normalize(scores):
    return scores - jax.nn.logsumexp(scores, -1, keepdims=True)

def embed(row_ids, row_bound, word_table, conv_weight, embed_extra):
    length = row_ids.shape[0]
    table_rows = word_table[row_ids].astype(jnp.float32)
    blank_row = jnp.zeros((1, table_rows.shape[1]), jnp.float32)
    after_rows = jnp.concatenate([table_rows[1:], blank_row], 0)
    before = jnp.concatenate([blank_row, table_rows[:-1]], 0)
    trigram = jnp.concatenate([after_rows, table_rows, before], 1)
    places = jnp.arange(length, dtype=jnp.int32)
    segment = (places >= row_bound[0]).astype(jnp.int32)
    return product(trigram, conv_weight.astype(jnp.float32)) + embed_extra[:length] + embed_extra[length + segment]

def teacher(inputs, valid_key, entry_w, project_w, mixer_w, expand_w, shrink_w, leave_w, norms):
    length = inputs.shape[0]
    breadth = entry_w.shape[1]
    gain_row, bias_row = (norms[0], norms[1])
    hidden = layer_norm(product(low(inputs), entry_w), gain_row[:breadth], bias_row[:breadth])
    triple = low(jnp.einsum('ld,dcf->lcf', low(hidden), project_w, precision=PRECISE))
    queries = triple[:, 0].reshape(length, THEADS, THD)
    key_rows = triple[:, 1].reshape(length, THEADS, THD)
    value_rows = triple[:, 2].reshape(length, THEADS, THD)
    scores = jnp.einsum('qhd,khd->hqk', queries, key_rows, precision=PRECISE) * THD ** (-0.5)
    log_weight = normalize(masked_scores(scores, valid_key))
    context = low(jnp.einsum('hqk,khd->qhd', low(jnp.exp(log_weight)), value_rows, precision=PRECISE).reshape(length, breadth))
    first_out = layer_norm(product(context, mixer_w) + hidden, gain_row[breadth:2 * breadth], bias_row[breadth:2 * breadth])
    inner_out = low(jax.nn.gelu(product(low(first_out), expand_w), approximate=False))
    second_out = layer_norm(product(inner_out, shrink_w) + first_out, gain_row[2 * breadth:3 * breadth], bias_row[2 * breadth:3 * breadth])
    feature = layer_norm(product(low(second_out), leave_w) + inputs, gain_row[3 * breadth:], bias_row[3 * breadth:])
    return (feature, low(log_weight).astype(jnp.bfloat16))

def assemble(tile_set):
    breadth = tile_set.shape[1]
    rows_in = HID // breadth
    rows_ff = SFF // breadth
    entry_w = tile_set[:rows_in].reshape(HID, breadth)
    value_w = tile_set[rows_in:2 * rows_in].reshape(HID, breadth)
    query_w = tile_set[2 * rows_in]
    key_w = tile_set[2 * rows_in + 1]
    mixer_w = tile_set[2 * rows_in + 2]
    start_at = 2 * rows_in + 3
    count_ff = NFFN * rows_ff
    expand = tile_set[start_at:start_at + count_ff].reshape(NFFN, rows_ff, breadth, breadth)
    expand = expand.transpose(0, 2, 1, 3).reshape(NFFN, breadth, SFF)
    shrink = tile_set[start_at + count_ff:start_at + 2 * count_ff].reshape(NFFN, SFF, breadth)
    leave_w = tile_set[start_at + 2 * count_ff:].reshape(rows_in, breadth, breadth).transpose(1, 0, 2).reshape(breadth, HID)
    return (entry_w, value_w, query_w, key_w, mixer_w, expand, shrink, leave_w)

def piece(vector, number):
    return vector[number * SW:(number + 1) * SW]

def student(inputs, valid_key, matrices, small_params):
    entry_w, value_w, query_w, key_w, mixer_w, expand, shrink, leave_w = matrices
    length = inputs.shape[0]
    gain_row, bias_row = (small_params[0], small_params[1])
    inputs_low = low(inputs)
    current = rounded_product(inputs_low, entry_w) * piece(gain_row, 0) + piece(bias_row, 0)
    current_low = low(current)
    queries = low(rounded_product(current_low, query_w)).reshape(length, SHEADS, SHD)
    key_rows = low(rounded_product(current_low, key_w)).reshape(length, SHEADS, SHD)
    value_rows = low(rounded_product(inputs_low, value_w)).reshape(length, SHEADS, SHD)
    scores = jnp.einsum('qhd,khd->hqk', queries, key_rows, precision=PRECISE) * SHD ** (-0.5)
    log_weight = normalize(low_back(masked_scores(scores, valid_key)))
    mixed = jnp.einsum('hqk,khd->qhd', low(jnp.exp(log_weight)), value_rows, precision=PRECISE).reshape(length, SW)
    context = low(low_back(mixed))
    current = (rounded_product(context, mixer_w) + current) * piece(gain_row, 1) + piece(bias_row, 1)
    for layer_index in range(NFFN):
        hidden = low(jnp.maximum(rounded_product(low(current), expand[layer_index]), 0.0))
        current = (rounded_product(hidden, shrink[layer_index]) + current) * piece(gain_row, 2 + layer_index) + piece(bias_row, 2 + layer_index)
    tail_start = (2 + NFFN) * SW
    student_out = (rounded_product(low(current), leave_w) + inputs) * gain_row[tail_start:] + bias_row[tail_start:]
    return (student_out, log_weight)

def row_loss(inputs, feature, teacher_logs, row_bound, weight_row, matrices, small_params):
    valid_key = jnp.arange(inputs.shape[0], dtype=jnp.int32) < row_bound[1]
    student_out, log_weight = student(inputs, valid_key, matrices, small_params)
    differ = student_out - feature
    squared = lax.optimization_barrier(jnp.mean(differ * differ, -1))
    target_logs = teacher_logs.astype(jnp.float32)
    target = jnp.exp(target_logs)
    diverge = lax.optimization_barrier(jnp.sum(target * (target_logs - log_weight), axis=(0, 2)))
    return jnp.sum(weight_row * (squared + diverge / SHEADS))

def slot_places(owners, slots):
    order_ids = jnp.arange(owners.shape[0], dtype=jnp.int32)
    same_owner = owners[:, None] == owners[None, :]
    earlier = order_ids[None, :] < order_ids[:, None]
    rank_in = lax.optimization_barrier(jnp.sum((same_owner & earlier).astype(jnp.int32), 1))
    return (owners * slots + rank_in).astype(jnp.int32)

def adam_update(weight, first_moment, second_moment, gradient, steps_done, decay_rate):
    first_moment = BETA_FIRST * first_moment + (1.0 - BETA_FIRST) * gradient
    second_moment = BETA_SECOND * second_moment + (1.0 - BETA_SECOND) * gradient * gradient
    first_fix = 1.0 - jnp.power(BETA_FIRST, steps_done)
    second_fix = 1.0 - jnp.power(BETA_SECOND, steps_done)
    update = first_moment / first_fix / (jnp.sqrt(second_moment / second_fix) + ADAM_EPSILON) + decay_rate * weight
    return (weight - LEARN_RATE * update, first_moment, second_moment)

def reference(token_ids, bounds, micro_batch, owners, step_count, word_table, conv_weight, embed_extra, teacher_entry, teacher_project, teacher_mixer, teacher_expand, teacher_shrink, teacher_leave, teacher_norms, tile_weight, tile_first, tile_second, small_weight, small_first, small_second):
    lengths = bounds[:, 1]
    choose = micro_batch[:, None] == jnp.arange(NMB, dtype=jnp.int32)[None, :]
    counts = lax.optimization_barrier(jnp.sum(jnp.where(choose, lengths[:, None], 0), 0)).astype(jnp.float32)
    places = jnp.arange(LEN, dtype=jnp.int32)
    row_weights = (places[None, :] < lengths[:, None]).astype(jnp.float32) / counts[micro_batch][:, None]
    frozen = tuple((matrix.astype(jnp.float32) for matrix in (teacher_entry, teacher_project, teacher_mixer, teacher_expand, teacher_shrink, teacher_leave)))

    def teacher_row(row_data):
        row_ids, row_bound = row_data
        inputs = embed(row_ids, row_bound, word_table, conv_weight, embed_extra)
        feature, teacher_logs = teacher(inputs, places < row_bound[1], *frozen, teacher_norms)
        return (inputs, feature, teacher_logs)
    inputs_all, features, logs_all = lax.map(teacher_row, (token_ids, bounds))
    slot_of = slot_places(owners, SLOTS)

    def total(tile_all, small_params):
        matrices = tuple((low(matrix) for matrix in assemble(tile_all[slot_of])))

        def advance(running, row_data):
            inputs, feature, teacher_logs, row_bound, weight_row = row_data
            term = jax.checkpoint(row_loss)(inputs, feature, teacher_logs, row_bound, weight_row, matrices, small_params)
            return (running + term, None)
        result, _ = lax.scan(advance, jnp.zeros((), jnp.float32), (inputs_all, features, logs_all, bounds, row_weights))
        return result
    total_loss, backward = jax.vjp(total, tile_weight, small_weight)
    tile_grad, small_grad = backward(jnp.ones((), jnp.float32))
    gradient_norm = jnp.sqrt(jnp.sum(tile_grad * tile_grad) + jnp.sum(small_grad * small_grad))
    factor = CLIP_NORM / jnp.maximum(gradient_norm, CLIP_NORM)
    small_gradient = small_grad * factor
    steps_done = step_count[0].astype(jnp.float32)
    slot_ids = jnp.arange(tile_weight.shape[0], dtype=jnp.int32)
    occupied = jnp.any(slot_of[None, :] == slot_ids[:, None], 1).astype(jnp.float32)[:, None, None]
    new_tiles, new_first, new_second = adam_update(tile_weight, tile_first, tile_second, tile_grad * factor, steps_done, WEIGHT_DECAY)
    new_small, small_moment, small_square = adam_update(small_weight, small_first, small_second, small_gradient, steps_done, 0.0)
    return (total_loss, gradient_norm, new_tiles * occupied, new_first * occupied, new_second * occupied, new_small, small_moment, small_square, small_gradient)
```

```python
import functools
import math

import jax
import jax.numpy as jnp
from jax import lax
from jax.experimental import pallas as pl
from jax.experimental.pallas import tpu as pltpu
from jax.sharding import PartitionSpec as P

HID = 512
THD = 256
SHEADS = 4
SHD = 32
SFF = 512
NFFN = 4
NMB = 2
NORM_EPSILON = 1e-05
CLIP_NORM = 0.05
LEARN_RATE = 0.1
BETA_FIRST = 0.9
BETA_SECOND = 0.999
ADAM_EPSILON = 1e-08
WEIGHT_DECAY = 0.01
MASKED_SCORE = -1e30
LOG2E = math.log2(math.e)
COUNT_BASE = 64

ATT = 256
ROWS_FF = 512
CUT_FF = 512
LOG_SLOTS = 4

MESH = pl.DeviceIdType.MESH
BF, F32 = jnp.bfloat16, jnp.float32
VMEM = pl.BlockSpec(memory_space=pltpu.VMEM)
SMEM = pl.BlockSpec(memory_space=pltpu.SMEM)
ANY = pl.BlockSpec(memory_space=pl.ANY)


def dot(left, right):
    return jnp.dot(left, right, preferred_element_type=F32)


def dot_nt(left, right):
    return lax.dot_general(left, right, (((1,), (1,)), ((), ())), preferred_element_type=F32)


def layer_norm(values, gain_row, bias_row):
    center = values - jnp.mean(values, -1, keepdims=True)
    spread = jnp.mean(center * center, -1, keepdims=True)
    return center * lax.rsqrt(spread + NORM_EPSILON) * gain_row + bias_row


def sum_over(ref, n):
    s = ref[0]
    for i in range(1, n):
        s = s + ref[i]
    return s


def attend_half(
    length, first_head, low_v, project_v, query_v, key_v, value_t, context_v, logs_out, logs_v, sem
):
    tokens = low_v.shape[0]
    width = project_v.shape[2]
    for start in range(0, tokens, ROWS_FF):
        rows = slice(start, start + ROWS_FF)
        low = low_v[rows]
        query_v[rows] = (dot(low, project_v[0]) * THD**-0.5).astype(BF)
        key_v[rows] = dot(low, project_v[1]).astype(BF)
        value_t[:, rows] = dot(low, project_v[2]).T.astype(BF)
    steps = [(h, q) for h in range(width // THD) for q in range(tokens // ATT)]
    least = tokens // 2
    valid = lax.broadcasted_iota(jnp.int32, (tokens - least, ATT), 0) + least < length

    def scores_of(i):
        h, q = steps[i]
        cols = slice(h * THD, (h + 1) * THD)
        return dot_nt(key_v[:, cols], query_v[q * ATT : (q + 1) * ATT, cols])

    def copy_of(i):
        h, q = steps[i]
        slot = i % LOG_SLOTS
        there = logs_out.at[first_head + h, :, pl.ds(q * ATT, ATT)]
        return pltpu.make_async_copy(logs_v.at[slot], there, sem.at[slot])

    ahead = scores_of(0)
    for i, (h, q) in enumerate(steps):
        if i >= LOG_SLOTS:
            copy_of(i - LOG_SLOTS).wait()
        scores = ahead
        if i + 1 < len(steps):
            ahead = scores_of(i + 1)
        upper = jnp.where(valid, scores[least:], MASKED_SCORE)
        scores = jnp.concatenate([scores[:least], upper], 0)
        top = jnp.max(scores, 0, keepdims=True)
        weight = jnp.exp(scores - top)
        total = jnp.sum(weight, 0, keepdims=True)
        logs_v[i % LOG_SLOTS] = (scores - (top + jnp.log(total))).astype(BF)
        mixed = dot(value_t[h * THD : (h + 1) * THD], weight.astype(BF)) * (1.0 / total)
        context_v[q * ATT : (q + 1) * ATT, h * THD : (h + 1) * THD] = mixed.T.astype(BF)
        copy_of(i).start()
    for i in range(len(steps) - LOG_SLOTS, len(steps)):
        copy_of(i).wait()


def lower_kernel(
    bound,
    core,
    words,
    conv,
    extra,
    norms,
    entry,
    project_own,
    project_mate,
    mixer_own,
    mixer_mate,
    inputs_out,
    first_out,
    logs_out,
    trigram,
    hidden_v,
    low_v,
    entry_v,
    project_v,
    mixer_v,
    query_v,
    key_v,
    value_t,
    context_v,
    logs_v,
    in_sem,
    out_sem,
    logs_sem,
):
    tokens, wide = words.shape
    breadth = entry.shape[1]
    half = project_own.shape[2]
    moves = (
        (entry, entry_v),
        (project_own, project_v.at[0]),
        (project_mate, project_v.at[1]),
        (mixer_own, mixer_v.at[0]),
        (mixer_mate, mixer_v.at[1]),
    )
    loads = [pltpu.make_async_copy(a, b, in_sem.at[n]) for n, (a, b) in enumerate(moves)]
    for c in loads:
        c.start()
    rows = words[...].astype(F32)
    place = lax.broadcasted_iota(jnp.int32, (tokens, wide), 0)
    after = jnp.where(place < tokens - 1, pltpu.roll(rows, tokens - 1, 0), 0.0)
    before = jnp.where(place > 0, pltpu.roll(rows, 1, 0), 0.0)
    trigram[:, :wide] = after.astype(BF)
    trigram[:, wide : 2 * wide] = words[...]
    trigram[:, 2 * wide :] = before.astype(BF)
    spot = lax.broadcasted_iota(jnp.int32, (ATT, 1), 0)
    gain, bias = norms[0:1], norms[1:2]
    loads[0].wait()
    for start in range(0, tokens, ATT):
        r = slice(start, start + ATT)
        second = spot + start >= bound[0]
        kind = jnp.where(second, extra[tokens + 1 : tokens + 2], extra[tokens : tokens + 1])
        value = dot(trigram[r], conv[...]) + extra[r] + kind
        inputs_out[r] = value
        hidden = layer_norm(dot(value.astype(BF), entry_v[...]), gain[:, :breadth], bias[:, :breadth])
        hidden_v[r] = hidden
        low_v[r] = hidden.astype(BF)
    heads = half // THD
    for p in range(2):
        loads[1 + p].wait()
        first_head = core[0] * heads if p == 0 else (1 - core[0]) * heads
        attend_half(
            bound[1],
            first_head,
            low_v,
            project_v.at[p],
            query_v,
            key_v,
            value_t,
            context_v.at[p],
            logs_out,
            logs_v,
            logs_sem,
        )
    for c in loads[3:]:
        c.wait()
    stores = []
    for n, start in enumerate(range(0, tokens, ATT)):
        r = slice(start, start + ATT)
        mixed = dot(context_v[0, r], mixer_v[0]) + dot(context_v[1, r], mixer_v[1])
        hidden_v[r] = layer_norm(
            mixed + hidden_v[r], gain[:, breadth : 2 * breadth], bias[:, breadth : 2 * breadth]
        )
        here = pl.ds(start, ATT)
        stores.append(pltpu.make_async_copy(hidden_v.at[here], first_out.at[here], out_sem.at[n]))
        stores[-1].start()
    for c in stores:
        c.wait()


def lower_teacher(bound, core, words, conv, extra, norms, entry, project_pair, mixer_pair):
    tokens, wide = words.shape
    breadth = entry.shape[1]
    half = project_pair[0].shape[2]
    heads = 2 * half // THD
    V, D = pltpu.VMEM, pltpu.SemaphoreType.DMA
    return pl.pallas_call(
        lower_kernel,
        out_shape=(
            jax.ShapeDtypeStruct((tokens, HID), F32),
            jax.ShapeDtypeStruct((tokens, breadth), F32),
            jax.ShapeDtypeStruct((heads, tokens, tokens), BF),
        ),
        in_specs=[SMEM, SMEM, VMEM, VMEM, VMEM, VMEM] + [ANY] * 5,
        out_specs=(VMEM, ANY, ANY),
        scratch_shapes=[
            V((tokens, 3 * wide), BF),
            V((tokens, breadth), F32),
            V((tokens, breadth), BF),
            V(entry.shape, BF),
            V((2,) + project_pair[0].shape, BF),
            V((2,) + mixer_pair[0].shape, BF),
            V((tokens, half), BF),
            V((tokens, half), BF),
            V((half, tokens), BF),
            V((2, tokens, half), BF),
            V((LOG_SLOTS, tokens, ATT), BF),
            D((5,)),
            D((tokens // ATT,)),
            D((LOG_SLOTS,)),
        ],
        compiler_params=pltpu.CompilerParams(vmem_limit_bytes=44 << 20),
        cost_estimate=pl.CostEstimate(
            flops=14_000_000_000, bytes_accessed=24 << 20, transcendentals=0
        ),
    )(bound, core, words, conv, extra, norms, entry, *project_pair, *mixer_pair)


def upper_kernel(
    first,
    inputs,
    norms,
    expand_own,
    expand_mate,
    shrink_own,
    shrink_mate,
    leave,
    feature_out,
    first_v,
    inputs_v,
    expand_v,
    shrink_v,
    leave_v,
    inner_v,
    in_sem,
):
    tokens, breadth = first.shape
    half = expand_own.shape[1]
    blocks = tokens // ROWS_FF
    cuts = half // CUT_FF
    moves = [(first.at[pl.ds(0, ROWS_FF)], first_v.at[pl.ds(0, ROWS_FF)])]
    for p, matrix in enumerate((expand_own, expand_mate)):
        for c in range(cuts):
            cols = pl.ds(c * CUT_FF, CUT_FF)
            moves.append((matrix.at[:, cols], expand_v.at[p, :, cols]))
    moves.append((shrink_own, shrink_v.at[0]))
    moves.append((shrink_mate, shrink_v.at[1]))
    moves.append((leave, leave_v))
    moves.append((inputs, inputs_v))
    rest = pl.ds(ROWS_FF, tokens - ROWS_FF)
    moves.append((first.at[rest], first_v.at[rest]))
    loads = [pltpu.make_async_copy(a, b, in_sem.at[n]) for n, (a, b) in enumerate(moves)]
    for c in loads:
        c.start()
    gain, bias = norms[0:1], norms[1:2]
    third = slice(2 * breadth, 3 * breadth)
    last = slice(3 * breadth, 3 * breadth + HID)
    tail = 1 + 2 * cuts
    for n in range(blocks):
        r = slice(n * ROWS_FF, (n + 1) * ROWS_FF)
        if n == 0:
            loads[0].wait()
        if n == 1:
            loads[tail + 4].wait()
        first_low = first_v[r].astype(BF)
        for p in range(2):
            for c in range(cuts):
                if n == 0:
                    loads[1 + p * cuts + c].wait()
                cols = slice(c * CUT_FF, (c + 1) * CUT_FF)
                before = dot(first_low, expand_v[p, :, cols])
                inner = 0.5 * before * (1.0 + lax.erf(before * math.sqrt(0.5)))
                there = slice(p * half + c * CUT_FF, p * half + (c + 1) * CUT_FF)
                inner_v[:, there] = inner.astype(BF)
        if n == 0:
            for c in loads[tail : tail + 4]:
                c.wait()
        total = dot(inner_v[:, :half], shrink_v[0]) + dot(inner_v[:, half:], shrink_v[1])
        second = layer_norm(total + first_v[r], gain[:, third], bias[:, third])
        raw = dot(second.astype(BF), leave_v[...]) + inputs_v[r]
        feature_out[r] = layer_norm(raw, gain[:, last], bias[:, last])


def upper_teacher(first, inputs, norms, expand_pair, shrink_pair, leave):
    tokens, breadth = first.shape
    half = expand_pair[0].shape[1]
    V, D = pltpu.VMEM, pltpu.SemaphoreType.DMA
    return pl.pallas_call(
        upper_kernel,
        out_shape=jax.ShapeDtypeStruct((tokens, HID), F32),
        in_specs=[ANY, ANY, VMEM] + [ANY] * 5,
        out_specs=VMEM,
        scratch_shapes=[
            V((tokens, breadth), F32),
            V((tokens, HID), F32),
            V((2,) + expand_pair[0].shape, BF),
            V((2,) + shrink_pair[0].shape, BF),
            V(leave.shape, BF),
            V((ROWS_FF, 2 * half), BF),
            D((2 * (half // CUT_FF) + 6,)),
        ],
        compiler_params=pltpu.CompilerParams(vmem_limit_bytes=48 << 20),
        cost_estimate=pl.CostEstimate(
            flops=19_000_000_000, bytes_accessed=26 << 20, transcendentals=0
        ),
    )(first, inputs, norms, *expand_pair, *shrink_pair, leave)


QB = ATT
TB = ROWS_FF


def student_kernel(owners, bound, place_of, inputs, feature, logs, tiles_own, tiles_mate, small,
                   grads_out, lines_out,
                   logs_v, wide_w, pair_w, mixer_w, expand_w, shrink_w, leave_w,
                   low_v, narrow_v, first_v, firstlow_v, query_v, query_m, key_m, value_m, key_t, value_t,
                   context_t, contextlow_t, shift_v, blocklow_v, hidden_v, sum_v,
                   dsum_v, dcontext_v, dcontext_t, dcontext_m, dvalue_v, dkey_v, dpair_v,
                   g_leave, g_mixer, g_expand, g_shrink, small_out, slot, held, sem):
    bf, f32 = BF, F32
    tokens = inputs.shape[0]
    breadth = tiles_own.shape[2]
    core, batch = place_of[0], place_of[1]
    copies = [pltpu.make_async_copy(logs.at[h], logs_v.at[h], sem.at[h]) for h in range(SHEADS)]
    for c in copies: c.start()
    length = bound[1]
    n_owners = tiles_own.shape[0]
    slots = grads_out.shape[0] // n_owners
    lines = breadth // 2

    def clear(i, carry):
        held[i] = 0
        return carry

    lax.fori_loop(0, n_owners, clear, 0)

    def assign(i, carry):
        owner = owners[i]
        slot[i] = owner * slots + held[owner]
        held[owner] = held[owner] + 1
        return carry

    lax.fori_loop(0, owners.shape[0], assign, 0)
    digits = tiles_own[0, slots * lines :].astype(F32)
    for i in range(1, n_owners):
        digits = digits + tiles_own[i, slots * lines :].astype(F32)
    digits = digits[0:1]
    at_lane = lax.broadcasted_iota(jnp.int32, digits.shape, 1)
    digits = jnp.where(at_lane == 2 * batch, digits * COUNT_BASE, jnp.where(at_lane == 2 * batch + 1, digits, 0.0))
    inverse = 1.0 / jnp.sum(digits, 1, keepdims=True)
    grads_out[...] = jnp.zeros_like(grads_out)
    small_out[...] = jnp.zeros_like(small_out)
    g_leave[...] = jnp.zeros_like(g_leave); g_mixer[...] = jnp.zeros_like(g_mixer)
    g_expand[...] = jnp.zeros_like(g_expand); g_shrink[...] = jnp.zeros_like(g_shrink)
    dvalue_v[...] = jnp.zeros_like(dvalue_v); dkey_v[...] = jnp.zeros_like(dkey_v)
    nin = HID // breadth; nff = SFF // breadth
    at = lambda j: slice(j*breadth, (j+1)*breadth)
    def load(i, put):
        owner, rank = slot[i] // slots, slot[i] % slots
        from_line = pl.ds(pl.multiple_of(rank * lines, lines), lines)
        put(pl.multiple_of(core * lines, lines), tiles_own[owner, from_line])
        put(pl.multiple_of((1 - core) * lines, lines), tiles_mate[owner, from_line])

    def fill(ref, row, col):
        def put(line, value):
            ref[pl.ds(row * breadth + line, lines), at(col)] = value

        return put

    for j in range(nin):
        load(j, fill(wide_w, j, 0))
        load(nin + j, fill(wide_w, j, 1))
    load(2 * nin, fill(pair_w, 0, 0))
    load(2 * nin + 1, fill(pair_w, 0, 1))
    load(2 * nin + 2, fill(mixer_w, 0, 0))
    first_ff = 2*nin+3
    for b in range(NFFN):
        for j in range(nff):
            load(first_ff + b * nff + j, fill(expand_w.at[b], 0, j))
            load(first_ff + (NFFN + b) * nff + j, fill(shrink_w.at[b], j, 0))
    first_leave = first_ff + 2*NFFN*nff
    for j in range(nin):
        load(first_leave + j, fill(leave_w, 0, j))
    gain = lambda n: small[0:1, at(n)]
    bias = lambda n: small[1:2, at(n)]
    tail = (2+NFFN)*breadth
    gain_out, bias_out = small[0:1, tail:], small[1:2, tail:]
    lane = lax.broadcasted_iota(jnp.int32, (1, breadth), 1) // SHD
    masks = [(lane == h) for h in range(SHEADS)]
    for start in range(0, tokens, TB):
        r = slice(start, start+TB)
        low = inputs[r].astype(bf)
        low_v[r] = low
        both = dot(low, wide_w[...])
        narrow = both[:, :breadth]
        narrow_v[r] = narrow
        value = both[:, breadth:]
        first = narrow*gain(0) + bias(0)
        first_v[r] = first
        firstlow_v[r] = first.astype(bf)
        pair = dot(first.astype(bf), pair_w[...])
        query, key = pair[:, :breadth], pair[:, breadth:]
        query_v[r] = query.astype(bf)
        for h in range(SHEADS):
            query_m[h, r] = jnp.where(masks[h], query, 0.0).astype(bf)
            key_m[h, r] = jnp.where(masks[h], key, 0.0).astype(bf)
            value_m[h, r] = jnp.where(masks[h], value, 0.0).astype(bf)
        key_t[:, r] = key.T.astype(bf)
        value_t[:, r] = value.T.astype(bf)
    scale = SHD**-0.5
    scale2 = scale*LOG2E
    least = tokens//2
    valid = lax.broadcasted_iota(jnp.int32, (tokens-least, QB), 0) + least < length
    def scores_of(h, r):
        scores = dot_nt(key_m[h], query_v[r])
        return jnp.concatenate([scores[:least], jnp.where(valid, scores[least:], MASKED_SCORE)], 0)
    def forward(n, carry):
        r = pl.ds(pl.multiple_of(n*QB, QB), QB)
        ahead = scores_of(0, r)
        parts = []
        for h in range(SHEADS):
            scores = ahead
            if h+1 < SHEADS: ahead = scores_of(h+1, r)
            top = jnp.max(scores, 0, keepdims=True)
            weight = jnp.exp2((scores-top)*scale2)
            total = jnp.sum(weight, 0, keepdims=True)
            shift_v[h:h+1, r] = top*scale2 + jnp.log2(total)
            parts.append(dot(value_t[h*SHD:(h+1)*SHD], weight.astype(bf)) * (1.0/total))
        mixed = jnp.concatenate(parts, 0)
        context_t[:, r] = mixed
        contextlow_t[:, r] = mixed.astype(bf)
        return carry
    lax.fori_loop(0, tokens//QB, forward, 0)
    def row_sums(n, d, value):
        small_out[0:1, at(n)] += jnp.sum(d*value, 0, keepdims=True)
        small_out[1:2, at(n)] += jnp.sum(d, 0, keepdims=True)
    def feed(n, loss):
        r = pl.ds(pl.multiple_of(n*TB, TB), TB)
        place = lax.broadcasted_iota(jnp.int32, (TB, 1), 0) + n*TB
        weight = jnp.where(place < length, inverse, 0.0)
        context = context_t[:, r].T.astype(bf)
        mixed_sum = dot(context, mixer_w[...]) + first_v[r]
        current = mixed_sum*gain(1) + bias(1)
        for b in range(NFFN):
            low = current.astype(bf)
            blocklow_v[b] = low
            hidden = jnp.maximum(dot(low, expand_w[b]), 0.0).astype(bf)
            hidden_v[b] = hidden
            total = dot(hidden, shrink_w[b]) + current
            sum_v[b] = total
            current = total*gain(2+b) + bias(2+b)
        low = current.astype(bf)
        joined = dot(low, leave_w[...]) + inputs[r]
        differ = joined*gain_out + bias_out - feature[r]
        loss = loss + jnp.sum(weight*jnp.mean(differ*differ, -1, keepdims=True), 0, keepdims=True)
        outer = differ*(weight*(2.0/HID))
        small_out[0:1, tail:] += jnp.sum(outer*joined, 0, keepdims=True)
        small_out[1:2, tail:] += jnp.sum(outer, 0, keepdims=True)
        back = (outer*gain_out).astype(bf)
        g_leave[...] += dot(current.T.astype(bf), back)
        d = dot_nt(back, leave_w[...])
        for b in reversed(range(NFFN)):
            row_sums(2+b, d, sum_v[b])
            d_sum = d*gain(2+b)
            d_branch = d_sum.astype(bf)
            hidden = hidden_v[b]
            g_shrink[b] += dot(d_sum.T.astype(bf), hidden)
            d_before = jnp.where(hidden > 0, dot_nt(d_branch, shrink_w[b]), 0.0).astype(bf)
            g_expand[b] += dot(blocklow_v[b].T, d_before)
            d = d_sum + dot_nt(d_before, expand_w[b])
        row_sums(1, d, mixed_sum)
        d_sum = d*gain(1)
        dsum_v[r] = d_sum
        d_mixed = d_sum.astype(bf)
        g_mixer[...] += dot(contextlow_t[:, r], d_mixed)
        d_context = dot_nt(d_mixed, mixer_w[...]).astype(bf)
        dcontext_v[r] = d_context
        dcontext_t[:, r] = d_context.astype(f32).T
        for h in range(SHEADS):
            dcontext_m[h, r] = jnp.where(masks[h], d_context, jnp.zeros_like(d_context))
        return loss
    loss = jnp.zeros((1, 1), f32)
    loss = lax.fori_loop(0, tokens//TB, feed, loss)
    for c in copies: c.wait()
    def backward(n, loss):
        r = pl.ds(pl.multiple_of(n*QB, QB), QB)
        place = lax.broadcasted_iota(jnp.int32, (1, QB), 1) + n*QB
        share = jnp.where(place < length, inverse/SHEADS, 0.0)
        ahead = (scores_of(0, r), dot_nt(value_m[0], dcontext_v[r]))
        parts = []
        for h in range(SHEADS):
            scores, d_weight = ahead
            if h+1 < SHEADS: ahead = (scores_of(h+1, r), dot_nt(value_m[h+1], dcontext_v[r]))
            shift = shift_v[h:h+1, r]
            weight = jnp.exp2(scores*scale2 - shift)
            target_logs = logs_v[h, :, r].astype(f32)
            target = jnp.exp2(target_logs*LOG2E)
            target_sum = jnp.sum(target, 0, keepdims=True)
            gap = jnp.sum(target*(target_logs - jnp.maximum(scores, -1e29)*scale), 0, keepdims=True) + target_sum*(shift*(1.0/LOG2E))
            loss = loss + jnp.sum(share*gap, 1, keepdims=True)
            heads = slice(h*SHD, (h+1)*SHD)
            along = jnp.sum(context_t[heads, r]*dcontext_t[heads, r], 0, keepdims=True)
            d_scores = weight*(d_weight - (along - share*target_sum)) - share*target
            d_low = d_scores.astype(bf)
            dvalue_v[...] += dot(weight.astype(bf), dcontext_m[h, r])
            dkey_v[...] += dot(d_low, query_m[h, r])
            parts.append(dot(key_t[heads], d_low))
        dpair_v[r, at(0)] = (jnp.concatenate(parts, 0)*scale).T.astype(bf)
        return loss
    loss = lax.fori_loop(0, tokens//QB, backward, loss)
    lines_out[...] = jnp.zeros_like(lines_out)
    n_lines = small.shape[1] // breadth
    lines_out[2*n_lines:2*n_lines+1, 0:1] = loss
    dpair_v[:, at(1)] = (dkey_v[...]*scale).astype(bf)
    d_pair = dpair_v[...]
    d_first = dsum_v[...] + dot_nt(d_pair, pair_w[...])
    row_sums(0, d_first, narrow_v[...])
    g_pair = dot(first_v[...].T.astype(bf), d_pair)
    wide_t = jnp.concatenate([(d_first*gain(0)).T.astype(bf), dvalue_v[...].T.astype(bf)], 0)
    g_wide = dot(wide_t, low_v[...])
    for j in range(nin):
        grads_out[slot[j]] = g_wide[:breadth, at(j)].T.astype(bf)
        grads_out[slot[nin+j]] = g_wide[breadth:, at(j)].T.astype(bf)
        grads_out[slot[first_leave+j]] = g_leave[:, at(j)].astype(bf)
    grads_out[slot[2*nin]] = g_pair[:, at(0)].astype(bf)
    grads_out[slot[2*nin+1]] = g_pair[:, at(1)].astype(bf)
    grads_out[slot[2*nin+2]] = g_mixer[...].astype(bf)
    for b in range(NFFN):
        for j in range(nff):
            grads_out[slot[first_ff + b*nff + j]] = g_expand[b, :, at(j)].astype(bf)
            grads_out[slot[first_ff + (NFFN+b)*nff + j]] = g_shrink[b, :, at(j)].T.astype(bf)
    for j in range(n_lines):
        lines_out[j:j+1] = small_out[0:1, at(j)]
        lines_out[n_lines+j:n_lines+j+1] = small_out[1:2, at(j)]


def student(owners, bound, place_of, inputs, feature, logs, tiles_own, tiles_mate, small, slots):
    tokens = inputs.shape[0]
    n_owners, _, w = tiles_own.shape
    n_lines = 8 * -(-(2 * small.shape[1] // w + 1) // 8)
    V, D = pltpu.VMEM, pltpu.SemaphoreType.DMA
    return pl.pallas_call(
        student_kernel,
        out_shape=(
            jax.ShapeDtypeStruct((n_owners * slots, w, w), BF),
            jax.ShapeDtypeStruct((n_lines, w), F32),
        ),
        in_specs=[SMEM, SMEM, SMEM, VMEM, VMEM, ANY, VMEM, VMEM, VMEM],
        out_specs=(VMEM, VMEM),
        scratch_shapes=[
            V(logs.shape, BF), V((HID, 2 * w), BF), V((w, 2 * w), BF), V((w, w), BF),
            V((NFFN, w, SFF), BF), V((NFFN, SFF, w), BF), V((w, HID), BF),
            V((tokens, HID), BF), V((tokens, w), F32), V((tokens, w), F32), V((tokens, w), BF), V((tokens, w), BF),
            V((SHEADS, tokens, w), BF), V((SHEADS, tokens, w), BF), V((SHEADS, tokens, w), BF), V((w, tokens), BF), V((w, tokens), BF),
            V((w, tokens), F32), V((w, tokens), BF), V((8, tokens), F32), V((NFFN, TB, w), BF), V((NFFN, TB, SFF), BF), V((NFFN, TB, w), F32),
            V((tokens, w), F32), V((tokens, w), BF), V((w, tokens), F32), V((SHEADS, tokens, w), BF), V((tokens, w), F32), V((tokens, w), F32), V((tokens, 2 * w), BF),
            V((w, HID), F32), V((w, w), F32), V((NFFN, w, SFF), F32), V((NFFN, w, SFF), F32),
            V((8, small.shape[1]), F32),
            pltpu.SMEM(owners.shape, jnp.int32), pltpu.SMEM((n_owners,), jnp.int32),
            D((SHEADS,)),
        ],
        compiler_params=pltpu.CompilerParams(vmem_limit_bytes=58 << 20),
        cost_estimate=pl.CostEstimate(flops=15_000_000_000, bytes_accessed=16 << 20, transcendentals=0),
    )(owners, bound, place_of, inputs, feature, logs, tiles_own, tiles_mate, small)


def reduce_kernel(side, deep, slots, grads, small, tiles_out, stats_out,
                  pair_in, first, first_in, second, second_in, third, third_in, half_own, half_in,
                  small_pair, small_a, small_b, small_z, norm_all, norm_own,
                  pair_send, pair_recv, first_send, first_recv, second_send, second_recv, third_send, third_recv,
                  half_send, half_recv, sp_send, sp_recv, sa_send, sa_recv, sb_send, sb_recv, sz_send, sz_recv, n_send, n_recv):
    bf, f32 = jnp.bfloat16, jnp.float32
    row, core = lax.axis_index("rows"), lax.axis_index("heads")
    plane = side*side
    z = row // plane
    y = (row // side) % side
    x = row % side
    total = plane*deep
    lines = grads.shape[-2]//2
    mate = (row, 1-core)
    mine = core*lines
    theirs = (1-core)*lines
    straight = core == 0
    a = jnp.where(straight, x, y)
    b = jnp.where(straight, y, x)
    pa = jnp.where(straight, y, x)
    def row_at(xx, yy, zz):
        return zz*plane + yy*side + xx
    def along_a(aa):
        return (jnp.where(straight, row_at(aa, y, z), row_at(x, aa, z)), core)
    def along_b(bb):
        return (jnp.where(straight, row_at(x, bb, z), row_at(bb, y, z)), core)
    def along_z(zz):
        return (row_at(x, y, zz), core)
    barrier = pltpu.get_barrier_semaphore()
    n_devices = 2*total
    me = row*2 + core
    def greet(i, carry):
        peer = lax.rem(me + i, n_devices)
        pl.semaphore_signal(barrier, inc=1, device_id=(peer // 2, peer % 2), device_id_type=MESH)
        return carry
    lax.fori_loop(1, n_devices, greet, 0)
    pl.semaphore_wait(barrier, n_devices-1)

    def remote(src, dst, send, recv, peer):
        return pltpu.make_async_remote_copy(src_ref=src, dst_ref=dst, send_sem=send, recv_sem=recv, device_id=peer, device_id_type=MESH)

    small_pair_copy = remote(small, small_pair, sp_send, sp_recv, mate)
    small_pair_copy.start()
    order = list(range(1, side)) + [0]
    for d in order:
        piece = lax.rem(pa + d, side)
        by_y = remote(grads.at[:, piece, :, :, pl.ds(theirs, lines), :], pair_in.at[d], pair_send.at[d], pair_recv.at[d], mate)
        by_x = remote(grads.at[:, :, piece, :, pl.ds(theirs, lines), :], pair_in.at[d], pair_send.at[d], pair_recv.at[d], mate)
        @pl.when(straight)
        def _(): by_y.start()
        @pl.when(jnp.logical_not(straight))
        def _(): by_x.start()
    def pair_wait(d):
        return remote(first.at[d], pair_in.at[d], pair_send.at[d], pair_recv.at[d], mate)
    first_copies = []
    for d in order:
        pair_wait(d).wait_recv()
        aa = lax.rem(a + d, side)
        def add(i, carry):
            zz, bb = i // side, i % side
            xx, yy = jnp.where(straight, aa, bb), jnp.where(straight, bb, aa)
            own = grads[zz, yy, xx, :, pl.ds(mine, lines), :].astype(f32)
            first[d, zz, bb] = (own + pair_in[d, zz, bb].astype(f32)).astype(bf)
            return carry
        lax.fori_loop(0, deep*side, add, 0)
        if d:
            c = remote(first.at[d], first_in.at[d-1], first_send.at[d-1], first_recv.at[d-1], along_a(aa))
            c.start(); first_copies.append(c)
    small_pair_copy.wait()
    small_a[x] = small[...] + small_pair[...]
    sa = []
    for d in range(1, side):
        c = remote(small_a.at[x], small_a.at[x], sa_send.at[d-1], sa_recv.at[d-1], (row_at(lax.rem(x+d, side), y, z), core))
        c.start(); sa.append(c)
    for c in first_copies: c.wait_recv()
    second_copies = []
    for d in order:
        bb = lax.rem(b + d, side)
        def add(zz, carry):
            s = first[0, zz, bb].astype(f32)
            for j in range(side-1): s = s + first_in[j, zz, bb].astype(f32)
            second[d, zz] = s.astype(bf)
            return carry
        lax.fori_loop(0, deep, add, 0)
        if d:
            c = remote(second.at[d], second_in.at[d-1], second_send.at[d-1], second_recv.at[d-1], along_b(bb))
            c.start(); second_copies.append(c)
    for c in sa: c.wait()
    small_b[y] = sum_over(small_a, side)
    sb = []
    for d in range(1, side):
        c = remote(small_b.at[y], small_b.at[y], sb_send.at[d-1], sb_recv.at[d-1], (row_at(x, lax.rem(y+d, side), z), core))
        c.start(); sb.append(c)
    for c in second_copies: c.wait_recv()
    third_copies = []
    own = None
    for d in list(range(1, deep)) + [0]:
        zz = lax.rem(z + d, deep)
        s = second[0, zz].astype(f32)
        for j in range(side-1): s = s + second_in[j, zz].astype(f32)
        if d:
            third[d-1] = s.astype(bf)
            c = remote(third.at[d-1], third_in.at[d-1], third_send.at[d-1], third_recv.at[d-1], along_z(zz))
            c.start(); third_copies.append(c)
        else:
            own = s
    for c in sb: c.wait()
    small_z[z] = sum_over(small_b, side)
    sz = []
    for d in range(1, deep):
        c = remote(small_z.at[z], small_z.at[z], sz_send.at[d-1], sz_recv.at[d-1], along_z(lax.rem(z+d, deep)))
        c.start(); sz.append(c)
    for c in third_copies: c.wait_recv()
    for j in range(deep-1): own = own + third_in[j].astype(f32)
    half_own[...] = own
    half_copy = remote(half_own, half_in, half_send, half_recv, mate)
    half_copy.start()
    part = jnp.sum(jnp.sum(own*own, 0), 0, keepdims=True)
    norm_own[...] = jnp.broadcast_to(part, norm_own.shape)
    norm_all[me] = norm_own[...]
    def tell(i, carry):
        peer = lax.rem(me + i, n_devices)
        remote(norm_own, norm_all.at[me], n_send.at[i-1], n_recv.at[i-1], (peer // 2, peer % 2)).start()
        return carry
    lax.fori_loop(1, n_devices, tell, 0)
    tiles_out[:, pl.ds(mine, lines), :] = own
    half_copy.wait()
    tiles_out[:, pl.ds(theirs, lines), :] = half_in[...]
    for c in sz: c.wait()
    small_total = sum_over(small_z, deep)
    def hear(i, carry):
        remote(norm_own, norm_all.at[me], n_send.at[i-1], n_recv.at[i-1], mate).wait()
        return carry
    lax.fori_loop(1, n_devices, hear, 0)
    def gather(i, s):
        return s + norm_all[i]
    squares = lax.fori_loop(0, n_devices, gather, jnp.zeros(norm_own.shape, f32))
    stats_out[0] = small_total[0:8]
    stats_out[1] = small_total[8:16]
    stats_out[2] = small_total[16:24]
    stats_out[3] = squares
    for d in order: pair_wait(d).wait_send()
    for c in first_copies + second_copies + third_copies: c.wait_send()

def reduce_call(n_rows, grads, small):
    deep = 4
    side = math.isqrt(n_rows // deep)
    assert side*side*deep == n_rows
    slots = grads.shape[0] // n_rows
    wide, lanes = grads.shape[1:]
    lines = wide//2
    bf, f32 = jnp.bfloat16, jnp.float32
    grads = grads.reshape(deep, side, side, slots, wide, lanes)
    V, D = pltpu.VMEM, pltpu.SemaphoreType.DMA
    s1, d1, n = side-1, deep-1, 2*n_rows
    return pl.pallas_call(functools.partial(reduce_kernel, side, deep, slots),
        out_shape=(jax.ShapeDtypeStruct((slots, wide, lanes), f32), jax.ShapeDtypeStruct((4, 8, lanes), f32)),
        in_specs=[VMEM, VMEM], out_specs=(VMEM, VMEM),
        scratch_shapes=[V((side, deep, side, slots, lines, lanes), bf), V((side, deep, side, slots, lines, lanes), bf), V((s1, deep, side, slots, lines, lanes), bf),
            V((side, deep, slots, lines, lanes), bf), V((s1, deep, slots, lines, lanes), bf), V((d1, slots, lines, lanes), bf), V((d1, slots, lines, lanes), bf),
            V((slots, lines, lanes), f32), V((slots, lines, lanes), f32),
            V(small.shape, f32), V((side,)+small.shape, f32), V((side,)+small.shape, f32), V((deep,)+small.shape, f32),
            V((n, 8, lanes), f32), V((8, lanes), f32),
            D((side,)), D((side,)), D((s1,)), D((s1,)), D((s1,)), D((s1,)), D((d1,)), D((d1,)), D, D, D, D, D((s1,)), D((s1,)), D((s1,)), D((s1,)), D((d1,)), D((d1,)), D((n-1,)), D((n-1,))],
        compiler_params=pltpu.CompilerParams(collective_id=0, has_side_effects=True, vmem_limit_bytes=48<<20),
        cost_estimate=pl.CostEstimate(flops=10_000_000, bytes_accessed=8<<20, transcendentals=0),
    )(grads, small)


def update_kernel(
    owners, step, own, summed, stats, weight, first, second, small, small_first, small_second,
    loss_out, norm_out, tiles_out, first_out, second_out, small_out, small_first_out, small_second_out, small_grad_out,
    small_v,
):
    breadth = summed.shape[2]
    n_lines = small.shape[1] // breadth
    steps = step[0]
    first_fix = 1.0 - lax.fori_loop(0, steps, lambda i, p: p * BETA_FIRST, jnp.float32(1.0))
    second_fix = 1.0 - lax.fori_loop(0, steps, lambda i, p: p * BETA_SECOND, jnp.float32(1.0))

    def adam(w, m, v, g, decay):
        m = BETA_FIRST * m + (1.0 - BETA_FIRST) * g
        v = BETA_SECOND * v + (1.0 - BETA_SECOND) * g * g
        change = m / first_fix / (jnp.sqrt(v / second_fix) + ADAM_EPSILON) + decay * w
        return w - LEARN_RATE * change, m, v

    line = lambda n: stats[n // 8, n % 8 : n % 8 + 1]
    squares = stats[3, 0:1]
    for n in range(2 * n_lines):
        squares = squares + line(n) * line(n)
    norm = jnp.sqrt(jnp.sum(squares, 1, keepdims=True))
    norm_out[...] = norm
    loss_out[...] = line(2 * n_lines)[:, 0:1]
    factor = CLIP_NORM / jnp.maximum(norm, CLIP_NORM)
    for n in range(n_lines):
        cols = slice(n * breadth, (n + 1) * breadth)
        small_v[0:1, cols] = line(n)
        small_v[1:2, cols] = line(n_lines + n)
    small_grad = small_v[0:2] * factor
    small_grad_out[...] = small_grad
    w, m, v = adam(small[...], small_first[...], small_second[...], small_grad, 0.0)
    small_out[...] = w
    small_first_out[...] = m
    small_second_out[...] = v

    def count(i, n):
        return n + (owners[i] == own[0]).astype(jnp.int32)

    held = lax.fori_loop(0, owners.shape[0], count, 0)
    for s in range(summed.shape[0]):
        keep = held > s
        w, m, v = adam(weight[s], first[s], second[s], summed[s] * factor, WEIGHT_DECAY)
        tiles_out[s] = jnp.where(keep, w, 0.0)
        first_out[s] = jnp.where(keep, m, 0.0)
        second_out[s] = jnp.where(keep, v, 0.0)


def update(owners, step, own, summed, stats, weight, first, second, small, small_first, small_second):
    one = jax.ShapeDtypeStruct((1, 1), F32)
    tile = jax.ShapeDtypeStruct(weight.shape, F32)
    row = jax.ShapeDtypeStruct(small.shape, F32)
    return pl.pallas_call(
        update_kernel,
        out_shape=(one, one, tile, tile, tile, row, row, row, row),
        in_specs=[SMEM] * 3 + [VMEM] * 8,
        out_specs=(VMEM,) * 9,
        scratch_shapes=[pltpu.VMEM((8, small.shape[1]), F32)],
        compiler_params=pltpu.CompilerParams(vmem_limit_bytes=24 << 20),
        cost_estimate=pl.CostEstimate(flops=2_000_000, bytes_accessed=2 << 20, transcendentals=0),
    )(owners, step, own, summed, stats, weight, first, second, small, small_first, small_second)


def swap_cores(values):
    return lax.ppermute(values, "heads", [(0, 1), (1, 0)])


def on_device(
    token_ids,
    bounds,
    micro_batch,
    owners,
    step_count,
    word_table,
    conv_weight,
    embed_extra,
    teacher_entry,
    teacher_project,
    teacher_mixer,
    teacher_expand,
    teacher_shrink,
    teacher_leave,
    teacher_norms,
    tile_weight,
    tile_first,
    tile_second,
    small_weight,
    small_first,
    small_second,
):
    core = lax.axis_index("heads")
    n_rows = lax.axis_size("rows")
    slots, breadth, _ = tile_weight.shape
    assert token_ids.shape[0] == lax.axis_size("heads")
    project = teacher_project.transpose(1, 0, 2)
    project_pair = (project, swap_cores(project))
    mixer_pair = (teacher_mixer, swap_cores(teacher_mixer))
    lengths = bounds[:, 1]
    batch_range = jnp.arange(NMB, dtype=jnp.int32)
    chosen = micro_batch[:, None] == batch_range[None, :]
    local = jnp.sum(jnp.where(chosen, lengths[:, None], 0), 0)
    digits = jnp.stack([local // COUNT_BASE, local % COUNT_BASE], 1).reshape(1, 2 * NMB)
    digits = jnp.pad(digits.astype(BF), ((0, 15), (0, breadth - 2 * NMB)))
    lines = breadth // 2
    half = lax.dynamic_slice_in_dim(tile_weight, core * lines, lines, 1).astype(BF)
    sent = jnp.concatenate([half.reshape(slots * lines, breadth), digits], 0)
    tiles_own = lax.all_gather(sent, "rows", axis=0)
    row_ids, bound, batch = (
        lax.dynamic_index_in_dim(whole, core, 0, keepdims=False)
        for whole in (token_ids, bounds, micro_batch)
    )
    words = word_table[row_ids]
    place_of = jnp.stack([core, batch])
    inputs, first, logs = lower_teacher(
        bound,
        core[None],
        words,
        conv_weight,
        embed_extra,
        teacher_norms,
        teacher_entry,
        project_pair,
        mixer_pair,
    )
    later = lax.optimization_barrier((teacher_expand, teacher_shrink, project_pair[1]))
    expand_pair = (teacher_expand, swap_cores(later[0]))
    shrink_pair = (teacher_shrink, swap_cores(later[1]))
    feature = upper_teacher(first, inputs, teacher_norms, expand_pair, shrink_pair, teacher_leave)
    tiles_mate = swap_cores(tiles_own)
    grads, small_lines = student(
        owners, bound, place_of, inputs, feature, logs, tiles_own, tiles_mate, small_weight, slots
    )
    summed, stats = reduce_call(n_rows, grads, small_lines)
    own = lax.axis_index("rows")[None]
    loss, norm, *rest = update(
        owners,
        step_count,
        own,
        summed,
        stats,
        tile_weight,
        tile_first,
        tile_second,
        small_weight,
        small_first,
        small_second,
    )
    return (loss[0, 0], norm[0, 0], *rest)


def solution(mesh):
    placed = (
        P("rows", None),
        P("rows", None),
        P("rows"),
        P(),
        P(),
        P(),
        P(),
        P(),
        P(),
        P(None, None, "heads"),
        P("heads", None),
        P(None, "heads"),
        P("heads", None),
        P(),
        P(),
        P("rows", None, None),
        P("rows", None, None),
        P("rows", None, None),
        P(),
        P(),
        P(),
    )
    tiles = P("rows", None, None)
    return jax.shard_map(
        on_device,
        mesh=mesh,
        in_specs=placed,
        out_specs=(P(), P(), tiles, tiles, tiles, P(), P(), P(), P()),
        check_vma=False,
    )
```

```python
import functools
import math

import jax
import jax.numpy as jnp
from jax import lax
from jax.experimental import pallas as pl
from jax.experimental.pallas import tpu as pltpu
from jax.sharding import PartitionSpec as P

HID = 512
THD = 256
SHEADS = 4
SHD = 32
SFF = 512
NFFN = 4
NMB = 2
NORM_EPSILON = 1e-05
CLIP_NORM = 0.05
LEARN_RATE = 0.1
BETA_FIRST = 0.9
BETA_SECOND = 0.999
ADAM_EPSILON = 1e-08
WEIGHT_DECAY = 0.01
MASKED_SCORE = -1e30
LOG2E = math.log2(math.e)
COUNT_BASE = 64

ATT = 256
ROWS_FF = 512
CUT_FF = 512
LOG_SLOTS = 4

MESH = pl.DeviceIdType.MESH
BF, F32 = jnp.bfloat16, jnp.float32
VMEM = pl.BlockSpec(memory_space=pltpu.VMEM)
SMEM = pl.BlockSpec(memory_space=pltpu.SMEM)
ANY = pl.BlockSpec(memory_space=pl.ANY)


def dot(left, right):
    return jnp.dot(left, right, preferred_element_type=F32)


def dot_nt(left, right):
    return lax.dot_general(left, right, (((1,), (1,)), ((), ())), preferred_element_type=F32)


def layer_norm(values, gain_row, bias_row):
    center = values - jnp.mean(values, -1, keepdims=True)
    spread = jnp.mean(center * center, -1, keepdims=True)
    return center * lax.rsqrt(spread + NORM_EPSILON) * gain_row + bias_row


def sum_over(ref, n):
    s = ref[0]
    for i in range(1, n):
        s = s + ref[i]
    return s


def attend_half(
    length, first_head, low_v, project_v, query_v, key_v, value_t, context_v, logs_out, logs_v, sem
):
    tokens = low_v.shape[0]
    width = project_v.shape[2]
    for start in range(0, tokens, ROWS_FF):
        rows = slice(start, start + ROWS_FF)
        low = low_v[rows]
        query_v[rows] = (dot(low, project_v[0]) * THD**-0.5).astype(BF)
        key_v[rows] = dot(low, project_v[1]).astype(BF)
        value_t[:, rows] = dot(low, project_v[2]).T.astype(BF)
    steps = [(h, q) for h in range(width // THD) for q in range(tokens // ATT)]
    least = tokens // 2
    valid = lax.broadcasted_iota(jnp.int32, (tokens - least, ATT), 0) + least < length

    def scores_of(i):
        h, q = steps[i]
        cols = slice(h * THD, (h + 1) * THD)
        return dot_nt(key_v[:, cols], query_v[q * ATT : (q + 1) * ATT, cols])

    def copy_of(i):
        h, q = steps[i]
        slot = i % LOG_SLOTS
        there = logs_out.at[first_head + h, :, pl.ds(q * ATT, ATT)]
        return pltpu.make_async_copy(logs_v.at[slot], there, sem.at[slot])

    ahead = scores_of(0)
    for i, (h, q) in enumerate(steps):
        if i >= LOG_SLOTS:
            copy_of(i - LOG_SLOTS).wait()
        scores = ahead
        if i + 1 < len(steps):
            ahead = scores_of(i + 1)
        upper = jnp.where(valid, scores[least:], MASKED_SCORE)
        scores = jnp.concatenate([scores[:least], upper], 0)
        top = jnp.max(scores, 0, keepdims=True)
        weight = jnp.exp(scores - top)
        total = jnp.sum(weight, 0, keepdims=True)
        logs_v[i % LOG_SLOTS] = (scores - (top + jnp.log(total))).astype(BF)
        mixed = dot(value_t[h * THD : (h + 1) * THD], weight.astype(BF)) * (1.0 / total)
        context_v[q * ATT : (q + 1) * ATT, h * THD : (h + 1) * THD] = mixed.T.astype(BF)
        copy_of(i).start()
    for i in range(len(steps) - LOG_SLOTS, len(steps)):
        copy_of(i).wait()


def teacher_kernel(
    bound,
    words,
    conv,
    extra,
    norms,
    sent,
    entry,
    project,
    mixer,
    expand,
    shrink,
    leave,
    inputs_out,
    feature_out,
    logs_out,
    tiles_own,
    tiles_mate,
    trigram,
    hidden_v,
    low_v,
    entry_v,
    project_v,
    mixer_v,
    expand_v,
    shrink_v,
    leave_v,
    query_v,
    key_v,
    value_t,
    context_v,
    logs_v,
    inner_v,
    in_sem,
    logs_sem,
    swap_send,
    swap_recv,
    tile_send,
    tile_recv,
    pass_send,
    pass_recv,
):
    tokens, wide = words.shape
    breadth = entry.shape[1]
    half = project.shape[2]
    hidden_half = expand.shape[1]
    n_rows = tiles_own.shape[0]
    row, core = lax.axis_index("rows"), lax.axis_index("heads")
    mate = (row, 1 - core)

    def peer(d):
        return (lax.rem(row + d, n_rows), core)

    local = [(entry, entry_v), (project, project_v.at[0]), (mixer, mixer_v.at[0])]
    local += [(expand, expand_v.at[0]), (shrink, shrink_v.at[0]), (leave, leave_v)]
    local += [(sent, tiles_own.at[row])]
    loads = [pltpu.make_async_copy(a, b, in_sem.at[n]) for n, (a, b) in enumerate(local)]
    for c in loads:
        c.start()
    barrier = pltpu.get_barrier_semaphore()
    pl.semaphore_signal(barrier, inc=1, device_id=mate, device_id_type=MESH)

    def greet(d, carry):
        pl.semaphore_signal(barrier, inc=1, device_id=peer(d), device_id_type=MESH)
        return carry

    lax.fori_loop(1, n_rows, greet, 0)
    pl.semaphore_wait(barrier, n_rows)
    swaps = []
    for n, (a, b) in enumerate(((project, project_v), (mixer, mixer_v), (expand, expand_v), (shrink, shrink_v))):
        swaps.append(
            pltpu.make_async_remote_copy(
                src_ref=a,
                dst_ref=b.at[1],
                send_sem=swap_send.at[n],
                recv_sem=swap_recv.at[n],
                device_id=mate,
                device_id_type=MESH,
            )
        )
        swaps[-1].start()

    def tile_copy(d):
        return pltpu.make_async_remote_copy(
            src_ref=sent,
            dst_ref=tiles_own.at[row],
            send_sem=tile_send.at[d - 1],
            recv_sem=tile_recv.at[d - 1],
            device_id=peer(d),
            device_id_type=MESH,
        )

    def send_tiles(d, carry):
        tile_copy(d).start()
        return carry

    lax.fori_loop(1, n_rows, send_tiles, 0)
    rows = words[...].astype(F32)
    place = lax.broadcasted_iota(jnp.int32, (tokens, wide), 0)
    after = jnp.where(place < tokens - 1, pltpu.roll(rows, tokens - 1, 0), 0.0)
    before = jnp.where(place > 0, pltpu.roll(rows, 1, 0), 0.0)
    trigram[:, :wide] = after.astype(BF)
    trigram[:, wide : 2 * wide] = words[...]
    trigram[:, 2 * wide :] = before.astype(BF)
    spot = lax.broadcasted_iota(jnp.int32, (ATT, 1), 0)
    gain, bias = norms[0:1], norms[1:2]
    loads[0].wait()
    for start in range(0, tokens, ATT):
        r = slice(start, start + ATT)
        second = spot + start >= bound[0]
        kind = jnp.where(second, extra[tokens + 1 : tokens + 2], extra[tokens : tokens + 1])
        value = dot(trigram[r], conv[...]) + extra[r] + kind
        inputs_out[r] = value
        hidden = layer_norm(dot(value.astype(BF), entry_v[...]), gain[:, :breadth], bias[:, :breadth])
        hidden_v[r] = hidden
        low_v[r] = hidden.astype(BF)
    heads = half // THD
    for p in range(2):
        if p == 0:
            loads[1].wait()
        else:
            swaps[0].wait()
        first_head = core * heads if p == 0 else (1 - core) * heads
        attend_half(
            bound[1],
            first_head,
            low_v,
            project_v.at[p],
            query_v,
            key_v,
            value_t,
            context_v.at[p],
            logs_out,
            logs_v,
            logs_sem,
        )
    loads[2].wait()
    for c in swaps[1:]:
        c.wait()
    for c in loads[3:]:
        c.wait()

    def feed(n, carry):
        r = pl.ds(pl.multiple_of(n * ROWS_FF, ROWS_FF), ROWS_FF)
        mixed = dot(context_v[0, r], mixer_v[0]) + dot(context_v[1, r], mixer_v[1])
        first = layer_norm(
            mixed + hidden_v[r], gain[:, breadth : 2 * breadth], bias[:, breadth : 2 * breadth]
        )
        hidden_v[r] = first
        first_low = first.astype(BF)
        for p in range(2):
            for c in range(0, hidden_half, CUT_FF):
                before = dot(first_low, expand_v[p, :, c : c + CUT_FF])
                inner = 0.5 * before * (1.0 + lax.erf(before * math.sqrt(0.5)))
                inner_v[:, p * hidden_half + c : p * hidden_half + c + CUT_FF] = inner.astype(BF)
        total = dot(inner_v[:, :hidden_half], shrink_v[0]) + dot(inner_v[:, hidden_half:], shrink_v[1])
        second = layer_norm(
            total + hidden_v[r], gain[:, 2 * breadth : 3 * breadth], bias[:, 2 * breadth : 3 * breadth]
        )
        raw = dot(second.astype(BF), leave_v[...]) + inputs_out[r]
        feature_out[r] = layer_norm(
            raw, gain[:, 3 * breadth : 3 * breadth + HID], bias[:, 3 * breadth : 3 * breadth + HID]
        )
        return carry

    blocks = tokens // ROWS_FF
    lax.fori_loop(0, blocks - 1, feed, 0)

    def take_tiles(d, carry):
        tile_copy(d).wait()
        return carry

    lax.fori_loop(1, n_rows, take_tiles, 0)
    over = pltpu.make_async_remote_copy(
        src_ref=tiles_own,
        dst_ref=tiles_mate,
        send_sem=pass_send,
        recv_sem=pass_recv,
        device_id=mate,
        device_id_type=MESH,
    )
    over.start()
    feed(blocks - 1, 0)
    over.wait()


def teacher(n_rows, bound, words, conv, extra, norms, sent, entry, project, mixer, expand, shrink, leave):
    tokens, wide = words.shape
    breadth = entry.shape[1]
    half = project.shape[2]
    hidden_half = expand.shape[1]
    V, D = pltpu.VMEM, pltpu.SemaphoreType.DMA
    gathered = jax.ShapeDtypeStruct((n_rows,) + sent.shape, BF)
    return pl.pallas_call(
        teacher_kernel,
        out_shape=(
            jax.ShapeDtypeStruct((tokens, HID), F32),
            jax.ShapeDtypeStruct((tokens, HID), F32),
            jax.ShapeDtypeStruct((2 * half // THD, tokens, tokens), BF),
            gathered,
            gathered,
        ),
        in_specs=[SMEM] + [VMEM] * 4 + [ANY] * 7,
        out_specs=(VMEM, VMEM, ANY, ANY, ANY),
        scratch_shapes=[
            V((tokens, 3 * wide), BF),
            V((tokens, breadth), F32),
            V((tokens, breadth), BF),
            V(entry.shape, BF),
            V((2,) + project.shape, BF),
            V((2,) + mixer.shape, BF),
            V((2,) + expand.shape, BF),
            V((2,) + shrink.shape, BF),
            V(leave.shape, BF),
            V((tokens, half), BF),
            V((tokens, half), BF),
            V((half, tokens), BF),
            V((2, tokens, half), BF),
            V((LOG_SLOTS, tokens, ATT), BF),
            V((ROWS_FF, 2 * hidden_half), BF),
            D((7,)),
            D((LOG_SLOTS,)),
            D((4,)),
            D((4,)),
            D((n_rows - 1,)),
            D((n_rows - 1,)),
            D,
            D,
        ],
        compiler_params=pltpu.CompilerParams(
            collective_id=1, has_side_effects=True, vmem_limit_bytes=62 << 20
        ),
        cost_estimate=pl.CostEstimate(
            flops=33_000_000_000, bytes_accessed=40 << 20, transcendentals=0
        ),
    )(bound, words, conv, extra, norms, sent, entry, project, mixer, expand, shrink, leave)


QB = ATT
TB = ROWS_FF


def student_kernel(owners, bound, place_of, inputs, feature, logs, tiles_own, tiles_mate, small,
                   grads_out, lines_out,
                   logs_v, wide_w, pair_w, mixer_w, expand_w, shrink_w, leave_w,
                   low_v, narrow_v, first_v, firstlow_v, query_v, query_m, key_m, value_m, key_t, value_t,
                   context_t, contextlow_t, shift_v, blocklow_v, hidden_v, sum_v,
                   dsum_v, dcontext_v, dcontext_t, dcontext_m, dvalue_v, dkey_v, dpair_v,
                   g_leave, g_mixer, g_expand, g_shrink, small_out, slot, held, sem):
    bf, f32 = BF, F32
    tokens = inputs.shape[0]
    breadth = tiles_own.shape[2]
    core, batch = place_of[0], place_of[1]
    copies = [pltpu.make_async_copy(logs.at[h], logs_v.at[h], sem.at[h]) for h in range(SHEADS)]
    for c in copies: c.start()
    length = bound[1]
    n_owners = tiles_own.shape[0]
    slots = grads_out.shape[0] // n_owners
    lines = breadth // 2

    def clear(i, carry):
        held[i] = 0
        return carry

    lax.fori_loop(0, n_owners, clear, 0)

    def assign(i, carry):
        owner = owners[i]
        slot[i] = owner * slots + held[owner]
        held[owner] = held[owner] + 1
        return carry

    lax.fori_loop(0, owners.shape[0], assign, 0)
    digits = tiles_own[0, slots * lines :].astype(F32)
    for i in range(1, n_owners):
        digits = digits + tiles_own[i, slots * lines :].astype(F32)
    digits = digits[0:1]
    at_lane = lax.broadcasted_iota(jnp.int32, digits.shape, 1)
    digits = jnp.where(at_lane == 2 * batch, digits * COUNT_BASE, jnp.where(at_lane == 2 * batch + 1, digits, 0.0))
    inverse = 1.0 / jnp.sum(digits, 1, keepdims=True)
    grads_out[...] = jnp.zeros_like(grads_out)
    small_out[...] = jnp.zeros_like(small_out)
    g_leave[...] = jnp.zeros_like(g_leave); g_mixer[...] = jnp.zeros_like(g_mixer)
    g_expand[...] = jnp.zeros_like(g_expand); g_shrink[...] = jnp.zeros_like(g_shrink)
    dvalue_v[...] = jnp.zeros_like(dvalue_v); dkey_v[...] = jnp.zeros_like(dkey_v)
    nin = HID // breadth; nff = SFF // breadth
    at = lambda j: slice(j*breadth, (j+1)*breadth)
    def load(i, put):
        owner, rank = slot[i] // slots, slot[i] % slots
        from_line = pl.ds(pl.multiple_of(rank * lines, lines), lines)
        put(pl.multiple_of(core * lines, lines), tiles_own[owner, from_line])
        put(pl.multiple_of((1 - core) * lines, lines), tiles_mate[owner, from_line])

    def fill(ref, row, col):
        def put(line, value):
            ref[pl.ds(row * breadth + line, lines), at(col)] = value

        return put

    for j in range(nin):
        load(j, fill(wide_w, j, 0))
        load(nin + j, fill(wide_w, j, 1))
    load(2 * nin, fill(pair_w, 0, 0))
    load(2 * nin + 1, fill(pair_w, 0, 1))
    load(2 * nin + 2, fill(mixer_w, 0, 0))
    first_ff = 2*nin+3
    for b in range(NFFN):
        for j in range(nff):
            load(first_ff + b * nff + j, fill(expand_w.at[b], 0, j))
            load(first_ff + (NFFN + b) * nff + j, fill(shrink_w.at[b], j, 0))
    first_leave = first_ff + 2*NFFN*nff
    for j in range(nin):
        load(first_leave + j, fill(leave_w, 0, j))
    gain = lambda n: small[0:1, at(n)]
    bias = lambda n: small[1:2, at(n)]
    tail = (2+NFFN)*breadth
    gain_out, bias_out = small[0:1, tail:], small[1:2, tail:]
    lane = lax.broadcasted_iota(jnp.int32, (1, breadth), 1) // SHD
    masks = [(lane == h) for h in range(SHEADS)]
    for start in range(0, tokens, TB):
        r = slice(start, start+TB)
        low = inputs[r].astype(bf)
        low_v[r] = low
        both = dot(low, wide_w[...])
        narrow = both[:, :breadth]
        narrow_v[r] = narrow
        value = both[:, breadth:]
        first = narrow*gain(0) + bias(0)
        first_v[r] = first
        firstlow_v[r] = first.astype(bf)
        pair = dot(first.astype(bf), pair_w[...])
        query, key = pair[:, :breadth], pair[:, breadth:]
        query_v[r] = query.astype(bf)
        for h in range(SHEADS):
            query_m[h, r] = jnp.where(masks[h], query, 0.0).astype(bf)
            key_m[h, r] = jnp.where(masks[h], key, 0.0).astype(bf)
            value_m[h, r] = jnp.where(masks[h], value, 0.0).astype(bf)
        key_t[:, r] = key.T.astype(bf)
        value_t[:, r] = value.T.astype(bf)
    scale = SHD**-0.5
    scale2 = scale*LOG2E
    least = tokens//2
    valid = lax.broadcasted_iota(jnp.int32, (tokens-least, QB), 0) + least < length
    def scores_of(h, r):
        scores = dot_nt(key_m[h], query_v[r])
        return jnp.concatenate([scores[:least], jnp.where(valid, scores[least:], MASKED_SCORE)], 0)
    def forward(n, carry):
        r = pl.ds(pl.multiple_of(n*QB, QB), QB)
        ahead = scores_of(0, r)
        parts = []
        for h in range(SHEADS):
            scores = ahead
            if h+1 < SHEADS: ahead = scores_of(h+1, r)
            top = jnp.max(scores, 0, keepdims=True)
            weight = jnp.exp2((scores-top)*scale2)
            total = jnp.sum(weight, 0, keepdims=True)
            shift_v[h:h+1, r] = top*scale2 + jnp.log2(total)
            parts.append(dot(value_t[h*SHD:(h+1)*SHD], weight.astype(bf)) * (1.0/total))
        mixed = jnp.concatenate(parts, 0)
        context_t[:, r] = mixed
        contextlow_t[:, r] = mixed.astype(bf)
        return carry
    lax.fori_loop(0, tokens//QB, forward, 0)
    def row_sums(n, d, value):
        small_out[0:1, at(n)] += jnp.sum(d*value, 0, keepdims=True)
        small_out[1:2, at(n)] += jnp.sum(d, 0, keepdims=True)
    def feed(n, loss):
        r = pl.ds(pl.multiple_of(n*TB, TB), TB)
        place = lax.broadcasted_iota(jnp.int32, (TB, 1), 0) + n*TB
        weight = jnp.where(place < length, inverse, 0.0)
        context = context_t[:, r].T.astype(bf)
        mixed_sum = dot(context, mixer_w[...]) + first_v[r]
        current = mixed_sum*gain(1) + bias(1)
        for b in range(NFFN):
            low = current.astype(bf)
            blocklow_v[b] = low
            hidden = jnp.maximum(dot(low, expand_w[b]), 0.0).astype(bf)
            hidden_v[b] = hidden
            total = dot(hidden, shrink_w[b]) + current
            sum_v[b] = total
            current = total*gain(2+b) + bias(2+b)
        low = current.astype(bf)
        joined = dot(low, leave_w[...]) + inputs[r]
        differ = joined*gain_out + bias_out - feature[r]
        loss = loss + jnp.sum(weight*jnp.mean(differ*differ, -1, keepdims=True), 0, keepdims=True)
        outer = differ*(weight*(2.0/HID))
        small_out[0:1, tail:] += jnp.sum(outer*joined, 0, keepdims=True)
        small_out[1:2, tail:] += jnp.sum(outer, 0, keepdims=True)
        back = (outer*gain_out).astype(bf)
        g_leave[...] += dot(current.T.astype(bf), back)
        d = dot_nt(back, leave_w[...])
        for b in reversed(range(NFFN)):
            row_sums(2+b, d, sum_v[b])
            d_sum = d*gain(2+b)
            d_branch = d_sum.astype(bf)
            hidden = hidden_v[b]
            g_shrink[b] += dot(d_sum.T.astype(bf), hidden)
            d_before = jnp.where(hidden > 0, dot_nt(d_branch, shrink_w[b]), 0.0).astype(bf)
            g_expand[b] += dot(blocklow_v[b].T, d_before)
            d = d_sum + dot_nt(d_before, expand_w[b])
        row_sums(1, d, mixed_sum)
        d_sum = d*gain(1)
        dsum_v[r] = d_sum
        d_mixed = d_sum.astype(bf)
        g_mixer[...] += dot(contextlow_t[:, r], d_mixed)
        d_context = dot_nt(d_mixed, mixer_w[...]).astype(bf)
        dcontext_v[r] = d_context
        dcontext_t[:, r] = d_context.astype(f32).T
        for h in range(SHEADS):
            dcontext_m[h, r] = jnp.where(masks[h], d_context, jnp.zeros_like(d_context))
        return loss
    loss = jnp.zeros((1, 1), f32)
    loss = lax.fori_loop(0, tokens//TB, feed, loss)
    for c in copies: c.wait()
    def backward(n, loss):
        r = pl.ds(pl.multiple_of(n*QB, QB), QB)
        place = lax.broadcasted_iota(jnp.int32, (1, QB), 1) + n*QB
        share = jnp.where(place < length, inverse/SHEADS, 0.0)
        ahead = (scores_of(0, r), dot_nt(value_m[0], dcontext_v[r]))
        parts = []
        for h in range(SHEADS):
            scores, d_weight = ahead
            if h+1 < SHEADS: ahead = (scores_of(h+1, r), dot_nt(value_m[h+1], dcontext_v[r]))
            shift = shift_v[h:h+1, r]
            weight = jnp.exp2(scores*scale2 - shift)
            target_logs = logs_v[h, :, r].astype(f32)
            target = jnp.exp2(target_logs*LOG2E)
            target_sum = jnp.sum(target, 0, keepdims=True)
            gap = jnp.sum(target*(target_logs - jnp.maximum(scores, -1e29)*scale), 0, keepdims=True) + target_sum*(shift*(1.0/LOG2E))
            loss = loss + jnp.sum(share*gap, 1, keepdims=True)
            heads = slice(h*SHD, (h+1)*SHD)
            along = jnp.sum(context_t[heads, r]*dcontext_t[heads, r], 0, keepdims=True)
            d_scores = weight*(d_weight - (along - share*target_sum)) - share*target
            d_low = d_scores.astype(bf)
            dvalue_v[...] += dot(weight.astype(bf), dcontext_m[h, r])
            dkey_v[...] += dot(d_low, query_m[h, r])
            parts.append(dot(key_t[heads], d_low))
        dpair_v[r, at(0)] = (jnp.concatenate(parts, 0)*scale).T.astype(bf)
        return loss
    loss = lax.fori_loop(0, tokens//QB, backward, loss)
    lines_out[...] = jnp.zeros_like(lines_out)
    n_lines = small.shape[1] // breadth
    lines_out[2*n_lines:2*n_lines+1, 0:1] = loss
    dpair_v[:, at(1)] = (dkey_v[...]*scale).astype(bf)
    d_pair = dpair_v[...]
    d_first = dsum_v[...] + dot_nt(d_pair, pair_w[...])
    row_sums(0, d_first, narrow_v[...])
    g_pair = dot(first_v[...].T.astype(bf), d_pair)
    wide_t = jnp.concatenate([(d_first*gain(0)).T.astype(bf), dvalue_v[...].T.astype(bf)], 0)
    g_wide = dot(wide_t, low_v[...])
    for j in range(nin):
        grads_out[slot[j]] = g_wide[:breadth, at(j)].T.astype(bf)
        grads_out[slot[nin+j]] = g_wide[breadth:, at(j)].T.astype(bf)
        grads_out[slot[first_leave+j]] = g_leave[:, at(j)].astype(bf)
    grads_out[slot[2*nin]] = g_pair[:, at(0)].astype(bf)
    grads_out[slot[2*nin+1]] = g_pair[:, at(1)].astype(bf)
    grads_out[slot[2*nin+2]] = g_mixer[...].astype(bf)
    for b in range(NFFN):
        for j in range(nff):
            grads_out[slot[first_ff + b*nff + j]] = g_expand[b, :, at(j)].astype(bf)
            grads_out[slot[first_ff + (NFFN+b)*nff + j]] = g_shrink[b, :, at(j)].T.astype(bf)
    for j in range(n_lines):
        lines_out[j:j+1] = small_out[0:1, at(j)]
        lines_out[n_lines+j:n_lines+j+1] = small_out[1:2, at(j)]


def student(owners, bound, place_of, inputs, feature, logs, tiles_own, tiles_mate, small, slots):
    tokens = inputs.shape[0]
    n_owners, _, w = tiles_own.shape
    n_lines = 8 * -(-(2 * small.shape[1] // w + 1) // 8)
    V, D = pltpu.VMEM, pltpu.SemaphoreType.DMA
    return pl.pallas_call(
        student_kernel,
        out_shape=(
            jax.ShapeDtypeStruct((n_owners * slots, w, w), BF),
            jax.ShapeDtypeStruct((n_lines, w), F32),
        ),
        in_specs=[SMEM, SMEM, SMEM, VMEM, VMEM, ANY, VMEM, VMEM, VMEM],
        out_specs=(VMEM, VMEM),
        scratch_shapes=[
            V(logs.shape, BF), V((HID, 2 * w), BF), V((w, 2 * w), BF), V((w, w), BF),
            V((NFFN, w, SFF), BF), V((NFFN, SFF, w), BF), V((w, HID), BF),
            V((tokens, HID), BF), V((tokens, w), F32), V((tokens, w), F32), V((tokens, w), BF), V((tokens, w), BF),
            V((SHEADS, tokens, w), BF), V((SHEADS, tokens, w), BF), V((SHEADS, tokens, w), BF), V((w, tokens), BF), V((w, tokens), BF),
            V((w, tokens), F32), V((w, tokens), BF), V((8, tokens), F32), V((NFFN, TB, w), BF), V((NFFN, TB, SFF), BF), V((NFFN, TB, w), F32),
            V((tokens, w), F32), V((tokens, w), BF), V((w, tokens), F32), V((SHEADS, tokens, w), BF), V((tokens, w), F32), V((tokens, w), F32), V((tokens, 2 * w), BF),
            V((w, HID), F32), V((w, w), F32), V((NFFN, w, SFF), F32), V((NFFN, w, SFF), F32),
            V((8, small.shape[1]), F32),
            pltpu.SMEM(owners.shape, jnp.int32), pltpu.SMEM((n_owners,), jnp.int32),
            D((SHEADS,)),
        ],
        compiler_params=pltpu.CompilerParams(vmem_limit_bytes=58 << 20),
        cost_estimate=pl.CostEstimate(flops=15_000_000_000, bytes_accessed=16 << 20, transcendentals=0),
    )(owners, bound, place_of, inputs, feature, logs, tiles_own, tiles_mate, small)


def reduce_kernel(side, deep, slots, grads, small, tiles_out, stats_out,
                  pair_in, first, first_in, second, second_in, third, third_in, half_own, half_in,
                  small_pair, small_a, small_b, small_z, norm_all, norm_own,
                  pair_send, pair_recv, first_send, first_recv, second_send, second_recv, third_send, third_recv,
                  half_send, half_recv, sp_send, sp_recv, sa_send, sa_recv, sb_send, sb_recv, sz_send, sz_recv, n_send, n_recv):
    bf, f32 = jnp.bfloat16, jnp.float32
    row, core = lax.axis_index("rows"), lax.axis_index("heads")
    plane = side*side
    z = row // plane
    y = (row // side) % side
    x = row % side
    total = plane*deep
    lines = grads.shape[-2]//2
    mate = (row, 1-core)
    mine = core*lines
    theirs = (1-core)*lines
    straight = core == 0
    a = jnp.where(straight, x, y)
    b = jnp.where(straight, y, x)
    pa = jnp.where(straight, y, x)
    def row_at(xx, yy, zz):
        return zz*plane + yy*side + xx
    def along_a(aa):
        return (jnp.where(straight, row_at(aa, y, z), row_at(x, aa, z)), core)
    def along_b(bb):
        return (jnp.where(straight, row_at(x, bb, z), row_at(bb, y, z)), core)
    def along_z(zz):
        return (row_at(x, y, zz), core)
    barrier = pltpu.get_barrier_semaphore()
    n_devices = 2*total
    me = row*2 + core
    def greet(i, carry):
        peer = lax.rem(me + i, n_devices)
        pl.semaphore_signal(barrier, inc=1, device_id=(peer // 2, peer % 2), device_id_type=MESH)
        return carry
    lax.fori_loop(1, n_devices, greet, 0)
    pl.semaphore_wait(barrier, n_devices-1)

    def remote(src, dst, send, recv, peer):
        return pltpu.make_async_remote_copy(src_ref=src, dst_ref=dst, send_sem=send, recv_sem=recv, device_id=peer, device_id_type=MESH)

    small_pair_copy = remote(small, small_pair, sp_send, sp_recv, mate)
    small_pair_copy.start()
    order = list(range(1, side)) + [0]
    for d in order:
        piece = lax.rem(pa + d, side)
        by_y = remote(grads.at[:, piece, :, :, pl.ds(theirs, lines), :], pair_in.at[d], pair_send.at[d], pair_recv.at[d], mate)
        by_x = remote(grads.at[:, :, piece, :, pl.ds(theirs, lines), :], pair_in.at[d], pair_send.at[d], pair_recv.at[d], mate)
        @pl.when(straight)
        def _(): by_y.start()
        @pl.when(jnp.logical_not(straight))
        def _(): by_x.start()
    def pair_wait(d):
        return remote(first.at[d], pair_in.at[d], pair_send.at[d], pair_recv.at[d], mate)
    first_copies = []
    for d in order:
        pair_wait(d).wait_recv()
        aa = lax.rem(a + d, side)
        def add(i, carry):
            zz, bb = i // side, i % side
            xx, yy = jnp.where(straight, aa, bb), jnp.where(straight, bb, aa)
            own = grads[zz, yy, xx, :, pl.ds(mine, lines), :].astype(f32)
            first[d, zz, bb] = (own + pair_in[d, zz, bb].astype(f32)).astype(bf)
            return carry
        lax.fori_loop(0, deep*side, add, 0)
        if d:
            c = remote(first.at[d], first_in.at[d-1], first_send.at[d-1], first_recv.at[d-1], along_a(aa))
            c.start(); first_copies.append(c)
    small_pair_copy.wait()
    small_a[x] = small[...] + small_pair[...]
    sa = []
    for d in range(1, side):
        c = remote(small_a.at[x], small_a.at[x], sa_send.at[d-1], sa_recv.at[d-1], (row_at(lax.rem(x+d, side), y, z), core))
        c.start(); sa.append(c)
    for c in first_copies: c.wait_recv()
    second_copies = []
    for d in order:
        bb = lax.rem(b + d, side)
        def add(zz, carry):
            s = first[0, zz, bb].astype(f32)
            for j in range(side-1): s = s + first_in[j, zz, bb].astype(f32)
            second[d, zz] = s.astype(bf)
            return carry
        lax.fori_loop(0, deep, add, 0)
        if d:
            c = remote(second.at[d], second_in.at[d-1], second_send.at[d-1], second_recv.at[d-1], along_b(bb))
            c.start(); second_copies.append(c)
    for c in sa: c.wait()
    small_b[y] = sum_over(small_a, side)
    sb = []
    for d in range(1, side):
        c = remote(small_b.at[y], small_b.at[y], sb_send.at[d-1], sb_recv.at[d-1], (row_at(x, lax.rem(y+d, side), z), core))
        c.start(); sb.append(c)
    for c in second_copies: c.wait_recv()
    third_copies = []
    own = None
    for d in list(range(1, deep)) + [0]:
        zz = lax.rem(z + d, deep)
        s = second[0, zz].astype(f32)
        for j in range(side-1): s = s + second_in[j, zz].astype(f32)
        if d:
            third[d-1] = s.astype(bf)
            c = remote(third.at[d-1], third_in.at[d-1], third_send.at[d-1], third_recv.at[d-1], along_z(zz))
            c.start(); third_copies.append(c)
        else:
            own = s
    for c in sb: c.wait()
    small_z[z] = sum_over(small_b, side)
    sz = []
    for d in range(1, deep):
        c = remote(small_z.at[z], small_z.at[z], sz_send.at[d-1], sz_recv.at[d-1], along_z(lax.rem(z+d, deep)))
        c.start(); sz.append(c)
    for c in third_copies: c.wait_recv()
    for j in range(deep-1): own = own + third_in[j].astype(f32)
    half_own[...] = own
    half_copy = remote(half_own, half_in, half_send, half_recv, mate)
    half_copy.start()
    part = jnp.sum(jnp.sum(own*own, 0), 0, keepdims=True)
    norm_own[...] = jnp.broadcast_to(part, norm_own.shape)
    norm_all[me] = norm_own[...]
    def tell(i, carry):
        peer = lax.rem(me + i, n_devices)
        remote(norm_own, norm_all.at[me], n_send.at[i-1], n_recv.at[i-1], (peer // 2, peer % 2)).start()
        return carry
    lax.fori_loop(1, n_devices, tell, 0)
    tiles_out[:, pl.ds(mine, lines), :] = own
    half_copy.wait()
    tiles_out[:, pl.ds(theirs, lines), :] = half_in[...]
    for c in sz: c.wait()
    small_total = sum_over(small_z, deep)
    def hear(i, carry):
        remote(norm_own, norm_all.at[me], n_send.at[i-1], n_recv.at[i-1], mate).wait()
        return carry
    lax.fori_loop(1, n_devices, hear, 0)
    def gather(i, s):
        return s + norm_all[i]
    squares = lax.fori_loop(0, n_devices, gather, jnp.zeros(norm_own.shape, f32))
    stats_out[0] = small_total[0:8]
    stats_out[1] = small_total[8:16]
    stats_out[2] = small_total[16:24]
    stats_out[3] = squares
    for d in order: pair_wait(d).wait_send()
    for c in first_copies + second_copies + third_copies: c.wait_send()

def reduce_call(n_rows, grads, small):
    deep = 4
    side = math.isqrt(n_rows // deep)
    assert side*side*deep == n_rows
    slots = grads.shape[0] // n_rows
    wide, lanes = grads.shape[1:]
    lines = wide//2
    bf, f32 = jnp.bfloat16, jnp.float32
    grads = grads.reshape(deep, side, side, slots, wide, lanes)
    V, D = pltpu.VMEM, pltpu.SemaphoreType.DMA
    s1, d1, n = side-1, deep-1, 2*n_rows
    return pl.pallas_call(functools.partial(reduce_kernel, side, deep, slots),
        out_shape=(jax.ShapeDtypeStruct((slots, wide, lanes), f32), jax.ShapeDtypeStruct((4, 8, lanes), f32)),
        in_specs=[VMEM, VMEM], out_specs=(VMEM, VMEM),
        scratch_shapes=[V((side, deep, side, slots, lines, lanes), bf), V((side, deep, side, slots, lines, lanes), bf), V((s1, deep, side, slots, lines, lanes), bf),
            V((side, deep, slots, lines, lanes), bf), V((s1, deep, slots, lines, lanes), bf), V((d1, slots, lines, lanes), bf), V((d1, slots, lines, lanes), bf),
            V((slots, lines, lanes), f32), V((slots, lines, lanes), f32),
            V(small.shape, f32), V((side,)+small.shape, f32), V((side,)+small.shape, f32), V((deep,)+small.shape, f32),
            V((n, 8, lanes), f32), V((8, lanes), f32),
            D((side,)), D((side,)), D((s1,)), D((s1,)), D((s1,)), D((s1,)), D((d1,)), D((d1,)), D, D, D, D, D((s1,)), D((s1,)), D((s1,)), D((s1,)), D((d1,)), D((d1,)), D((n-1,)), D((n-1,))],
        compiler_params=pltpu.CompilerParams(collective_id=0, has_side_effects=True, vmem_limit_bytes=48<<20),
        cost_estimate=pl.CostEstimate(flops=10_000_000, bytes_accessed=8<<20, transcendentals=0),
    )(grads, small)


def update_kernel(
    owners, step, own, summed, stats, weight, first, second, small, small_first, small_second,
    loss_out, norm_out, tiles_out, first_out, second_out, small_out, small_first_out, small_second_out, small_grad_out,
    small_v,
):
    breadth = summed.shape[2]
    n_lines = small.shape[1] // breadth
    steps = step[0]
    first_fix = 1.0 - lax.fori_loop(0, steps, lambda i, p: p * BETA_FIRST, jnp.float32(1.0))
    second_fix = 1.0 - lax.fori_loop(0, steps, lambda i, p: p * BETA_SECOND, jnp.float32(1.0))

    def adam(w, m, v, g, decay):
        m = BETA_FIRST * m + (1.0 - BETA_FIRST) * g
        v = BETA_SECOND * v + (1.0 - BETA_SECOND) * g * g
        change = m / first_fix / (jnp.sqrt(v / second_fix) + ADAM_EPSILON) + decay * w
        return w - LEARN_RATE * change, m, v

    line = lambda n: stats[n // 8, n % 8 : n % 8 + 1]
    squares = stats[3, 0:1]
    for n in range(2 * n_lines):
        squares = squares + line(n) * line(n)
    norm = jnp.sqrt(jnp.sum(squares, 1, keepdims=True))
    norm_out[...] = norm
    loss_out[...] = line(2 * n_lines)[:, 0:1]
    factor = CLIP_NORM / jnp.maximum(norm, CLIP_NORM)
    for n in range(n_lines):
        cols = slice(n * breadth, (n + 1) * breadth)
        small_v[0:1, cols] = line(n)
        small_v[1:2, cols] = line(n_lines + n)
    small_grad = small_v[0:2] * factor
    small_grad_out[...] = small_grad
    w, m, v = adam(small[...], small_first[...], small_second[...], small_grad, 0.0)
    small_out[...] = w
    small_first_out[...] = m
    small_second_out[...] = v

    def count(i, n):
        return n + (owners[i] == own[0]).astype(jnp.int32)

    held = lax.fori_loop(0, owners.shape[0], count, 0)
    for s in range(summed.shape[0]):
        keep = held > s
        w, m, v = adam(weight[s], first[s], second[s], summed[s] * factor, WEIGHT_DECAY)
        tiles_out[s] = jnp.where(keep, w, 0.0)
        first_out[s] = jnp.where(keep, m, 0.0)
        second_out[s] = jnp.where(keep, v, 0.0)


def update(owners, step, own, summed, stats, weight, first, second, small, small_first, small_second):
    one = jax.ShapeDtypeStruct((1, 1), F32)
    tile = jax.ShapeDtypeStruct(weight.shape, F32)
    row = jax.ShapeDtypeStruct(small.shape, F32)
    return pl.pallas_call(
        update_kernel,
        out_shape=(one, one, tile, tile, tile, row, row, row, row),
        in_specs=[SMEM] * 3 + [VMEM] * 8,
        out_specs=(VMEM,) * 9,
        scratch_shapes=[pltpu.VMEM((8, small.shape[1]), F32)],
        compiler_params=pltpu.CompilerParams(vmem_limit_bytes=24 << 20),
        cost_estimate=pl.CostEstimate(flops=2_000_000, bytes_accessed=2 << 20, transcendentals=0),
    )(owners, step, own, summed, stats, weight, first, second, small, small_first, small_second)


def on_device(
    token_ids,
    bounds,
    micro_batch,
    owners,
    step_count,
    word_table,
    conv_weight,
    embed_extra,
    teacher_entry,
    teacher_project,
    teacher_mixer,
    teacher_expand,
    teacher_shrink,
    teacher_leave,
    teacher_norms,
    tile_weight,
    tile_first,
    tile_second,
    small_weight,
    small_first,
    small_second,
):
    core = lax.axis_index("heads")
    n_rows = lax.axis_size("rows")
    slots, breadth, _ = tile_weight.shape
    assert token_ids.shape[0] == lax.axis_size("heads")
    lengths = bounds[:, 1]
    batch_range = jnp.arange(NMB, dtype=jnp.int32)
    chosen = micro_batch[:, None] == batch_range[None, :]
    local = jnp.sum(jnp.where(chosen, lengths[:, None], 0), 0)
    digits = jnp.stack([local // COUNT_BASE, local % COUNT_BASE], 1).reshape(1, 2 * NMB)
    digits = jnp.pad(digits.astype(BF), ((0, 15), (0, breadth - 2 * NMB)))
    lines = breadth // 2
    half = lax.dynamic_slice_in_dim(tile_weight, core * lines, lines, 1).astype(BF)
    sent = jnp.concatenate([half.reshape(slots * lines, breadth), digits], 0)
    row_ids, bound, batch = (
        lax.dynamic_index_in_dim(whole, core, 0, keepdims=False)
        for whole in (token_ids, bounds, micro_batch)
    )
    words = word_table[row_ids]
    place_of = jnp.stack([core, batch])
    inputs, feature, logs, tiles_own, tiles_mate = teacher(
        n_rows,
        bound,
        words,
        conv_weight,
        embed_extra,
        teacher_norms,
        sent,
        teacher_entry,
        teacher_project.transpose(1, 0, 2),
        teacher_mixer,
        teacher_expand,
        teacher_shrink,
        teacher_leave,
    )
    grads, small_lines = student(
        owners, bound, place_of, inputs, feature, logs, tiles_own, tiles_mate, small_weight, slots
    )
    summed, stats = reduce_call(n_rows, grads, small_lines)
    own = lax.axis_index("rows")[None]
    loss, norm, *rest = update(
        owners,
        step_count,
        own,
        summed,
        stats,
        tile_weight,
        tile_first,
        tile_second,
        small_weight,
        small_first,
        small_second,
    )
    return (loss[0, 0], norm[0, 0], *rest)


def solution(mesh):
    placed = (
        P("rows", None),
        P("rows", None),
        P("rows"),
        P(),
        P(),
        P(),
        P(),
        P(),
        P(),
        P(None, None, "heads"),
        P("heads", None),
        P(None, "heads"),
        P("heads", None),
        P(),
        P(),
        P("rows", None, None),
        P("rows", None, None),
        P("rows", None, None),
        P(),
        P(),
        P(),
    )
    tiles = P("rows", None, None)
    return jax.shard_map(
        on_device,
        mesh=mesh,
        in_specs=placed,
        out_specs=(P(), P(), tiles, tiles, tiles, P(), P(), P(), P()),
        check_vma=False,
    )
```

```python
import functools
import math

import jax
import jax.numpy as jnp
from jax import lax
from jax.experimental import pallas as pl
from jax.experimental.pallas import tpu as pltpu
from jax.sharding import PartitionSpec as P

HID = 512
THD = 256
SHEADS = 4
SHD = 32
SFF = 512
NFFN = 4
NMB = 2
NORM_EPSILON = 1e-05
CLIP_NORM = 0.05
LEARN_RATE = 0.1
BETA_FIRST = 0.9
BETA_SECOND = 0.999
ADAM_EPSILON = 1e-08
WEIGHT_DECAY = 0.01
MASKED_SCORE = -1e30
LOG2E = math.log2(math.e)
COUNT_BASE = 64

ATT = 256
ROWS_FF = 512
CUT_FF = 512
LOG_SLOTS = 4

MESH = pl.DeviceIdType.MESH
BF, F32 = jnp.bfloat16, jnp.float32
VMEM = pl.BlockSpec(memory_space=pltpu.VMEM)
SMEM = pl.BlockSpec(memory_space=pltpu.SMEM)
ANY = pl.BlockSpec(memory_space=pl.ANY)


def dot(left, right):
    return jnp.dot(left, right, preferred_element_type=F32)


def dot_nt(left, right):
    return lax.dot_general(left, right, (((1,), (1,)), ((), ())), preferred_element_type=F32)


def layer_norm(values, gain_row, bias_row):
    center = values - jnp.mean(values, -1, keepdims=True)
    spread = jnp.mean(center * center, -1, keepdims=True)
    return center * lax.rsqrt(spread + NORM_EPSILON) * gain_row + bias_row


def sum_over(ref, n):
    s = ref[0]
    for i in range(1, n):
        s = s + ref[i]
    return s


def split_rows(refs, rows=64):
    for start in range(0, refs.shape[-2], rows):
        yield slice(start, start + rows)


def column_max(ref):
    best = None
    for c in split_rows(ref):
        best = ref[c] if best is None else jnp.maximum(best, ref[c])
    return jnp.max(best, 0, keepdims=True)


def attend_half(
    length,
    first_head,
    low_v,
    project_v,
    query_v,
    key_v,
    value_t,
    context_v,
    logs_out,
    sums_out,
    logs_v,
    scores_v,
    weight_v,
    sem,
    pending,
):
    tokens = low_v.shape[0]
    width = project_v.shape[2]
    for start in range(0, tokens, ROWS_FF):
        rows = slice(start, start + ROWS_FF)
        low = low_v[rows]
        query_v[rows] = (dot(low, project_v[0]) * THD**-0.5).astype(BF)
        key_v[rows] = dot(low, project_v[1]).astype(BF)
        value_t[:, rows] = dot(low, project_v[2]).T.astype(BF)
    steps = [(h, q) for h in range(width // THD) for q in range(tokens // ATT)]
    least = tokens // 2

    def scores_of(i):
        h, q = steps[i]
        cols = slice(h * THD, (h + 1) * THD)
        query = query_v[q * ATT : (q + 1) * ATT, cols]
        scores_v[i % 2, :least] = dot_nt(key_v[:least, cols], query)
        valid = lax.broadcasted_iota(jnp.int32, (tokens - least, ATT), 0) + least < length
        scores_v[i % 2, least:] = jnp.where(valid, dot_nt(key_v[least:, cols], query), MASKED_SCORE)

    scores_of(0)
    for i, (h, q) in enumerate(steps):
        if len(pending) == LOG_SLOTS:
            pending.pop(0).wait()
        if i + 1 < len(steps):
            scores_of(i + 1)
        at = i % LOG_SLOTS
        scores, weight, logs = scores_v.at[i % 2], weight_v.at[i % 2], logs_v.at[at]
        top = column_max(scores)
        part = 0.0
        for c in split_rows(scores):
            piece = jnp.exp(scores[c] - top)
            weight[c] = piece.astype(BF)
            part = part + piece
        total = jnp.sum(part, 0, keepdims=True)
        shift = top + jnp.log(total)
        part = 0.0
        for c in split_rows(scores):
            piece = (scores[c] - shift).astype(BF)
            logs[c] = piece
            part = part + jnp.exp(piece.astype(F32))
        sums_out[first_head + h, :, q * ATT : (q + 1) * ATT] = jnp.sum(part, 0, keepdims=True)
        mixed = dot(value_t[h * THD : (h + 1) * THD], weight[...]) * (1.0 / total)
        context_v[q * ATT : (q + 1) * ATT, h * THD : (h + 1) * THD] = mixed.T.astype(BF)
        there = logs_out.at[first_head + h, :, pl.ds(q * ATT, ATT)]
        pending.append(pltpu.make_async_copy(logs, there, sem.at[at]))
        pending[-1].start()
    assert len(steps) % LOG_SLOTS == 0


def teacher_kernel(
    bounds,
    micro_batch,
    words,
    conv,
    extra,
    norms,
    weight,
    entry,
    project,
    mixer,
    expand,
    shrink,
    leave,
    inputs_out,
    feature_out,
    logs_out,
    sums_out,
    tiles_own,
    tiles_mate,
    trigram,
    hidden_v,
    low_v,
    entry_v,
    project_v,
    mixer_v,
    expand_v,
    shrink_v,
    leave_v,
    query_v,
    key_v,
    value_t,
    context_v,
    logs_v,
    scores_v,
    weight_v,
    inner_v,
    sent,
    in_sem,
    logs_sem,
    swap_send,
    swap_recv,
    tile_send,
    tile_recv,
    pass_send,
    pass_recv,
):
    tokens, wide = words.shape
    breadth = entry.shape[1]
    half = project.shape[2]
    hidden_half = expand.shape[1]
    n_rows = tiles_own.shape[0]
    row, core = lax.axis_index("rows"), lax.axis_index("heads")
    mate = (row, 1 - core)
    start_at, length = bounds[core, 0], bounds[core, 1]
    slots, _, lanes = weight.shape
    lines = weight.shape[1] // 2
    for n in range(slots):
        sent[n * lines : (n + 1) * lines] = weight[n, pl.ds(core * lines, lines)].astype(BF)
    lane = lax.broadcasted_iota(jnp.int32, (16, lanes), 1)
    digits = jnp.zeros((16, lanes), F32)
    for m in range(NMB):
        held = jnp.int32(0)
        for n in range(micro_batch.shape[0]):
            held = held + jnp.where(micro_batch[n] == m, bounds[n, 1], 0)
        digits = jnp.where(lane == 2 * m, (held // COUNT_BASE).astype(F32), digits)
        digits = jnp.where(lane == 2 * m + 1, (held % COUNT_BASE).astype(F32), digits)
    sent[slots * lines :] = digits.astype(BF)

    def peer(d):
        return (lax.rem(row + d, n_rows), core)

    local = [(entry, entry_v), (project, project_v.at[0]), (mixer, mixer_v.at[0])]
    local += [(expand, expand_v.at[0]), (shrink, shrink_v.at[0]), (leave, leave_v)]
    local += [(sent, tiles_own.at[row])]
    loads = [pltpu.make_async_copy(a, b, in_sem.at[n]) for n, (a, b) in enumerate(local)]
    for c in loads:
        c.start()
    barrier = pltpu.get_barrier_semaphore()
    pl.semaphore_signal(barrier, inc=1, device_id=mate, device_id_type=MESH)

    def greet(d, carry):
        pl.semaphore_signal(barrier, inc=1, device_id=peer(d), device_id_type=MESH)
        return carry

    lax.fori_loop(1, n_rows, greet, 0)
    pl.semaphore_wait(barrier, n_rows)
    swaps = []
    for n, (a, b) in enumerate(((project, project_v), (mixer, mixer_v), (expand, expand_v), (shrink, shrink_v))):
        swaps.append(
            pltpu.make_async_remote_copy(
                src_ref=a,
                dst_ref=b.at[1],
                send_sem=swap_send.at[n],
                recv_sem=swap_recv.at[n],
                device_id=mate,
                device_id_type=MESH,
            )
        )
        swaps[-1].start()

    def tile_copy(d):
        return pltpu.make_async_remote_copy(
            src_ref=sent,
            dst_ref=tiles_own.at[row],
            send_sem=tile_send.at[d - 1],
            recv_sem=tile_recv.at[d - 1],
            device_id=peer(d),
            device_id_type=MESH,
        )

    def send_tiles(d, carry):
        tile_copy(d).start()
        return carry

    lax.fori_loop(1, n_rows, send_tiles, 0)
    rows = words[...].astype(F32)
    place = lax.broadcasted_iota(jnp.int32, (tokens, wide), 0)
    after = jnp.where(place < tokens - 1, pltpu.roll(rows, tokens - 1, 0), 0.0)
    before = jnp.where(place > 0, pltpu.roll(rows, 1, 0), 0.0)
    trigram[:, :wide] = after.astype(BF)
    trigram[:, wide : 2 * wide] = words[...]
    trigram[:, 2 * wide :] = before.astype(BF)
    spot = lax.broadcasted_iota(jnp.int32, (ATT, 1), 0)
    gain, bias = norms[0:1], norms[1:2]
    loads[0].wait()
    for start in range(0, tokens, ATT):
        r = slice(start, start + ATT)
        second = spot + start >= start_at
        kind = jnp.where(second, extra[tokens + 1 : tokens + 2], extra[tokens : tokens + 1])
        value = dot(trigram[r], conv[...]) + extra[r] + kind
        inputs_out[r] = value
        hidden = layer_norm(dot(value.astype(BF), entry_v[...]), gain[:, :breadth], bias[:, :breadth])
        hidden_v[r] = hidden
        low_v[r] = hidden.astype(BF)
    heads = half // THD
    pending = []
    for p in range(2):
        if p == 0:
            loads[1].wait()
        else:
            swaps[0].wait()
        first_head = core * heads if p == 0 else (1 - core) * heads
        attend_half(
            length,
            first_head,
            low_v,
            project_v.at[p],
            query_v,
            key_v,
            value_t,
            context_v.at[p],
            logs_out,
            sums_out,
            logs_v,
            scores_v,
            weight_v,
            logs_sem,
            pending,
        )
    loads[2].wait()
    swaps[1].wait()
    for c in loads[3:]:
        c.wait()
    blocks = tokens // ROWS_FF

    def hidden_units(p, low):
        for c in range(0, hidden_half, CUT_FF):
            before = dot(low, expand_v[p, :, c : c + CUT_FF])
            inner = 0.5 * before * (1.0 + lax.erf(before * math.sqrt(0.5)))
            inner_v[:, c : c + CUT_FF] = inner.astype(BF)

    def feed_own(n, carry):
        r = pl.ds(pl.multiple_of(n * ROWS_FF, ROWS_FF), ROWS_FF)
        mixed = dot(context_v[0, r], mixer_v[0]) + dot(context_v[1, r], mixer_v[1])
        first = layer_norm(
            mixed + hidden_v[r], gain[:, breadth : 2 * breadth], bias[:, breadth : 2 * breadth]
        )
        hidden_v[r] = first
        low_v[r] = first.astype(BF)
        hidden_units(0, low_v[r])
        hidden_v[r] += dot(inner_v[...], shrink_v[0])
        return carry

    def feed_mate(n, carry):
        r = pl.ds(pl.multiple_of(n * ROWS_FF, ROWS_FF), ROWS_FF)
        hidden_units(1, low_v[r])
        total = dot(inner_v[...], shrink_v[1]) + hidden_v[r]
        second = layer_norm(
            total, gain[:, 2 * breadth : 3 * breadth], bias[:, 2 * breadth : 3 * breadth]
        )
        raw = dot(second.astype(BF), leave_v[...]) + inputs_out[r]
        feature_out[r] = layer_norm(
            raw, gain[:, 3 * breadth : 3 * breadth + HID], bias[:, 3 * breadth : 3 * breadth + HID]
        )
        return carry

    lax.fori_loop(0, blocks, feed_own, 0)

    def take_tiles(d, carry):
        tile_copy(d).wait()
        return carry

    lax.fori_loop(1, n_rows, take_tiles, 0)
    over = pltpu.make_async_remote_copy(
        src_ref=tiles_own,
        dst_ref=tiles_mate,
        send_sem=pass_send,
        recv_sem=pass_recv,
        device_id=mate,
        device_id_type=MESH,
    )
    over.start()
    for c in swaps[2:]:
        c.wait()
    lax.fori_loop(0, blocks, feed_mate, 0)
    over.wait()
    for c in pending:
        c.wait()


def teacher(n_rows, bounds, micro_batch, words, conv, extra, norms, weight, entry, project, mixer, expand, shrink, leave):
    tokens, wide = words.shape
    breadth = entry.shape[1]
    half = project.shape[2]
    hidden_half = expand.shape[1]
    V, D = pltpu.VMEM, pltpu.SemaphoreType.DMA
    slots, lines, lanes = weight.shape
    sent = (slots * lines // 2 + 16, lanes)
    gathered = jax.ShapeDtypeStruct((n_rows,) + sent, BF)
    return pl.pallas_call(
        teacher_kernel,
        out_shape=(
            jax.ShapeDtypeStruct((tokens, HID), F32),
            jax.ShapeDtypeStruct((tokens, HID), F32),
            jax.ShapeDtypeStruct((2 * half // THD, tokens, tokens), BF),
            jax.ShapeDtypeStruct((2 * half // THD, 1, tokens), F32),
            gathered,
            gathered,
        ),
        in_specs=[SMEM] * 2 + [VMEM] * 5 + [ANY] * 6,
        out_specs=(VMEM, VMEM, ANY, VMEM, ANY, ANY),
        scratch_shapes=[
            V((tokens, 3 * wide), BF),
            V((tokens, breadth), F32),
            V((tokens, breadth), BF),
            V(entry.shape, BF),
            V((2,) + project.shape, BF),
            V((2,) + mixer.shape, BF),
            V((2,) + expand.shape, BF),
            V((2,) + shrink.shape, BF),
            V(leave.shape, BF),
            V((tokens, half), BF),
            V((tokens, half), BF),
            V((half, tokens), BF),
            V((2, tokens, half), BF),
            V((LOG_SLOTS, tokens, ATT), BF),
            V((2, tokens, ATT), F32),
            V((2, tokens, ATT), BF),
            V((ROWS_FF, hidden_half), BF),
            V(sent, BF),
            D((7,)),
            D((LOG_SLOTS,)),
            D((4,)),
            D((4,)),
            D((n_rows - 1,)),
            D((n_rows - 1,)),
            D,
            D,
        ],
        compiler_params=pltpu.CompilerParams(
            collective_id=1, has_side_effects=True, vmem_limit_bytes=62 << 20
        ),
        cost_estimate=pl.CostEstimate(
            flops=33_000_000_000, bytes_accessed=40 << 20, transcendentals=0
        ),
    )(bounds, micro_batch, words, conv, extra, norms, weight, entry, project, mixer, expand, shrink, leave)


def three_parts(value):
    high = value.astype(BF).astype(F32)
    middle = (value - high).astype(BF).astype(F32)
    return high, middle, value - high - middle


def student_kernel(
    owners,
    bounds,
    micro_batch,
    inputs,
    feature,
    logs,
    sums,
    tiles_own,
    tiles_mate,
    small,
    grads_out,
    lines_out,
    logs_v,
    wide_w,
    pair_w,
    mixer_w,
    expand_w,
    shrink_w,
    leave_w,
    low_v,
    narrow_v,
    first_v,
    query_v,
    query_m,
    key_m,
    value_m,
    key_t,
    value_t,
    context_t,
    contextlow_t,
    blocklow_v,
    hidden_v,
    sum_v,
    dsum_v,
    dcontext_v,
    dcontext_t,
    dcontext_m,
    dvalue_v,
    dkey_v,
    dpair_v,
    scores_v,
    dweight_v,
    weight_v,
    dscores_v,
    g_leave,
    g_mixer,
    g_expand,
    g_shrink,
    small_v,
    slot,
    held,
    sem,
):
    tokens = inputs.shape[0]
    breadth = tiles_own.shape[2]
    core = lax.axis_index("heads")
    copies = [pltpu.make_async_copy(logs.at[h], logs_v.at[h], sem.at[h]) for h in range(SHEADS)]
    for c in copies:
        c.start()
    length, batch = bounds[core, 1], micro_batch[core]
    n_owners = tiles_own.shape[0]
    slots = grads_out.shape[0] // n_owners
    lines = breadth // 2

    def clear(i, carry):
        held[i] = 0
        return carry

    lax.fori_loop(0, n_owners, clear, 0)

    def assign(i, carry):
        owner = owners[i]
        slot[i] = owner * slots + held[owner]
        held[owner] = held[owner] + 1
        return carry

    lax.fori_loop(0, owners.shape[0], assign, 0)
    digits = tiles_own[0, slots * lines :].astype(F32)
    for i in range(1, n_owners):
        digits = digits + tiles_own[i, slots * lines :].astype(F32)
    digits = digits[0:1]
    at_lane = lax.broadcasted_iota(jnp.int32, digits.shape, 1)
    digits = jnp.where(
        at_lane == 2 * batch,
        digits * COUNT_BASE,
        jnp.where(at_lane == 2 * batch + 1, digits, 0.0),
    )
    inverse = 1.0 / jnp.sum(digits, 1, keepdims=True)
    for ref in (grads_out, g_leave, g_mixer, g_expand, g_shrink, dvalue_v, dkey_v, small_v):
        ref[...] = jnp.zeros_like(ref)

    nin = HID // breadth
    nff = SFF // breadth

    def at(j):
        return slice(j * breadth, (j + 1) * breadth)

    def load(i, ref, row, col):
        owner, rank = slot[i] // slots, slot[i] % slots
        there = pl.ds(pl.multiple_of(rank * lines, lines), lines)
        own_line = pl.multiple_of(core * lines, lines)
        mate_line = pl.multiple_of((1 - core) * lines, lines)
        ref[pl.ds(row * breadth + own_line, lines), at(col)] = tiles_own[owner, there]
        ref[pl.ds(row * breadth + mate_line, lines), at(col)] = tiles_mate[owner, there]

    at_pair, at_mixer, at_ff = 2 * nin, 2 * nin + 2, 2 * nin + 3
    at_shrink = at_ff + NFFN * nff
    at_leave = at_shrink + NFFN * nff
    for j in range(nin):
        load(j, wide_w, j, 0)
        load(nin + j, wide_w, j, 1)
        load(at_leave + j, leave_w, 0, j)
    load(at_pair, pair_w, 0, 0)
    load(at_pair + 1, pair_w, 0, 1)
    load(at_mixer, mixer_w, 0, 0)
    for b in range(NFFN):
        for j in range(nff):
            load(at_ff + b * nff + j, expand_w.at[b], 0, j)
            load(at_shrink + b * nff + j, shrink_w.at[b], j, 0)

    def gain(n):
        return small[0:1, at(n)]

    def bias(n):
        return small[1:2, at(n)]

    tail = (2 + NFFN) * breadth
    gain_out, bias_out = small[0:1, tail:], small[1:2, tail:]
    lane = lax.broadcasted_iota(jnp.int32, (1, breadth), 1)
    of_head = [(lane // SHD) == h for h in range(SHEADS)]
    for start in range(0, tokens, ROWS_FF):
        r = slice(start, start + ROWS_FF)
        low = inputs[r].astype(BF)
        low_v[r] = low
        both = dot(low, wide_w[...])
        narrow, value = both[:, :breadth], both[:, breadth:]
        narrow_v[r] = narrow
        first = narrow * gain(0) + bias(0)
        first_v[r] = first
        pair = dot(first.astype(BF), pair_w[...])
        query, key = pair[:, :breadth], pair[:, breadth:]
        query_v[r, :breadth] = query.astype(BF)
        place = lax.broadcasted_iota(jnp.int32, (ROWS_FF, 1), 0) + start
        mask = jnp.where(place < length, 0.0, MASKED_SCORE)
        for h in range(SHEADS):
            query_m[h, r] = jnp.where(of_head[h], query, 0.0).astype(BF)
            key_m[h, r, :breadth] = jnp.where(of_head[h], key, 0.0).astype(BF)
            value_m[h, r, :breadth] = jnp.where(of_head[h], value, 0.0).astype(BF)
            of_part = (lane >= 1 + 3 * h) & (lane < 4 + 3 * h)
            less = jnp.where(of_part, -1.0, 0.0)
            key_m[h, r, breadth:] = jnp.where(lane == 0, mask, less).astype(BF)
            value_m[h, r, breadth:] = jnp.broadcast_to(less, (ROWS_FF, breadth)).astype(BF)
        query_v[r, breadth:] = jnp.broadcast_to(jnp.where(lane == 0, 1.0, 0.0), (ROWS_FF, breadth)).astype(BF)
        key_t[:, r] = key.T.astype(BF)
        value_t[:, r] = value.T.astype(BF)
    scale = SHD**-0.5
    scale2 = scale * LOG2E

    def extra_columns(mark, values):
        rows = [jnp.full((1, ATT), mark, F32)]
        for v in values:
            rows.extend(three_parts(v))
        rows.append(jnp.zeros((breadth - len(rows), ATT), F32))
        return jnp.concatenate(rows, 0).T.astype(BF)

    def forward(n, carry):
        r = pl.ds(pl.multiple_of(n * ATT, ATT), ATT)
        query = query_v[r]
        shifts, parts = [], []
        scores_v[0] = dot_nt(key_m[0], query)
        for h in range(SHEADS):
            if h + 1 < SHEADS:
                scores_v[(h + 1) % 2] = dot_nt(key_m[h + 1], query)
            scores, weight = scores_v.at[h % 2], weight_v.at[h % 2]
            top = column_max(scores)
            part = 0.0
            for c in split_rows(scores):
                piece = jnp.exp2((scores[c] - top) * scale2)
                weight[c] = piece.astype(BF)
                part = part + piece
            total = jnp.sum(part, 0, keepdims=True)
            shifts.append(top + jnp.log2(total) * (1.0 / scale2))
            parts.append(dot(value_t[h * SHD : (h + 1) * SHD], weight[...]) * (1.0 / total))
        mixed = jnp.concatenate(parts, 0)
        context_t[:, r] = mixed
        contextlow_t[:, r] = mixed.astype(BF)
        query_v[r, breadth:] = extra_columns(1.0, shifts)
        return carry

    lax.fori_loop(0, tokens // ATT, forward, 0)

    def row_sums(n, d, value):
        small_v[0:1, at(n)] += jnp.sum(d * value, 0, keepdims=True)
        small_v[1:2, at(n)] += jnp.sum(d, 0, keepdims=True)

    def feed(n, loss):
        r = pl.ds(pl.multiple_of(n * ROWS_FF, ROWS_FF), ROWS_FF)
        place = lax.broadcasted_iota(jnp.int32, (ROWS_FF, 1), 0) + n * ROWS_FF
        weight = jnp.where(place < length, inverse, 0.0)
        context = context_t[:, r].T.astype(BF)
        mixed_sum = dot(context, mixer_w[...]) + first_v[r]
        current = mixed_sum * gain(1) + bias(1)
        for b in range(NFFN):
            low = current.astype(BF)
            blocklow_v[b] = low
            hidden = jnp.maximum(dot(low, expand_w[b]), 0.0).astype(BF)
            hidden_v[b] = hidden
            total = dot(hidden, shrink_w[b]) + current
            sum_v[b] = total
            current = total * gain(2 + b) + bias(2 + b)
        joined = dot(current.astype(BF), leave_w[...]) + inputs[r]
        differ = joined * gain_out + bias_out - feature[r]
        loss = loss + jnp.sum(weight * jnp.mean(differ * differ, -1, keepdims=True), 0, keepdims=True)
        outer = differ * (weight * (2.0 / HID))
        small_v[0:1, tail:] += jnp.sum(outer * joined, 0, keepdims=True)
        small_v[1:2, tail:] += jnp.sum(outer, 0, keepdims=True)
        back = (outer * gain_out).astype(BF)
        g_leave[...] += dot(current.T.astype(BF), back)
        d = dot_nt(back, leave_w[...])
        for b in reversed(range(NFFN)):
            row_sums(2 + b, d, sum_v[b])
            d_sum = d * gain(2 + b)
            hidden = hidden_v[b]
            g_shrink[b] += dot(d_sum.T.astype(BF), hidden)
            d_hidden = dot_nt(d_sum.astype(BF), shrink_w[b])
            d_before = jnp.where(hidden > 0, d_hidden, 0.0).astype(BF)
            g_expand[b] += dot(blocklow_v[b].T, d_before)
            d = d_sum + dot_nt(d_before, expand_w[b])
        row_sums(1, d, mixed_sum)
        d_sum = d * gain(1)
        dsum_v[r] = d_sum
        d_mixed = d_sum.astype(BF)
        g_mixer[...] += dot(contextlow_t[:, r], d_mixed)
        d_context = dot_nt(d_mixed, mixer_w[...])
        dcontext_v[r, :breadth] = d_context.astype(BF)
        dcontext_t[:, r] = d_context.astype(BF).astype(F32).T
        for h in range(SHEADS):
            dcontext_m[h, r] = jnp.where(of_head[h], d_context, 0.0).astype(BF)
        return loss

    loss = lax.fori_loop(0, tokens // ROWS_FF, feed, jnp.zeros((1, 1), F32))
    for c in copies:
        c.wait()

    log_share = jnp.log2(inverse * (1.0 / SHEADS))

    def backward(n, loss):
        r = pl.ds(pl.multiple_of(n * ATT, ATT), ATT)
        place = lax.broadcasted_iota(jnp.int32, (1, ATT), 1) + n * ATT
        inside = place < length
        share = jnp.where(inside, inverse * (1.0 / SHEADS), 0.0)
        share2 = jnp.where(inside, log_share, MASKED_SCORE)
        less = []
        for h in range(SHEADS):
            heads = slice(h * SHD, (h + 1) * SHD)
            along = jnp.sum(context_t[heads, r] * dcontext_t[heads, r], 0, keepdims=True)
            less.append(along - share * sums[h, :, r])
        dcontext_v[r, breadth:] = extra_columns(0.0, less)
        query, d_context = query_v[r], dcontext_v[r]

        def products(h):
            scores_v[h % 2] = dot_nt(key_m[h], query)
            dweight_v[h % 2] = dot_nt(value_m[h], d_context)

        products(0)
        parts = []
        gap = 0.0
        for h in range(SHEADS):
            if h + 1 < SHEADS:
                products(h + 1)
            scores, dweight = scores_v.at[h % 2], dweight_v.at[h % 2]
            weight, dscores = weight_v.at[h % 2], dscores_v.at[h % 2]
            for c in split_rows(scores):
                score = scores[c]
                piece = jnp.exp2(score * scale2)
                weight[c] = piece.astype(BF)
                target_log = logs_v[h, c, r].astype(F32)
                target = jnp.exp2(target_log * LOG2E + share2)
                gap = gap + target * (target_log - score * scale)
                dscores[c] = (piece * dweight[c] - target).astype(BF)
            dvalue_v[...] += dot(weight[...], dcontext_m[h, r])
            dkey_v[...] += dot(dscores[...], query_m[h, r])
            parts.append(dot(key_t[h * SHD : (h + 1) * SHD], dscores[...]))
        dpair_v[r, at(0)] = (jnp.concatenate(parts, 0) * scale).T.astype(BF)
        return loss + jnp.sum(jnp.sum(gap, 0, keepdims=True), 1, keepdims=True)

    loss = lax.fori_loop(0, tokens // ATT, backward, loss)
    dpair_v[:, at(1)] = (dkey_v[...] * scale).astype(BF)
    d_pair = dpair_v[...]
    d_first = dsum_v[...] + dot_nt(d_pair, pair_w[...])
    row_sums(0, d_first, narrow_v[...])
    g_pair = dot(first_v[...].T.astype(BF), d_pair)
    wide_t = jnp.concatenate([(d_first * gain(0)).T.astype(BF), dvalue_v[...].T.astype(BF)], 0)
    g_wide = dot(wide_t, low_v[...])
    for j in range(nin):
        grads_out[slot[j]] = g_wide[:breadth, at(j)].T.astype(BF)
        grads_out[slot[nin + j]] = g_wide[breadth:, at(j)].T.astype(BF)
        grads_out[slot[at_leave + j]] = g_leave[:, at(j)].astype(BF)
    grads_out[slot[at_pair]] = g_pair[:, at(0)].astype(BF)
    grads_out[slot[at_pair + 1]] = g_pair[:, at(1)].astype(BF)
    grads_out[slot[at_mixer]] = g_mixer[...].astype(BF)
    for b in range(NFFN):
        for j in range(nff):
            grads_out[slot[at_ff + b * nff + j]] = g_expand[b, :, at(j)].astype(BF)
            grads_out[slot[at_shrink + b * nff + j]] = g_shrink[b, :, at(j)].T.astype(BF)
    lines_out[...] = jnp.zeros_like(lines_out)
    n_lines = small.shape[1] // breadth
    for j in range(n_lines):
        lines_out[j : j + 1] = small_v[0:1, at(j)]
        lines_out[n_lines + j : n_lines + j + 1] = small_v[1:2, at(j)]
    lines_out[2 * n_lines : 2 * n_lines + 1, 0:1] = loss


def student(owners, bounds, micro_batch, inputs, feature, logs, sums, tiles_own, tiles_mate, small, slots):
    tokens = inputs.shape[0]
    n_owners, _, w = tiles_own.shape
    n_lines = 8 * -(-(2 * small.shape[1] // w + 1) // 8)
    D = pltpu.SemaphoreType.DMA

    def low(*shape):
        return pltpu.VMEM(shape, BF)

    def full(*shape):
        return pltpu.VMEM(shape, F32)

    return pl.pallas_call(
        student_kernel,
        out_shape=(
            jax.ShapeDtypeStruct((n_owners * slots, w, w), BF),
            jax.ShapeDtypeStruct((n_lines, w), F32),
        ),
        in_specs=[SMEM, SMEM, SMEM, VMEM, VMEM, ANY, VMEM, VMEM, VMEM, VMEM],
        out_specs=(VMEM, VMEM),
        scratch_shapes=[
            low(*logs.shape),
            low(HID, 2 * w),
            low(w, 2 * w),
            low(w, w),
            low(NFFN, w, SFF),
            low(NFFN, SFF, w),
            low(w, HID),
            low(tokens, HID),
            full(tokens, w),
            full(tokens, w),
            low(tokens, 2 * w),
            low(SHEADS, tokens, w),
            low(SHEADS, tokens, 2 * w),
            low(SHEADS, tokens, 2 * w),
            low(w, tokens),
            low(w, tokens),
            full(w, tokens),
            low(w, tokens),
            low(NFFN, ROWS_FF, w),
            low(NFFN, ROWS_FF, SFF),
            full(NFFN, ROWS_FF, w),
            full(tokens, w),
            low(tokens, 2 * w),
            full(w, tokens),
            low(SHEADS, tokens, w),
            full(tokens, w),
            full(tokens, w),
            low(tokens, 2 * w),
            full(2, tokens, ATT),
            full(2, tokens, ATT),
            low(2, tokens, ATT),
            low(2, tokens, ATT),
            full(w, HID),
            full(w, w),
            full(NFFN, w, SFF),
            full(NFFN, w, SFF),
            full(8, small.shape[1]),
            pltpu.SMEM(owners.shape, jnp.int32),
            pltpu.SMEM((n_owners,), jnp.int32),
            D((SHEADS,)),
        ],
        compiler_params=pltpu.CompilerParams(vmem_limit_bytes=60 << 20),
        cost_estimate=pl.CostEstimate(
            flops=15_000_000_000, bytes_accessed=16 << 20, transcendentals=0
        ),
    )(owners, bounds, micro_batch, inputs, feature, logs, sums, tiles_own, tiles_mate, small)


def reduce_kernel(side, deep, slots, grads, small, tiles_out, stats_out,
                  pair_in, first, first_in, second, second_in, third, third_in, half_own, half_in,
                  small_pair, small_a, small_b, small_z, norm_all, norm_own,
                  pair_send, pair_recv, first_send, first_recv, second_send, second_recv, third_send, third_recv,
                  half_send, half_recv, sp_send, sp_recv, sa_send, sa_recv, sb_send, sb_recv, sz_send, sz_recv, n_send, n_recv):
    bf, f32 = jnp.bfloat16, jnp.float32
    row, core = lax.axis_index("rows"), lax.axis_index("heads")
    plane = side*side
    z = row // plane
    y = (row // side) % side
    x = row % side
    total = plane*deep
    lines = grads.shape[-2]//2
    mate = (row, 1-core)
    mine = core*lines
    theirs = (1-core)*lines
    straight = core == 0
    a = jnp.where(straight, x, y)
    b = jnp.where(straight, y, x)
    pa = jnp.where(straight, y, x)
    def row_at(xx, yy, zz):
        return zz*plane + yy*side + xx
    def along_a(aa):
        return (jnp.where(straight, row_at(aa, y, z), row_at(x, aa, z)), core)
    def along_b(bb):
        return (jnp.where(straight, row_at(x, bb, z), row_at(bb, y, z)), core)
    def along_z(zz):
        return (row_at(x, y, zz), core)
    barrier = pltpu.get_barrier_semaphore()
    n_devices = 2*total
    me = row*2 + core
    def greet(i, carry):
        peer = lax.rem(me + i, n_devices)
        pl.semaphore_signal(barrier, inc=1, device_id=(peer // 2, peer % 2), device_id_type=MESH)
        return carry
    lax.fori_loop(1, n_devices, greet, 0)
    pl.semaphore_wait(barrier, n_devices-1)

    def remote(src, dst, send, recv, peer):
        return pltpu.make_async_remote_copy(src_ref=src, dst_ref=dst, send_sem=send, recv_sem=recv, device_id=peer, device_id_type=MESH)

    small_pair_copy = remote(small, small_pair, sp_send, sp_recv, mate)
    small_pair_copy.start()
    order = list(range(1, side)) + [0]
    for d in order:
        piece = lax.rem(pa + d, side)
        by_y = remote(grads.at[:, piece, :, :, pl.ds(theirs, lines), :], pair_in.at[d], pair_send.at[d], pair_recv.at[d], mate)
        by_x = remote(grads.at[:, :, piece, :, pl.ds(theirs, lines), :], pair_in.at[d], pair_send.at[d], pair_recv.at[d], mate)
        @pl.when(straight)
        def _(): by_y.start()
        @pl.when(jnp.logical_not(straight))
        def _(): by_x.start()
    def pair_wait(d):
        return remote(first.at[d], pair_in.at[d], pair_send.at[d], pair_recv.at[d], mate)
    first_copies = []
    for d in order:
        pair_wait(d).wait_recv()
        aa = lax.rem(a + d, side)
        def add(i, carry):
            zz, bb = i // side, i % side
            xx, yy = jnp.where(straight, aa, bb), jnp.where(straight, bb, aa)
            own = grads[zz, yy, xx, :, pl.ds(mine, lines), :].astype(f32)
            first[d, zz, bb] = (own + pair_in[d, zz, bb].astype(f32)).astype(bf)
            return carry
        lax.fori_loop(0, deep*side, add, 0)
        if d:
            c = remote(first.at[d], first_in.at[d-1], first_send.at[d-1], first_recv.at[d-1], along_a(aa))
            c.start(); first_copies.append(c)
    small_pair_copy.wait()
    small_a[x] = small[...] + small_pair[...]
    sa = []
    for d in range(1, side):
        c = remote(small_a.at[x], small_a.at[x], sa_send.at[d-1], sa_recv.at[d-1], (row_at(lax.rem(x+d, side), y, z), core))
        c.start(); sa.append(c)
    for c in first_copies: c.wait_recv()
    second_copies = []
    for d in order:
        bb = lax.rem(b + d, side)
        def add(zz, carry):
            s = first[0, zz, bb].astype(f32)
            for j in range(side-1): s = s + first_in[j, zz, bb].astype(f32)
            second[d, zz] = s.astype(bf)
            return carry
        lax.fori_loop(0, deep, add, 0)
        if d:
            c = remote(second.at[d], second_in.at[d-1], second_send.at[d-1], second_recv.at[d-1], along_b(bb))
            c.start(); second_copies.append(c)
    for c in sa: c.wait()
    small_b[y] = sum_over(small_a, side)
    sb = []
    for d in range(1, side):
        c = remote(small_b.at[y], small_b.at[y], sb_send.at[d-1], sb_recv.at[d-1], (row_at(x, lax.rem(y+d, side), z), core))
        c.start(); sb.append(c)
    for c in second_copies: c.wait_recv()
    third_copies = []
    own = None
    for d in list(range(1, deep)) + [0]:
        zz = lax.rem(z + d, deep)
        s = second[0, zz].astype(f32)
        for j in range(side-1): s = s + second_in[j, zz].astype(f32)
        if d:
            third[d-1] = s.astype(bf)
            c = remote(third.at[d-1], third_in.at[d-1], third_send.at[d-1], third_recv.at[d-1], along_z(zz))
            c.start(); third_copies.append(c)
        else:
            own = s
    for c in sb: c.wait()
    small_z[z] = sum_over(small_b, side)
    sz = []
    for d in range(1, deep):
        c = remote(small_z.at[z], small_z.at[z], sz_send.at[d-1], sz_recv.at[d-1], along_z(lax.rem(z+d, deep)))
        c.start(); sz.append(c)
    for c in third_copies: c.wait_recv()
    for j in range(deep-1): own = own + third_in[j].astype(f32)
    half_own[...] = own
    half_copy = remote(half_own, half_in, half_send, half_recv, mate)
    half_copy.start()
    part = jnp.sum(jnp.sum(own*own, 0), 0, keepdims=True)
    norm_own[...] = jnp.broadcast_to(part, norm_own.shape)
    norm_all[me] = norm_own[...]
    def tell(i, carry):
        peer = lax.rem(me + i, n_devices)
        remote(norm_own, norm_all.at[me], n_send.at[i-1], n_recv.at[i-1], (peer // 2, peer % 2)).start()
        return carry
    lax.fori_loop(1, n_devices, tell, 0)
    tiles_out[:, pl.ds(mine, lines), :] = own
    half_copy.wait()
    tiles_out[:, pl.ds(theirs, lines), :] = half_in[...]
    for c in sz: c.wait()
    small_total = sum_over(small_z, deep)
    def hear(i, carry):
        remote(norm_own, norm_all.at[me], n_send.at[i-1], n_recv.at[i-1], mate).wait()
        return carry
    lax.fori_loop(1, n_devices, hear, 0)
    def gather(i, s):
        return s + norm_all[i]
    squares = lax.fori_loop(0, n_devices, gather, jnp.zeros(norm_own.shape, f32))
    stats_out[0] = small_total[0:8]
    stats_out[1] = small_total[8:16]
    stats_out[2] = small_total[16:24]
    stats_out[3] = squares
    for d in order: pair_wait(d).wait_send()
    for c in first_copies + second_copies + third_copies: c.wait_send()

def reduce_call(n_rows, grads, small):
    deep = 4
    side = math.isqrt(n_rows // deep)
    assert side*side*deep == n_rows
    slots = grads.shape[0] // n_rows
    wide, lanes = grads.shape[1:]
    lines = wide//2
    bf, f32 = jnp.bfloat16, jnp.float32
    grads = grads.reshape(deep, side, side, slots, wide, lanes)
    V, D = pltpu.VMEM, pltpu.SemaphoreType.DMA
    s1, d1, n = side-1, deep-1, 2*n_rows
    return pl.pallas_call(functools.partial(reduce_kernel, side, deep, slots),
        out_shape=(jax.ShapeDtypeStruct((slots, wide, lanes), f32), jax.ShapeDtypeStruct((4, 8, lanes), f32)),
        in_specs=[VMEM, VMEM], out_specs=(VMEM, VMEM),
        scratch_shapes=[V((side, deep, side, slots, lines, lanes), bf), V((side, deep, side, slots, lines, lanes), bf), V((s1, deep, side, slots, lines, lanes), bf),
            V((side, deep, slots, lines, lanes), bf), V((s1, deep, slots, lines, lanes), bf), V((d1, slots, lines, lanes), bf), V((d1, slots, lines, lanes), bf),
            V((slots, lines, lanes), f32), V((slots, lines, lanes), f32),
            V(small.shape, f32), V((side,)+small.shape, f32), V((side,)+small.shape, f32), V((deep,)+small.shape, f32),
            V((n, 8, lanes), f32), V((8, lanes), f32),
            D((side,)), D((side,)), D((s1,)), D((s1,)), D((s1,)), D((s1,)), D((d1,)), D((d1,)), D, D, D, D, D((s1,)), D((s1,)), D((s1,)), D((s1,)), D((d1,)), D((d1,)), D((n-1,)), D((n-1,))],
        compiler_params=pltpu.CompilerParams(collective_id=0, has_side_effects=True, vmem_limit_bytes=48<<20),
        cost_estimate=pl.CostEstimate(flops=10_000_000, bytes_accessed=8<<20, transcendentals=0),
    )(grads, small)


def update_kernel(
    owners, step, own, summed, stats, weight, first, second, small, small_first, small_second,
    loss_out, norm_out, tiles_out, first_out, second_out, small_out, small_first_out, small_second_out, small_grad_out,
    small_v,
):
    breadth = summed.shape[2]
    n_lines = small.shape[1] // breadth
    steps = step[0]
    first_fix = 1.0 - lax.fori_loop(0, steps, lambda i, p: p * BETA_FIRST, jnp.float32(1.0))
    second_fix = 1.0 - lax.fori_loop(0, steps, lambda i, p: p * BETA_SECOND, jnp.float32(1.0))

    def adam(w, m, v, g, decay):
        m = BETA_FIRST * m + (1.0 - BETA_FIRST) * g
        v = BETA_SECOND * v + (1.0 - BETA_SECOND) * g * g
        change = m / first_fix / (jnp.sqrt(v / second_fix) + ADAM_EPSILON) + decay * w
        return w - LEARN_RATE * change, m, v

    line = lambda n: stats[n // 8, n % 8 : n % 8 + 1]
    squares = stats[3, 0:1]
    for n in range(2 * n_lines):
        squares = squares + line(n) * line(n)
    norm = jnp.sqrt(jnp.sum(squares, 1, keepdims=True))
    norm_out[...] = norm
    loss_out[...] = line(2 * n_lines)[:, 0:1]
    factor = CLIP_NORM / jnp.maximum(norm, CLIP_NORM)
    for n in range(n_lines):
        cols = slice(n * breadth, (n + 1) * breadth)
        small_v[0:1, cols] = line(n)
        small_v[1:2, cols] = line(n_lines + n)
    small_grad = small_v[0:2] * factor
    small_grad_out[...] = small_grad
    w, m, v = adam(small[...], small_first[...], small_second[...], small_grad, 0.0)
    small_out[...] = w
    small_first_out[...] = m
    small_second_out[...] = v

    def count(i, n):
        return n + (owners[i] == own[0]).astype(jnp.int32)

    held = lax.fori_loop(0, owners.shape[0], count, 0)
    for s in range(summed.shape[0]):
        keep = held > s
        w, m, v = adam(weight[s], first[s], second[s], summed[s] * factor, WEIGHT_DECAY)
        tiles_out[s] = jnp.where(keep, w, 0.0)
        first_out[s] = jnp.where(keep, m, 0.0)
        second_out[s] = jnp.where(keep, v, 0.0)


def update(owners, step, own, summed, stats, weight, first, second, small, small_first, small_second):
    one = jax.ShapeDtypeStruct((1, 1), F32)
    tile = jax.ShapeDtypeStruct(weight.shape, F32)
    row = jax.ShapeDtypeStruct(small.shape, F32)
    return pl.pallas_call(
        update_kernel,
        out_shape=(one, one, tile, tile, tile, row, row, row, row),
        in_specs=[SMEM] * 3 + [VMEM] * 8,
        out_specs=(VMEM,) * 9,
        scratch_shapes=[pltpu.VMEM((8, small.shape[1]), F32)],
        compiler_params=pltpu.CompilerParams(vmem_limit_bytes=24 << 20),
        cost_estimate=pl.CostEstimate(flops=2_000_000, bytes_accessed=2 << 20, transcendentals=0),
    )(owners, step, own, summed, stats, weight, first, second, small, small_first, small_second)


def on_device(
    token_ids,
    bounds,
    micro_batch,
    owners,
    step_count,
    word_table,
    conv_weight,
    embed_extra,
    teacher_entry,
    teacher_project,
    teacher_mixer,
    teacher_expand,
    teacher_shrink,
    teacher_leave,
    teacher_norms,
    tile_weight,
    tile_first,
    tile_second,
    small_weight,
    small_first,
    small_second,
):
    core = lax.axis_index("heads")
    n_rows = lax.axis_size("rows")
    assert token_ids.shape[0] == lax.axis_size("heads")
    row_ids = lax.dynamic_index_in_dim(token_ids, core, 0, keepdims=False)
    words = word_table.at[row_ids].get(mode="promise_in_bounds")
    inputs, feature, logs, sums, tiles_own, tiles_mate = teacher(
        n_rows,
        bounds,
        micro_batch,
        words,
        conv_weight,
        embed_extra,
        teacher_norms,
        tile_weight,
        teacher_entry,
        teacher_project.transpose(1, 0, 2),
        teacher_mixer,
        teacher_expand,
        teacher_shrink,
        teacher_leave,
    )
    grads, small_lines = student(
        owners,
        bounds,
        micro_batch,
        inputs,
        feature,
        logs,
        sums,
        tiles_own,
        tiles_mate,
        small_weight,
        tile_weight.shape[0],
    )
    summed, stats = reduce_call(n_rows, grads, small_lines)
    own = lax.axis_index("rows")[None]
    loss, norm, *rest = update(
        owners,
        step_count,
        own,
        summed,
        stats,
        tile_weight,
        tile_first,
        tile_second,
        small_weight,
        small_first,
        small_second,
    )
    return (loss[0, 0], norm[0, 0], *rest)


def solution(mesh):
    placed = (
        P("rows", None),
        P("rows", None),
        P("rows"),
        P(),
        P(),
        P(),
        P(),
        P(),
        P(),
        P(None, None, "heads"),
        P("heads", None),
        P(None, "heads"),
        P("heads", None),
        P(),
        P(),
        P("rows", None, None),
        P("rows", None, None),
        P("rows", None, None),
        P(),
        P(),
        P(),
    )
    tiles = P("rows", None, None)
    return jax.shard_map(
        on_device,
        mesh=mesh,
        in_specs=placed,
        out_specs=(P(), P(), tiles, tiles, tiles, P(), P(), P(), P()),
        check_vma=False,
    )
```

```python
import functools
import math

import jax
import jax.numpy as jnp
from jax import lax
from jax.experimental import pallas as pl
from jax.experimental.pallas import tpu as pltpu
from jax.sharding import PartitionSpec as P

HID = 512
THD = 256
SHEADS = 4
SHD = 32
SFF = 512
NFFN = 4
NMB = 2
NORM_EPSILON = 1e-05
CLIP_NORM = 0.05
LEARN_RATE = 0.1
BETA_FIRST = 0.9
BETA_SECOND = 0.999
ADAM_EPSILON = 1e-08
WEIGHT_DECAY = 0.01
MASKED_SCORE = -1e30
LOG2E = math.log2(math.e)
COUNT_BASE = 64

ATT = 256
ROWS_FF = 512
CUT_FF = 512
LOG_SLOTS = 4

MESH = pl.DeviceIdType.MESH
BF, F32 = jnp.bfloat16, jnp.float32
VMEM = pl.BlockSpec(memory_space=pltpu.VMEM)
SMEM = pl.BlockSpec(memory_space=pltpu.SMEM)
ANY = pl.BlockSpec(memory_space=pl.ANY)


def dot(left, right):
    return jnp.dot(left, right, preferred_element_type=F32)


def dot_nt(left, right):
    return lax.dot_general(left, right, (((1,), (1,)), ((), ())), preferred_element_type=F32)


def layer_norm(values, gain_row, bias_row):
    center = values - jnp.mean(values, -1, keepdims=True)
    spread = jnp.mean(center * center, -1, keepdims=True)
    return center * lax.rsqrt(spread + NORM_EPSILON) * gain_row + bias_row


def sum_over(ref, n):
    s = ref[0]
    for i in range(1, n):
        s = s + ref[i]
    return s


def split_rows(refs, rows=64):
    for start in range(0, refs.shape[-2], rows):
        yield slice(start, start + rows)


def column_max(ref):
    best = None
    for c in split_rows(ref):
        best = ref[c] if best is None else jnp.maximum(best, ref[c])
    return jnp.max(best, 0, keepdims=True)


def attend_half(
    length,
    first_head,
    low_v,
    project_v,
    query_v,
    key_v,
    value_t,
    context_v,
    logs_out,
    sums_out,
    logs_v,
    scores_v,
    weight_v,
    sem,
    pending,
):
    tokens = low_v.shape[0]
    width = project_v.shape[2]
    for start in range(0, tokens, ROWS_FF):
        rows = slice(start, start + ROWS_FF)
        low = low_v[rows]
        query_v[rows] = (dot(low, project_v[0]) * THD**-0.5).astype(BF)
        key_v[rows] = dot(low, project_v[1]).astype(BF)
        value_t[:, rows] = dot(low, project_v[2]).T.astype(BF)
    steps = [(h, q) for h in range(width // THD) for q in range(tokens // ATT)]
    least = tokens // 2

    def scores_of(i):
        h, q = steps[i]
        cols = slice(h * THD, (h + 1) * THD)
        query = query_v[q * ATT : (q + 1) * ATT, cols]
        scores_v[i % 2, :least] = dot_nt(key_v[:least, cols], query)
        valid = lax.broadcasted_iota(jnp.int32, (tokens - least, ATT), 0) + least < length
        scores_v[i % 2, least:] = jnp.where(valid, dot_nt(key_v[least:, cols], query), MASKED_SCORE)

    scores_of(0)
    for i, (h, q) in enumerate(steps):
        if len(pending) == LOG_SLOTS:
            pending.pop(0).wait()
        if i + 1 < len(steps):
            scores_of(i + 1)
        at = i % LOG_SLOTS
        scores, weight, logs = scores_v.at[i % 2], weight_v.at[i % 2], logs_v.at[at]
        top = column_max(scores)
        part = 0.0
        for c in split_rows(scores):
            piece = jnp.exp(scores[c] - top)
            weight[c] = piece.astype(BF)
            part = part + piece
        total = jnp.sum(part, 0, keepdims=True)
        shift = top + jnp.log(total)
        part = 0.0
        for c in split_rows(scores):
            piece = (scores[c] - shift).astype(BF)
            logs[c] = piece
            part = part + jnp.exp(piece.astype(F32))
        sums_out[first_head + h, :, q * ATT : (q + 1) * ATT] = jnp.sum(part, 0, keepdims=True)
        mixed = dot(value_t[h * THD : (h + 1) * THD], weight[...]) * (1.0 / total)
        context_v[q * ATT : (q + 1) * ATT, h * THD : (h + 1) * THD] = mixed.T.astype(BF)
        there = logs_out.at[first_head + h, :, pl.ds(q * ATT, ATT)]
        pending.append(pltpu.make_async_copy(logs, there, sem.at[at]))
        pending[-1].start()
    assert len(steps) % LOG_SLOTS == 0


def teacher_kernel(
    bounds,
    micro_batch,
    words,
    conv,
    extra,
    norms,
    weight,
    entry,
    project,
    mixer,
    expand,
    shrink,
    leave,
    inputs_out,
    feature_out,
    logs_out,
    sums_out,
    tiles_own,
    tiles_mate,
    trigram,
    hidden_v,
    low_v,
    entry_v,
    project_v,
    mixer_v,
    expand_v,
    shrink_v,
    leave_v,
    query_v,
    key_v,
    value_t,
    context_v,
    logs_v,
    scores_v,
    weight_v,
    inner_v,
    sent,
    in_sem,
    logs_sem,
    swap_send,
    swap_recv,
    tile_send,
    tile_recv,
    pass_send,
    pass_recv,
):
    tokens, wide = words.shape
    breadth = entry.shape[1]
    half = project.shape[2]
    hidden_half = expand.shape[1]
    n_rows = tiles_own.shape[0]
    row, core = lax.axis_index("rows"), lax.axis_index("heads")
    mate = (row, 1 - core)
    start_at, length = bounds[core, 0], bounds[core, 1]
    slots, _, lanes = weight.shape
    lines = weight.shape[1] // 2
    for n in range(slots):
        sent[n * lines : (n + 1) * lines] = weight[n, pl.ds(core * lines, lines)].astype(BF)
    lane = lax.broadcasted_iota(jnp.int32, (16, lanes), 1)
    digits = jnp.zeros((16, lanes), F32)
    for m in range(NMB):
        held = jnp.int32(0)
        for n in range(micro_batch.shape[0]):
            held = held + jnp.where(micro_batch[n] == m, bounds[n, 1], 0)
        digits = jnp.where(lane == 2 * m, (held // COUNT_BASE).astype(F32), digits)
        digits = jnp.where(lane == 2 * m + 1, (held % COUNT_BASE).astype(F32), digits)
    sent[slots * lines :] = digits.astype(BF)

    def peer(d):
        return (lax.rem(row + d, n_rows), core)

    local = [(entry, entry_v), (project, project_v.at[0]), (mixer, mixer_v.at[0])]
    local += [(expand, expand_v.at[0]), (shrink, shrink_v.at[0]), (leave, leave_v)]
    local += [(sent, tiles_own.at[row])]
    loads = [pltpu.make_async_copy(a, b, in_sem.at[n]) for n, (a, b) in enumerate(local)]
    for c in loads:
        c.start()
    barrier = pltpu.get_barrier_semaphore()
    pl.semaphore_signal(barrier, inc=1, device_id=mate, device_id_type=MESH)

    def greet(d, carry):
        pl.semaphore_signal(barrier, inc=1, device_id=peer(d), device_id_type=MESH)
        return carry

    lax.fori_loop(1, n_rows, greet, 0)
    pl.semaphore_wait(barrier, n_rows)
    swaps = []
    for n, (a, b) in enumerate(((project, project_v), (mixer, mixer_v), (expand, expand_v), (shrink, shrink_v))):
        swaps.append(
            pltpu.make_async_remote_copy(
                src_ref=a,
                dst_ref=b.at[1],
                send_sem=swap_send.at[n],
                recv_sem=swap_recv.at[n],
                device_id=mate,
                device_id_type=MESH,
            )
        )
        swaps[-1].start()

    def tile_copy(d):
        return pltpu.make_async_remote_copy(
            src_ref=sent,
            dst_ref=tiles_own.at[row],
            send_sem=tile_send.at[d - 1],
            recv_sem=tile_recv.at[d - 1],
            device_id=peer(d),
            device_id_type=MESH,
        )

    def send_tiles(d, carry):
        tile_copy(d).start()
        return carry

    lax.fori_loop(1, n_rows, send_tiles, 0)
    rows = words[...].astype(F32)
    place = lax.broadcasted_iota(jnp.int32, (tokens, wide), 0)
    after = jnp.where(place < tokens - 1, pltpu.roll(rows, tokens - 1, 0), 0.0)
    before = jnp.where(place > 0, pltpu.roll(rows, 1, 0), 0.0)
    trigram[:, :wide] = after.astype(BF)
    trigram[:, wide : 2 * wide] = words[...]
    trigram[:, 2 * wide :] = before.astype(BF)
    spot = lax.broadcasted_iota(jnp.int32, (ATT, 1), 0)
    gain, bias = norms[0:1], norms[1:2]
    loads[0].wait()
    for start in range(0, tokens, ATT):
        r = slice(start, start + ATT)
        second = spot + start >= start_at
        kind = jnp.where(second, extra[tokens + 1 : tokens + 2], extra[tokens : tokens + 1])
        value = dot(trigram[r], conv[...]) + extra[r] + kind
        inputs_out[r] = value
        hidden = layer_norm(dot(value.astype(BF), entry_v[...]), gain[:, :breadth], bias[:, :breadth])
        hidden_v[r] = hidden
        low_v[r] = hidden.astype(BF)
    heads = half // THD
    pending = []
    for p in range(2):
        if p == 0:
            loads[1].wait()
        else:
            swaps[0].wait()
        first_head = core * heads if p == 0 else (1 - core) * heads
        attend_half(
            length,
            first_head,
            low_v,
            project_v.at[p],
            query_v,
            key_v,
            value_t,
            context_v.at[p],
            logs_out,
            sums_out,
            logs_v,
            scores_v,
            weight_v,
            logs_sem,
            pending,
        )
    loads[2].wait()
    swaps[1].wait()
    for c in loads[3:]:
        c.wait()
    blocks = tokens // ROWS_FF

    def hidden_units(p, low):
        for c in range(0, hidden_half, CUT_FF):
            before = dot(low, expand_v[p, :, c : c + CUT_FF])
            inner = 0.5 * before * (1.0 + lax.erf(before * math.sqrt(0.5)))
            inner_v[:, c : c + CUT_FF] = inner.astype(BF)

    def feed_own(n, carry):
        r = pl.ds(pl.multiple_of(n * ROWS_FF, ROWS_FF), ROWS_FF)
        mixed = dot(context_v[0, r], mixer_v[0]) + dot(context_v[1, r], mixer_v[1])
        first = layer_norm(
            mixed + hidden_v[r], gain[:, breadth : 2 * breadth], bias[:, breadth : 2 * breadth]
        )
        hidden_v[r] = first
        low_v[r] = first.astype(BF)
        hidden_units(0, low_v[r])
        hidden_v[r] += dot(inner_v[...], shrink_v[0])
        return carry

    def feed_mate(n, carry):
        r = pl.ds(pl.multiple_of(n * ROWS_FF, ROWS_FF), ROWS_FF)
        hidden_units(1, low_v[r])
        total = dot(inner_v[...], shrink_v[1]) + hidden_v[r]
        second = layer_norm(
            total, gain[:, 2 * breadth : 3 * breadth], bias[:, 2 * breadth : 3 * breadth]
        )
        raw = dot(second.astype(BF), leave_v[...]) + inputs_out[r]
        feature_out[r] = layer_norm(
            raw, gain[:, 3 * breadth : 3 * breadth + HID], bias[:, 3 * breadth : 3 * breadth + HID]
        )
        return carry

    lax.fori_loop(0, blocks, feed_own, 0)

    def take_tiles(d, carry):
        tile_copy(d).wait()
        return carry

    lax.fori_loop(1, n_rows, take_tiles, 0)
    over = pltpu.make_async_remote_copy(
        src_ref=tiles_own,
        dst_ref=tiles_mate,
        send_sem=pass_send,
        recv_sem=pass_recv,
        device_id=mate,
        device_id_type=MESH,
    )
    over.start()
    for c in swaps[2:]:
        c.wait()
    lax.fori_loop(0, blocks, feed_mate, 0)
    over.wait()
    for c in pending:
        c.wait()


def teacher(n_rows, bounds, micro_batch, words, conv, extra, norms, weight, entry, project, mixer, expand, shrink, leave):
    tokens, wide = words.shape
    breadth = entry.shape[1]
    half = project.shape[2]
    hidden_half = expand.shape[1]
    V, D = pltpu.VMEM, pltpu.SemaphoreType.DMA
    slots, lines, lanes = weight.shape
    sent = (slots * lines // 2 + 16, lanes)
    gathered = jax.ShapeDtypeStruct((n_rows,) + sent, BF)
    return pl.pallas_call(
        teacher_kernel,
        out_shape=(
            jax.ShapeDtypeStruct((tokens, HID), F32),
            jax.ShapeDtypeStruct((tokens, HID), F32),
            jax.ShapeDtypeStruct((2 * half // THD, tokens, tokens), BF),
            jax.ShapeDtypeStruct((2 * half // THD, 1, tokens), F32),
            gathered,
            gathered,
        ),
        in_specs=[SMEM] * 2 + [VMEM] * 5 + [ANY] * 6,
        out_specs=(VMEM, VMEM, ANY, VMEM, ANY, ANY),
        scratch_shapes=[
            V((tokens, 3 * wide), BF),
            V((tokens, breadth), F32),
            V((tokens, breadth), BF),
            V(entry.shape, BF),
            V((2,) + project.shape, BF),
            V((2,) + mixer.shape, BF),
            V((2,) + expand.shape, BF),
            V((2,) + shrink.shape, BF),
            V(leave.shape, BF),
            V((tokens, half), BF),
            V((tokens, half), BF),
            V((half, tokens), BF),
            V((2, tokens, half), BF),
            V((LOG_SLOTS, tokens, ATT), BF),
            V((2, tokens, ATT), F32),
            V((2, tokens, ATT), BF),
            V((ROWS_FF, hidden_half), BF),
            V(sent, BF),
            D((7,)),
            D((LOG_SLOTS,)),
            D((4,)),
            D((4,)),
            D((n_rows - 1,)),
            D((n_rows - 1,)),
            D,
            D,
        ],
        compiler_params=pltpu.CompilerParams(
            collective_id=1, has_side_effects=True, vmem_limit_bytes=62 << 20
        ),
        cost_estimate=pl.CostEstimate(
            flops=33_000_000_000, bytes_accessed=40 << 20, transcendentals=0
        ),
    )(bounds, micro_batch, words, conv, extra, norms, weight, entry, project, mixer, expand, shrink, leave)


def matrices_kernel(
    owners, tiles_own, tiles_mate, wide_w, pair_w, mixer_w, expand_w, shrink_w, leave_w, counted, tile_at, later_at, slot, held
):
    n_rows, n_lines, breadth = tiles_own.shape
    n_slots, n_tiles = tile_at.shape[0], owners.shape[0]
    slots = n_slots // n_rows
    lines = breadth // 2
    core = lax.axis_index("heads")
    nin, nff = HID // breadth, SFF // breadth
    at_pair, at_mixer, at_ff = 2 * nin, 2 * nin + 2, 2 * nin + 3
    at_shrink = at_ff + NFFN * nff
    at_leave = at_shrink + NFFN * nff

    def clear(i, carry):
        tile_at[i] = n_tiles
        later_at[i] = n_tiles - at_mixer
        return carry

    lax.fori_loop(0, n_slots, clear, 0)

    def clear_held(i, carry):
        held[i] = 0
        return carry

    lax.fori_loop(0, n_rows, clear_held, 0)

    def assign(i, carry):
        owner = owners[i]
        rank = held[owner]
        held[owner] = rank + 1
        slot[i] = rank
        tile_at[owner * slots + rank] = i
        later_at[owner * slots + rank] = jnp.where(i >= at_mixer, i - at_mixer, n_tiles - at_mixer)
        return carry

    lax.fori_loop(0, n_tiles, assign, 0)

    def at(j):
        return slice(j * breadth, (j + 1) * breadth)

    def load(i, ref, row, col):
        owner = owners[i]
        there = pl.ds(pl.multiple_of(slot[i] * lines, lines), lines)
        own_line = pl.multiple_of(core * lines, lines)
        mate_line = pl.multiple_of((1 - core) * lines, lines)
        ref[pl.ds(row * breadth + own_line, lines), at(col)] = tiles_own[owner, there]
        ref[pl.ds(row * breadth + mate_line, lines), at(col)] = tiles_mate[owner, there]

    for j in range(nin):
        load(j, wide_w, j, 0)
        load(nin + j, wide_w, j, 1)
        load(at_leave + j, leave_w, 0, j)
    load(at_pair, pair_w, 0, 0)
    load(at_pair + 1, pair_w, 0, 1)
    load(at_mixer, mixer_w, 0, 0)
    for b in range(NFFN):
        for j in range(nff):
            load(at_ff + b * nff + j, expand_w.at[b], 0, j)
            load(at_shrink + b * nff + j, shrink_w.at[b], j, 0)
    digits = tiles_own[0, slots * lines :].astype(F32)
    for i in range(1, n_rows):
        digits = digits + tiles_own[i, slots * lines :].astype(F32)
    counted[...] = digits[0:8]


def matrices_of(owners, tiles_own, tiles_mate, slots):
    n_rows, _, w = tiles_own.shape
    shapes = [(HID, 2 * w), (w, 2 * w), (w, w), (NFFN, w, SFF), (NFFN, SFF, w), (w, HID)]
    places = jax.ShapeDtypeStruct((n_rows * slots,), jnp.int32)
    return pl.pallas_call(
        matrices_kernel,
        out_shape=[jax.ShapeDtypeStruct(s, BF) for s in shapes]
        + [jax.ShapeDtypeStruct((8, w), F32), places, places],
        in_specs=[SMEM, VMEM, VMEM],
        out_specs=[VMEM] * 7 + [SMEM] * 2,
        scratch_shapes=[pltpu.SMEM(owners.shape, jnp.int32), pltpu.SMEM((n_rows,), jnp.int32)],
        compiler_params=pltpu.CompilerParams(vmem_limit_bytes=40 << 20),
    )(owners, tiles_own, tiles_mate)


def three_parts(value):
    high = value.astype(BF).astype(F32)
    middle = (value - high).astype(BF).astype(F32)
    return high, middle, value - high - middle


def student_kernel(
    side,
    deep,
    tile_at,
    bounds,
    micro_batch,
    counted,
    wide_w,
    pair_w,
    mixer_w,
    expand_w,
    shrink_w,
    leave_w,
    inputs,
    feature,
    logs,
    sums,
    small,
    summed_out,
    rest_out,
    lines_out,
    inputs_v,
    logs_v,
    low_v,
    narrow_v,
    first_v,
    query_v,
    key_m,
    value_m,
    key_t,
    value_t,
    context_t,
    contextlow_t,
    blocklow_v,
    hidden_v,
    sum_v,
    dsum_v,
    dcontext_v,
    dcontext_t,
    dvalue_v,
    dkey_v,
    dpair_v,
    scores_v,
    dweight_v,
    weight_v,
    dscores_v,
    g_leave,
    g_mixer,
    g_expand,
    g_shrink,
    small_v,
    tiles_v,
    pool,
    pair_in,
    first_in,
    second,
    second_in,
    third,
    third_in,
    half_own,
    half_in,
    rest_v,
    rest_in,
    rest_sum,
    rest_part,
    rest_all,
    lines_v,
    in_sem,
    sem,
    pair_send,
    pair_recv,
    first_send,
    first_recv,
    second_send,
    second_recv,
    third_send,
    third_recv,
    half_send,
    half_recv,
    swap_send,
    swap_recv,
    part_send,
    part_recv,
    all_send,
    all_recv,
    over_send,
    over_recv,
):
    tokens = inputs.shape[0]
    breadth = small.shape[1] - HID
    breadth = breadth // (2 + NFFN)
    row, core = lax.axis_index("rows"), lax.axis_index("heads")
    n_rows = side * side * deep
    mate = (row, 1 - core)
    barrier = pltpu.get_barrier_semaphore()
    pl.semaphore_signal(barrier, inc=1, device_id=mate, device_id_type=MESH)

    def greet(d, carry):
        peer = (lax.rem(row + d, n_rows), core)
        pl.semaphore_signal(barrier, inc=1, device_id=peer, device_id_type=MESH)
        return carry

    lax.fori_loop(1, n_rows, greet, 0)
    loads = [
        (inputs, inputs_v),
        (feature.at[:, pl.ds(0, ATT)], dweight_v.at[0]),
        (feature.at[:, pl.ds(ATT, ATT)], dweight_v.at[1]),
    ]
    loads = [pltpu.make_async_copy(p, q, in_sem.at[n]) for n, (p, q) in enumerate(loads)]
    for c in loads:
        c.start()

    def logs_copy(n):
        return pltpu.make_async_copy(logs.at[:, :, pl.ds(n * ATT, ATT)], logs_v.at[n % 2], sem.at[n % 2])

    for n in range(2):
        logs_copy(n).start()
    length, batch = bounds[core, 1], micro_batch[core]
    slots = summed_out.shape[0]
    lines = breadth // 2
    for ref in (rest_v, g_leave, g_mixer, g_expand, g_shrink, dvalue_v, dkey_v, small_v):
        ref[...] = jnp.zeros_like(ref)
    plane = side * side

    def of_row(n):
        return n // plane, n // side % side, n % side

    digits = counted[...]
    digits = digits[0:1]
    at_lane = lax.broadcasted_iota(jnp.int32, digits.shape, 1)
    digits = jnp.where(
        at_lane == 2 * batch,
        digits * COUNT_BASE,
        jnp.where(at_lane == 2 * batch + 1, digits, 0.0),
    )
    inverse = 1.0 / jnp.sum(digits, 1, keepdims=True)
    nin = HID // breadth
    nff = SFF // breadth

    def at(j):
        return slice(j * breadth, (j + 1) * breadth)

    at_pair, at_mixer, at_ff = 2 * nin, 2 * nin + 2, 2 * nin + 3
    at_shrink = at_ff + NFFN * nff
    at_leave = at_shrink + NFFN * nff
    def gain(n):
        return small[0:1, at(n)]

    def bias(n):
        return small[1:2, at(n)]

    tail = (2 + NFFN) * breadth
    gain_out, bias_out = small[0:1, tail:], small[1:2, tail:]
    lane = lax.broadcasted_iota(jnp.int32, (1, breadth), 1)
    of_head = [(lane // SHD) == h for h in range(SHEADS)]
    loads[0].wait()
    for start in range(0, tokens, ROWS_FF):
        r = slice(start, start + ROWS_FF)
        low = inputs_v[r].astype(BF)
        low_v[r] = low
        both = dot(low, wide_w[...])
        narrow, value = both[:, :breadth], both[:, breadth:]
        narrow_v[r] = narrow
        first = narrow * gain(0) + bias(0)
        first_v[r] = first
        pair = dot(first.astype(BF), pair_w[...])
        query, key = pair[:, :breadth], pair[:, breadth:]
        query_v[r, :breadth] = query.astype(BF)
        place = lax.broadcasted_iota(jnp.int32, (ROWS_FF, 1), 0) + start
        mask = jnp.where(place < length, 0.0, MASKED_SCORE)
        for h in range(SHEADS):
            key_m[h, r, :breadth] = jnp.where(of_head[h], key, 0.0).astype(BF)
            value_m[h, r, :breadth] = jnp.where(of_head[h], value, 0.0).astype(BF)
            of_part = (lane >= 1 + 3 * h) & (lane < 4 + 3 * h)
            less = jnp.where(of_part, -1.0, 0.0)
            key_m[h, r, breadth:] = jnp.where(lane == 0, mask, less).astype(BF)
            value_m[h, r, breadth:] = jnp.broadcast_to(less, (ROWS_FF, breadth)).astype(BF)
        query_v[r, breadth:] = jnp.broadcast_to(jnp.where(lane == 0, 1.0, 0.0), (ROWS_FF, breadth)).astype(BF)
        key_t[:, r] = key.T.astype(BF)
        value_t[:, r] = value.T.astype(BF)
    scale = SHD**-0.5
    scale2 = scale * LOG2E

    def extra_columns(mark, values):
        rows = [jnp.full((1, ATT), mark, F32)]
        for v in values:
            rows.extend(three_parts(v))
        rows.append(jnp.zeros((breadth - len(rows), ATT), F32))
        return jnp.concatenate(rows, 0).T.astype(BF)

    def forward(n, carry):
        r = pl.ds(pl.multiple_of(n * ATT, ATT), ATT)
        query = query_v[r]
        shifts, parts = [], []
        scores_v[0] = dot_nt(key_m[0], query)
        for h in range(SHEADS):
            if h + 1 < SHEADS:
                scores_v[(h + 1) % 2] = dot_nt(key_m[h + 1], query)
            scores, weight = scores_v.at[h % 2], weight_v.at[h % 2]
            top = column_max(scores)
            part = 0.0
            for c in split_rows(scores):
                piece = jnp.exp2((scores[c] - top) * scale2)
                weight[c] = piece.astype(BF)
                part = part + piece
            total = jnp.sum(part, 0, keepdims=True)
            shifts.append(top + jnp.log2(total) * (1.0 / scale2))
            parts.append(dot(value_t[h * SHD : (h + 1) * SHD], weight[...]) * (1.0 / total))
        mixed = jnp.concatenate(parts, 0)
        context_t[:, r] = mixed
        contextlow_t[:, r] = mixed.astype(BF)
        query_v[r, breadth:] = extra_columns(1.0, shifts)
        return carry

    lax.fori_loop(0, tokens // ATT, forward, 0)

    def row_sums(n, d, value):
        small_v[0:1, at(n)] += jnp.sum(d * value, 0, keepdims=True)
        small_v[1:2, at(n)] += jnp.sum(d, 0, keepdims=True)

    def feed(n, loss):
        r = pl.ds(pl.multiple_of(n * ROWS_FF, ROWS_FF), ROWS_FF)
        place = lax.broadcasted_iota(jnp.int32, (ROWS_FF, 1), 0) + n * ROWS_FF
        weight = jnp.where(place < length, inverse, 0.0)
        context = context_t[:, r].T.astype(BF)
        mixed_sum = dot(context, mixer_w[...]) + first_v[r]
        current = mixed_sum * gain(1) + bias(1)
        for b in range(NFFN):
            low = current.astype(BF)
            blocklow_v[b] = low
            hidden = jnp.maximum(dot(low, expand_w[b]), 0.0).astype(BF)
            hidden_v[b] = hidden
            total = dot(hidden, shrink_w[b]) + current
            sum_v[b] = total
            current = total * gain(2 + b) + bias(2 + b)
        joined = dot(current.astype(BF), leave_w[...]) + inputs_v[r]
        differ = joined * gain_out + bias_out - jnp.concatenate([dweight_v[0, r], dweight_v[1, r]], 1)
        loss = loss + jnp.sum(weight * jnp.mean(differ * differ, -1, keepdims=True), 0, keepdims=True)
        outer = differ * (weight * (2.0 / HID))
        small_v[0:1, tail:] += jnp.sum(outer * joined, 0, keepdims=True)
        small_v[1:2, tail:] += jnp.sum(outer, 0, keepdims=True)
        back = (outer * gain_out).astype(BF)
        g_leave[...] += dot(current.T.astype(BF), back)
        d = dot_nt(back, leave_w[...])
        for b in reversed(range(NFFN)):
            row_sums(2 + b, d, sum_v[b])
            d_sum = d * gain(2 + b)
            hidden = hidden_v[b]
            g_shrink[b] += dot(d_sum.T.astype(BF), hidden)
            d_hidden = dot_nt(d_sum.astype(BF), shrink_w[b])
            d_before = jnp.where(hidden > 0, d_hidden, 0.0).astype(BF)
            g_expand[b] += dot(blocklow_v[b].T, d_before)
            d = d_sum + dot_nt(d_before, expand_w[b])
        row_sums(1, d, mixed_sum)
        d_sum = d * gain(1)
        dsum_v[r] = d_sum
        d_mixed = d_sum.astype(BF)
        g_mixer[...] += dot(contextlow_t[:, r], d_mixed)
        d_context = dot_nt(d_mixed, mixer_w[...])
        dcontext_v[r, :breadth] = d_context.astype(BF)
        dcontext_t[:, r] = d_context.astype(BF).astype(F32).T
        return loss

    for c in loads[1:]:
        c.wait()
    loss = lax.fori_loop(0, tokens // ROWS_FF, feed, jnp.zeros((1, 1), F32))
    n_rest = at_mixer
    tiles_v[0] = g_mixer[...].astype(BF)
    for j in range(nin):
        tiles_v[at_leave - n_rest + j] = g_leave[:, at(j)].astype(BF)
    for b in range(NFFN):
        for j in range(nff):
            tiles_v[at_ff - n_rest + b * nff + j] = g_expand[b, :, at(j)].astype(BF)
            tiles_v[at_shrink - n_rest + b * nff + j] = g_shrink[b, :, at(j)].T.astype(BF)
    nothing = tiles_v.shape[0] - 1
    tiles_v[nothing] = jnp.zeros((breadth, breadth), BF)
    z, y, x = row // plane, (row // side) % side, row % side
    mine = pl.multiple_of(core * lines, lines)
    theirs = pl.multiple_of((1 - core) * lines, lines)
    my_half = pl.multiple_of(core * slots * lines, slots * lines)
    their_half = pl.multiple_of((1 - core) * slots * lines, slots * lines)
    straight = core == 0
    a, b_ = jnp.where(straight, x, y), jnp.where(straight, y, x)
    mate_a = b_

    def lay(n, carry):
        which = tile_at[n]
        zz, yy, xx = of_row(n // slots)
        line = pl.multiple_of(n % slots * lines, lines)
        pool[zz, yy, xx, pl.ds(line, lines)] = tiles_v[which, :lines]
        pool[zz, yy, xx, pl.ds(slots * lines + line, lines)] = tiles_v[which, lines:]
        return carry

    lax.fori_loop(0, n_rows * slots, lay, 0)
    pl.semaphore_wait(barrier, n_rows)

    def row_at(xx, yy, zz):
        return zz * plane + yy * side + xx

    def along_a(aa):
        return (jnp.where(straight, row_at(aa, y, z), row_at(x, aa, z)), core)

    def along_b(bb):
        return (jnp.where(straight, row_at(x, bb, z), row_at(bb, y, z)), core)

    def along_z(zz):
        return (row_at(x, y, zz), core)

    def remote(src, dst, send, recv, peer):
        return pltpu.make_async_remote_copy(
            src_ref=src,
            dst_ref=dst,
            send_sem=send,
            recv_sem=recv,
            device_id=peer,
            device_id_type=MESH,
        )

    order = list(range(1, side)) + [0]
    for d in order:
        piece = lax.rem(mate_a + d, side)
        half = pl.ds(their_half, slots * lines)
        by_y = remote(pool.at[:, piece, :, half, :], pair_in.at[d], pair_send.at[d], pair_recv.at[d], mate)
        by_x = remote(pool.at[:, :, piece, half, :], pair_in.at[d], pair_send.at[d], pair_recv.at[d], mate)

        @pl.when(straight)
        def _():
            by_y.start()

        @pl.when(jnp.logical_not(straight))
        def _():
            by_x.start()

    def pair_copy(d):
        return remote(pool.at[:, 0, :, pl.ds(0, slots * lines), :], pair_in.at[d], pair_send.at[d], pair_recv.at[d], mate)

    first_copies, second_copies, third_copies = [], [], []

    def add_pair():
        for d in order:
            pair_copy(d).wait_recv()
            aa = lax.rem(a + d, side)

            def add(i, carry):
                zz, bb = i // side, i % side
                xx, yy = jnp.where(straight, aa, bb), jnp.where(straight, bb, aa)
                own = pool[zz, yy, xx, pl.ds(my_half, slots * lines)].astype(F32)
                pair_in[d, zz, bb] = (own + pair_in[d, zz, bb].astype(F32)).astype(BF)
                return carry

            lax.fori_loop(0, deep * side, add, 0)
            if d:
                c = remote(pair_in.at[d], first_in.at[d - 1], first_send.at[d - 1], first_recv.at[d - 1], along_a(aa))
                c.start()
                first_copies.append(c)

    def add_first():
        for c in first_copies:
            c.wait_recv()
        for d in order:
            bb = lax.rem(b_ + d, side)

            def add(zz, carry):
                s = pair_in[0, zz, bb].astype(F32)
                for j in range(side - 1):
                    s = s + first_in[j, zz, bb].astype(F32)
                second[d, zz] = s.astype(BF)
                return carry

            lax.fori_loop(0, deep, add, 0)
            if d:
                c = remote(second.at[d], second_in.at[d - 1], second_send.at[d - 1], second_recv.at[d - 1], along_b(bb))
                c.start()
                second_copies.append(c)

    def add_second():
        for c in second_copies:
            c.wait_recv()
        for d in list(range(1, deep)) + [0]:
            zz = lax.rem(z + d, deep)
            s = second[0, zz].astype(F32)
            for j in range(side - 1):
                s = s + second_in[j, zz].astype(F32)
            if d:
                third[d - 1] = s.astype(BF)
                c = remote(third.at[d - 1], third_in.at[d - 1], third_send.at[d - 1], third_recv.at[d - 1], along_z(zz))
                c.start()
                third_copies.append(c)
            else:
                half_own[...] = s

    def add_third():
        for c in third_copies:
            c.wait_recv()
        s = half_own[...]
        for j in range(deep - 1):
            s = s + third_in[j].astype(F32)
        half_own[...] = s
        half_copy.start()

    half_copy = remote(half_own, half_in, half_send, half_recv, mate)
    stages = [add_pair, add_first, add_second]

    log_share = jnp.log2(inverse * (1.0 / SHEADS))

    def backward(n, loss):
        r = slice(n * ATT, (n + 1) * ATT)
        place = lax.broadcasted_iota(jnp.int32, (1, ATT), 1) + n * ATT
        inside = place < length
        share = jnp.where(inside, inverse * (1.0 / SHEADS), 0.0)
        share2 = jnp.where(inside, log_share, MASKED_SCORE)
        less = []
        for h in range(SHEADS):
            heads = slice(h * SHD, (h + 1) * SHD)
            along = jnp.sum(context_t[heads, r] * dcontext_t[heads, r], 0, keepdims=True)
            less.append(along - share * sums[h, :, r])
        dcontext_v[r, breadth:] = extra_columns(0.0, less)
        query, d_context = query_v[r], dcontext_v[r]
        logs_copy(n).wait()
        here = logs_v.at[n % 2]

        def products(h):
            scores_v[h % 2] = dot_nt(key_m[h], query)
            dweight_v[h % 2] = dot_nt(value_m[h], d_context)

        products(0)
        parts = []
        gap = 0.0
        for h in range(SHEADS):
            if h + 1 < SHEADS:
                products(h + 1)
            scores, dweight = scores_v.at[h % 2], dweight_v.at[h % 2]
            weight, dscores = weight_v.at[h % 2], dscores_v.at[h % 2]
            for c in split_rows(scores):
                score = scores[c]
                piece = jnp.exp2(score * scale2)
                weight[c] = piece.astype(BF)
                target_log = here[h, c].astype(F32)
                target = jnp.exp2(target_log * LOG2E + share2)
                gap = gap + target * (target_log - score * scale)
                dscores[c] = (piece * dweight[c] - target).astype(BF)
            none = jnp.zeros((ATT, breadth), BF)
            dvalue_v[...] += dot(weight[...], jnp.where(of_head[h], d_context[:, :breadth], none))
            dkey_v[...] += dot(dscores[...], jnp.where(of_head[h], query[:, :breadth], none))
            parts.append(dot(key_t[h * SHD : (h + 1) * SHD], dscores[...]))
        dpair_v[r, at(0)] = (jnp.concatenate(parts, 0) * scale).T.astype(BF)
        if n + 2 < tokens // ATT:
            logs_copy(n + 2).start()
        return loss + jnp.sum(jnp.sum(gap, 0, keepdims=True), 1, keepdims=True)

    for n in range(tokens // ATT):
        loss = backward(n, loss)
        if n < len(stages):
            stages[n]()
    dpair_v[:, at(1)] = (dkey_v[...] * scale).astype(BF)
    d_pair = dpair_v[...]
    d_first = dsum_v[...] + dot_nt(d_pair, pair_w[...])
    row_sums(0, d_first, narrow_v[...])
    g_pair = dot(first_v[...].T.astype(BF), d_pair)
    wide_t = jnp.concatenate([(d_first * gain(0)).T.astype(BF), dvalue_v[...].T.astype(BF)], 0)
    g_wide = dot(wide_t, low_v[...])
    n_lines = small.shape[1] // breadth
    lines_v[...] = jnp.zeros_like(lines_v)
    for j in range(n_lines):
        lines_v[j : j + 1] = small_v[0:1, at(j)]
        lines_v[n_lines + j : n_lines + j + 1] = small_v[1:2, at(j)]
    lines_v[2 * n_lines : 2 * n_lines + 1, 0:1] = loss
    add_third()
    summed = half_own[...]
    lines_v[2 * n_lines + 1 : 2 * n_lines + 2] = jnp.sum(summed * summed, 0, keepdims=True)
    groups = lines_v.shape[0] // 8
    top = 16 * groups
    each = n_rest // 2

    def two_parts(value):
        high = value.astype(BF)
        return high, (value - high.astype(F32)).astype(BF)

    for g in range(groups):
        high, rest = two_parts(lines_v[8 * g : 8 * g + 8])
        rest_v[0, 16 * g : 16 * g + 8] = high
        rest_v[0, 16 * g + 8 : 16 * g + 16] = rest

    def keep(n, value):
        line = top + (n % each) * breadth
        rest_v[n // each, line : line + breadth] = value.astype(BF)

    for j in range(nin):
        keep(j, g_wide[:breadth, at(j)].T)
        keep(nin + j, g_wide[breadth:, at(j)].T)
    keep(at_pair, g_pair[:, at(0)])
    keep(at_pair + 1, g_pair[:, at(1)])
    swap = remote(rest_v.at[1 - core], rest_in, swap_send, swap_recv, mate)
    swap.start()
    swap.wait()
    rest_sum[...] = (rest_v[core].astype(F32) + rest_in[...].astype(F32)).astype(BF)
    for g in range(groups):
        high_at, rest_at = slice(16 * g, 16 * g + 8), slice(16 * g + 8, 16 * g + 16)
        value = rest_v[core, high_at].astype(F32) + rest_v[core, rest_at].astype(F32)
        value = value + rest_in[high_at].astype(F32) + rest_in[rest_at].astype(F32)
        rest_sum[high_at], rest_sum[rest_at] = two_parts(value)
    chunk = rest_part.shape[1]

    def lines_of(n):
        return pl.ds(pl.multiple_of(n * chunk, chunk), chunk)

    def part_copy(d):
        to = lax.rem(row + d, n_rows)
        return remote(rest_sum.at[lines_of(to)], rest_part.at[d - 1], part_send.at[d - 1], part_recv.at[d - 1], (to, core))

    def all_copy(d):
        here = rest_all.at[core, lines_of(row)]
        return remote(here, here, all_send.at[d - 1], all_recv.at[d - 1], (lax.rem(row + d, n_rows), core))

    def each_peer(act):
        def one(d, carry):
            act(d)
            return carry

        lax.fori_loop(1, n_rows, one, 0)

    each_peer(lambda d: part_copy(d).start())
    each_peer(lambda d: part_copy(d).wait())
    total = lax.fori_loop(
        0, n_rows - 1, lambda d, t: t + rest_part[d].astype(F32), rest_sum[lines_of(row)].astype(F32)
    )
    high_of = []
    for g in range(chunk // 16):
        piece = total[16 * g : 16 * g + 16]
        high, rest = two_parts(piece[:8] + piece[8:])
        split = jnp.concatenate([high.astype(F32), rest.astype(F32)], 0)
        high_of.append(jnp.where(row * (chunk // 16) + g < groups, split, piece))
    rest_all[core, lines_of(row)] = jnp.where(core == 0, jnp.concatenate(high_of, 0), total).astype(BF)
    each_peer(lambda d: all_copy(d).start())
    half_copy.wait()
    for k in range(slots):
        summed_out[k, pl.ds(mine, lines)] = half_own[k * lines : (k + 1) * lines]
        summed_out[k, pl.ds(theirs, lines)] = half_in[k * lines : (k + 1) * lines]
    each_peer(lambda d: all_copy(d).wait())
    over = remote(rest_all.at[core], rest_all.at[core], over_send, over_recv, mate)
    over.start()
    for d in order:
        pair_copy(d).wait_send()
    for c in first_copies + second_copies + third_copies:
        c.wait_send()
    over.wait()
    squares = jnp.zeros((1, breadth), F32)
    for n in range(n_rest):
        line = top + (n % each) * breadth
        rest_out[n] = rest_all[n // each, line : line + breadth]
        tile = rest_out[n].astype(F32)
        squares = squares + jnp.sum(tile * tile, 0, keepdims=True)
    for g in range(groups):
        high = rest_all[0, 16 * g : 16 * g + 8].astype(F32)
        lines_out[8 * g : 8 * g + 8] = high + rest_all[0, 16 * g + 8 : 16 * g + 16].astype(F32)
    lines_out[2 * n_lines + 2 : 2 * n_lines + 3] = squares


def student(n_rows, tile_at, bounds, micro_batch, counted, matrices, inputs, feature, logs, sums, small, slots):
    tokens = inputs.shape[0]
    w = counted.shape[1]
    deep = 4
    side = math.isqrt(n_rows // deep)
    assert side * side * deep == n_rows
    n_lines = 8 * -(-(2 * small.shape[1] // w + 3) // 8)
    n_rest = 2 * HID // w + 2
    n_tiles = 1 + 2 * NFFN * (SFF // w) + HID // w
    half = w // 2
    in_half = 2 * n_lines + (HID // w + 1) * w
    chunk = 16 * -(-in_half // (16 * n_rows))
    s1, d1 = side - 1, deep - 1
    D = pltpu.SemaphoreType.DMA

    def low(*shape):
        return pltpu.VMEM(shape, BF)

    def full(*shape):
        return pltpu.VMEM(shape, F32)

    return pl.pallas_call(
        functools.partial(student_kernel, side, deep),
        out_shape=(
            jax.ShapeDtypeStruct((slots, w, w), F32),
            jax.ShapeDtypeStruct((n_rest, w, w), BF),
            jax.ShapeDtypeStruct((n_lines, w), F32),
        ),
        in_specs=[SMEM] * 3 + [VMEM] * 7 + [ANY, ANY, ANY, VMEM, VMEM],
        out_specs=(VMEM, VMEM, VMEM),
        scratch_shapes=[
            full(tokens, HID),
            low(2, SHEADS, tokens, ATT),
            low(tokens, HID),
            full(tokens, w),
            full(tokens, w),
            low(tokens, 2 * w),
            low(SHEADS, tokens, 2 * w),
            low(SHEADS, tokens, 2 * w),
            low(w, tokens),
            low(w, tokens),
            full(w, tokens),
            low(w, tokens),
            low(NFFN, ROWS_FF, w),
            low(NFFN, ROWS_FF, SFF),
            full(NFFN, ROWS_FF, w),
            full(tokens, w),
            low(tokens, 2 * w),
            full(w, tokens),
            full(tokens, w),
            full(tokens, w),
            low(tokens, 2 * w),
            full(2, tokens, ATT),
            full(2, tokens, ATT),
            low(2, tokens, ATT),
            low(2, tokens, ATT),
            full(w, HID),
            full(w, w),
            full(NFFN, w, SFF),
            full(NFFN, w, SFF),
            full(8, small.shape[1]),
            low(n_tiles + 1, w, w),
            low(deep, side, side, slots * w, w),
            low(side, deep, side, slots * half, w),
            low(s1, deep, side, slots * half, w),
            low(side, deep, slots * half, w),
            low(s1, deep, slots * half, w),
            low(d1, slots * half, w),
            low(d1, slots * half, w),
            full(slots * half, w),
            full(slots * half, w),
            low(2, chunk * n_rows, w),
            low(chunk * n_rows, w),
            low(chunk * n_rows, w),
            low(n_rows - 1, chunk, w),
            low(2, chunk * n_rows, w),
            full(n_lines, w),
            D((3,)),
            D((2,)),
            D((side,)),
            D((side,)),
            D((s1,)),
            D((s1,)),
            D((s1,)),
            D((s1,)),
            D((d1,)),
            D((d1,)),
            D,
            D,
            D,
            D,
            D((n_rows - 1,)),
            D((n_rows - 1,)),
            D((n_rows - 1,)),
            D((n_rows - 1,)),
            D,
            D,
        ],
        compiler_params=pltpu.CompilerParams(
            collective_id=0, has_side_effects=True, vmem_limit_bytes=63 << 20
        ),
        cost_estimate=pl.CostEstimate(
            flops=15_000_000_000, bytes_accessed=16 << 20, transcendentals=0
        ),
    )(tile_at, bounds, micro_batch, counted, *matrices, inputs, feature, logs, sums, small)


def update_kernel(
    n_tiles, tile_at, step, own, summed, rest, lines, weight, first, second, small, small_first, small_second,
    loss_out, norm_out, tiles_out, first_out, second_out, small_out, small_first_out, small_second_out, small_grad_out,
    small_v,
):
    breadth = summed.shape[2]
    n_lines = small.shape[1] // breadth
    steps = step[0]
    first_fix = 1.0 - lax.fori_loop(0, steps, lambda i, p: p * BETA_FIRST, jnp.float32(1.0))
    second_fix = 1.0 - lax.fori_loop(0, steps, lambda i, p: p * BETA_SECOND, jnp.float32(1.0))

    def adam(w, m, v, g, decay):
        m = BETA_FIRST * m + (1.0 - BETA_FIRST) * g
        v = BETA_SECOND * v + (1.0 - BETA_SECOND) * g * g
        change = m / first_fix / (jnp.sqrt(v / second_fix) + ADAM_EPSILON) + decay * w
        return w - LEARN_RATE * change, m, v

    line = lambda n: lines[n : n + 1]
    squares = line(2 * n_lines + 1) + line(2 * n_lines + 2)
    for n in range(2 * n_lines):
        squares = squares + line(n) * line(n)
    norm = jnp.sqrt(jnp.sum(squares, 1, keepdims=True))
    norm_out[...] = norm
    loss_out[...] = line(2 * n_lines)[:, 0:1]
    factor = CLIP_NORM / jnp.maximum(norm, CLIP_NORM)
    for n in range(n_lines):
        cols = slice(n * breadth, (n + 1) * breadth)
        small_v[0:1, cols] = line(n)
        small_v[1:2, cols] = line(n_lines + n)
    small_grad = small_v[0:2] * factor
    small_grad_out[...] = small_grad
    w, m, v = adam(small[...], small_first[...], small_second[...], small_grad, 0.0)
    small_out[...] = w
    small_first_out[...] = m
    small_second_out[...] = v

    slots, n_rest = summed.shape[0], rest.shape[0]
    for s in range(summed.shape[0]):
        which = tile_at[own[0] * slots + s]
        keep = which < n_tiles
        other = rest[jnp.minimum(which, n_rest - 1)].astype(F32)
        total = summed[s] + jnp.where(which < n_rest, other, 0.0)
        w, m, v = adam(weight[s], first[s], second[s], total * factor, WEIGHT_DECAY)
        tiles_out[s] = jnp.where(keep, w, 0.0)
        first_out[s] = jnp.where(keep, m, 0.0)
        second_out[s] = jnp.where(keep, v, 0.0)


def update(n_tiles, tile_at, step, own, summed, rest, lines, weight, first, second, small, small_first, small_second):
    one = jax.ShapeDtypeStruct((1, 1), F32)
    tile = jax.ShapeDtypeStruct(weight.shape, F32)
    row = jax.ShapeDtypeStruct(small.shape, F32)
    return pl.pallas_call(
        functools.partial(update_kernel, n_tiles),
        out_shape=(one, one, tile, tile, tile, row, row, row, row),
        in_specs=[SMEM] * 3 + [VMEM] * 9,
        out_specs=(VMEM,) * 9,
        scratch_shapes=[pltpu.VMEM((8, small.shape[1]), F32)],
        compiler_params=pltpu.CompilerParams(vmem_limit_bytes=24 << 20),
        cost_estimate=pl.CostEstimate(flops=2_000_000, bytes_accessed=2 << 20, transcendentals=0),
    )(tile_at, step, own, summed, rest, lines, weight, first, second, small, small_first, small_second)


def on_device(
    token_ids,
    bounds,
    micro_batch,
    owners,
    step_count,
    word_table,
    conv_weight,
    embed_extra,
    teacher_entry,
    teacher_project,
    teacher_mixer,
    teacher_expand,
    teacher_shrink,
    teacher_leave,
    teacher_norms,
    tile_weight,
    tile_first,
    tile_second,
    small_weight,
    small_first,
    small_second,
):
    core = lax.axis_index("heads")
    n_rows = lax.axis_size("rows")
    assert token_ids.shape[0] == lax.axis_size("heads")
    row_ids = lax.dynamic_index_in_dim(token_ids, core, 0, keepdims=False)
    words = word_table.at[row_ids].get(mode="promise_in_bounds")
    inputs, feature, logs, sums, tiles_own, tiles_mate = teacher(
        n_rows,
        bounds,
        micro_batch,
        words,
        conv_weight,
        embed_extra,
        teacher_norms,
        tile_weight,
        teacher_entry,
        teacher_project.transpose(1, 0, 2),
        teacher_mixer,
        teacher_expand,
        teacher_shrink,
        teacher_leave,
    )
    *matrices, counted, tile_at, later_at = matrices_of(owners, tiles_own, tiles_mate, tile_weight.shape[0])
    summed, rest, lines = student(
        n_rows,
        later_at,
        bounds,
        micro_batch,
        counted,
        matrices,
        inputs,
        feature,
        logs,
        sums,
        small_weight,
        tile_weight.shape[0],
    )
    own = lax.axis_index("rows")[None]
    loss, norm, *rest = update(
        owners.shape[0],
        tile_at,
        step_count,
        own,
        summed,
        rest,
        lines,
        tile_weight,
        tile_first,
        tile_second,
        small_weight,
        small_first,
        small_second,
    )
    return (loss[0, 0], norm[0, 0], *rest)


def solution(mesh):
    placed = (
        P("rows", None),
        P("rows", None),
        P("rows"),
        P(),
        P(),
        P(),
        P(),
        P(),
        P(),
        P(None, None, "heads"),
        P("heads", None),
        P(None, "heads"),
        P("heads", None),
        P(),
        P(),
        P("rows", None, None),
        P("rows", None, None),
        P("rows", None, None),
        P(),
        P(),
        P(),
    )
    tiles = P("rows", None, None)
    return jax.shard_map(
        on_device,
        mesh=mesh,
        in_specs=placed,
        out_specs=(P(), P(), tiles, tiles, tiles, P(), P(), P(), P()),
        check_vma=False,
    )
```

```python
import functools
import math

import jax
import jax.numpy as jnp
from jax import lax
from jax.experimental import pallas as pl
from jax.experimental.pallas import tpu as pltpu
from jax.sharding import PartitionSpec as P

HID = 512
THD = 256
SHEADS = 4
SHD = 32
SFF = 512
NFFN = 4
NMB = 2
NORM_EPSILON = 1e-05
CLIP_NORM = 0.05
LEARN_RATE = 0.1
BETA_FIRST = 0.9
BETA_SECOND = 0.999
ADAM_EPSILON = 1e-08
WEIGHT_DECAY = 0.01
MASKED_SCORE = -1e30
LOG2E = math.log2(math.e)
COUNT_BASE = 64

ATT = 256
ROWS_FF = 512
CUT_FF = 512
LOG_SLOTS = 4
DEEP = 4

MESH = pl.DeviceIdType.MESH
BF, F32 = jnp.bfloat16, jnp.float32
VMEM = pl.BlockSpec(memory_space=pltpu.VMEM)
SMEM = pl.BlockSpec(memory_space=pltpu.SMEM)
HBM = pl.BlockSpec(memory_space=pltpu.HBM)
ANY = pl.BlockSpec(memory_space=pl.ANY)


def dot(left, right):
    return jnp.dot(left, right, preferred_element_type=F32)


def dot_nt(left, right):
    return lax.dot_general(left, right, (((1,), (1,)), ((), ())), preferred_element_type=F32)


def layer_norm(values, gain_row, bias_row):
    center = values - jnp.mean(values, -1, keepdims=True)
    spread = jnp.mean(center * center, -1, keepdims=True)
    return center * lax.rsqrt(spread + NORM_EPSILON) * gain_row + bias_row


def sum_over(ref, n):
    s = ref[0]
    for i in range(1, n):
        s = s + ref[i]
    return s


def split_rows(refs, rows=64):
    for start in range(0, refs.shape[-2], rows):
        yield slice(start, start + rows)


def column_max(ref):
    best = None
    for c in split_rows(ref):
        best = ref[c] if best is None else jnp.maximum(best, ref[c])
    return jnp.max(best, 0, keepdims=True)


def attend_half(
    length,
    first_head,
    low_v,
    project_v,
    query_v,
    key_v,
    value_t,
    context_v,
    logs_out,
    sums_out,
    logs_v,
    scores_v,
    weight_v,
    sem,
    pending,
):
    tokens = low_v.shape[0]
    width = project_v.shape[2]
    for start in range(0, tokens, ROWS_FF):
        rows = slice(start, start + ROWS_FF)
        low = low_v[rows]
        query_v[rows] = (dot(low, project_v[0]) * THD**-0.5).astype(BF)
        key_v[rows] = dot(low, project_v[1]).astype(BF)
        value_t[:, rows] = dot(low, project_v[2]).T.astype(BF)
    steps = [(h, q) for h in range(width // THD) for q in range(tokens // ATT)]
    least = tokens // 2

    def scores_of(i):
        h, q = steps[i]
        cols = slice(h * THD, (h + 1) * THD)
        query = query_v[q * ATT : (q + 1) * ATT, cols]
        scores_v[i % 2, :least] = dot_nt(key_v[:least, cols], query)
        valid = lax.broadcasted_iota(jnp.int32, (tokens - least, ATT), 0) + least < length
        scores_v[i % 2, least:] = jnp.where(valid, dot_nt(key_v[least:, cols], query), MASKED_SCORE)

    scores_of(0)
    for i, (h, q) in enumerate(steps):
        if len(pending) == LOG_SLOTS:
            pending.pop(0).wait()
        if i + 1 < len(steps):
            scores_of(i + 1)
        at = i % LOG_SLOTS
        scores, weight, logs = scores_v.at[i % 2], weight_v.at[i % 2], logs_v.at[at]
        top = column_max(scores)
        part = 0.0
        for c in split_rows(scores):
            piece = jnp.exp(scores[c] - top)
            weight[c] = piece.astype(BF)
            part = part + piece
        total = jnp.sum(part, 0, keepdims=True)
        shift = top + jnp.log(total)
        part = 0.0
        for c in split_rows(scores):
            piece = (scores[c] - shift).astype(BF)
            logs[c] = piece
            part = part + jnp.exp(piece.astype(F32))
        sums_out[first_head + h, :, q * ATT : (q + 1) * ATT] = jnp.sum(part, 0, keepdims=True)
        mixed = dot(value_t[h * THD : (h + 1) * THD], weight[...]) * (1.0 / total)
        context_v[q * ATT : (q + 1) * ATT, h * THD : (h + 1) * THD] = mixed.T.astype(BF)
        there = logs_out.at[first_head + h, :, pl.ds(q * ATT, ATT)]
        pending.append(pltpu.make_async_copy(logs, there, sem.at[at]))
        pending[-1].start()
    assert len(steps) % LOG_SLOTS == 0


def teacher_kernel(
    bounds,
    micro_batch,
    owners,
    words,
    conv,
    extra,
    norms,
    weight,
    entry,
    project,
    mixer,
    expand,
    shrink,
    leave,
    inputs_out,
    feature_out,
    logs_out,
    sums_out,
    where_out,
    tiles_own,
    tiles_mate,
    trigram,
    hidden_v,
    low_v,
    entry_v,
    project_v,
    mixer_v,
    expand_v,
    shrink_v,
    leave_v,
    query_v,
    key_v,
    value_t,
    context_v,
    logs_v,
    scores_v,
    weight_v,
    inner_v,
    sent,
    in_sem,
    logs_sem,
    swap_send,
    swap_recv,
    tile_send,
    tile_recv,
    pass_send,
    pass_recv,
):
    tokens, wide = words.shape
    breadth = entry.shape[1]
    half = project.shape[2]
    hidden_half = expand.shape[1]
    n_rows = tiles_own.shape[0]
    row, core = lax.axis_index("rows"), lax.axis_index("heads")
    mate = (row, 1 - core)
    start_at, length = bounds[core, 0], bounds[core, 1]
    slots, _, lanes = weight.shape
    lines = weight.shape[1] // 2
    blocks = lines // 16
    for n in range(slots):
        half_tile = weight[n, pl.ds(core * lines, lines)].astype(BF)
        sent[n * blocks : (n + 1) * blocks] = half_tile.reshape(blocks, 16, lanes)
    lane = lax.broadcasted_iota(jnp.int32, (16, lanes), 1)
    digits = jnp.zeros((16, lanes), F32)
    for m in range(NMB):
        held = jnp.int32(0)
        for n in range(micro_batch.shape[0]):
            held = held + jnp.where(micro_batch[n] == m, bounds[n, 1], 0)
        digits = jnp.where(lane == 2 * m, (held // COUNT_BASE).astype(F32), digits)
        digits = jnp.where(lane == 2 * m + 1, (held % COUNT_BASE).astype(F32), digits)
    sent[slots * blocks] = digits.astype(BF)
    n_tiles, n_rest = owners.shape[0], 2 * HID // lanes + 2
    side = math.isqrt(tiles_own.shape[0] // DEEP)
    bits = side.bit_length() - 1
    spot = lax.broadcasted_iota(jnp.int32, (1, where_out.shape[2]), 1)
    owner_of = jnp.zeros(spot.shape, jnp.int32)
    rank_of = jnp.zeros(spot.shape, jnp.int32)
    for i in range(n_tiles):
        owner_of = jnp.where(spot == i, owners[i], owner_of)
    for i in range(n_tiles):
        rank_of = rank_of + jnp.where((owner_of == owners[i]) & (spot > i), 1, 0)
    where_out[0] = lax.shift_right_logical(owner_of, 2 * bits)
    where_out[1] = lax.shift_right_logical(owner_of, bits) & (side - 1)
    where_out[2] = owner_of & (side - 1)
    where_out[3] = rank_of * blocks
    where_out[4] = rank_of * blocks + slots * blocks + 1
    for g in range(where_out.shape[0] // 2 - 2):
        spots = spot + g * where_out.shape[2]
        owner_here = lax.shift_right_logical(spots, slots.bit_length() - 1)
        rank_here = spots & (slots - 1)
        seen = jnp.zeros(spot.shape, jnp.int32)
        which = jnp.full(spot.shape, n_tiles, jnp.int32)
        for i in range(n_tiles):
            same = owner_here == owners[i]
            which = jnp.where(same & (seen == rank_here), i, which)
            seen = seen + jnp.where(same, 1, 0)
        where_out[5 + 2 * g] = which
        where_out[6 + 2 * g] = jnp.where(which >= n_rest, which - n_rest, n_tiles - n_rest)

    def peer(d):
        return (lax.rem(row + d, n_rows), core)

    local = [(entry, entry_v), (project, project_v.at[0]), (mixer, mixer_v.at[0])]
    local += [(expand, expand_v.at[0]), (shrink, shrink_v.at[0]), (leave, leave_v)]
    local += [(sent, tiles_own.at[row])]
    loads = [pltpu.make_async_copy(a, b, in_sem.at[n]) for n, (a, b) in enumerate(local)]
    for c in loads:
        c.start()
    barrier = pltpu.get_barrier_semaphore()
    pl.semaphore_signal(barrier, inc=1, device_id=mate, device_id_type=MESH)

    def greet(d, carry):
        pl.semaphore_signal(barrier, inc=1, device_id=peer(d), device_id_type=MESH)
        return carry

    lax.fori_loop(1, n_rows, greet, 0)
    pl.semaphore_wait(barrier, n_rows)
    swaps = []
    for n, (a, b) in enumerate(((project, project_v), (mixer, mixer_v), (expand, expand_v), (shrink, shrink_v))):
        swaps.append(
            pltpu.make_async_remote_copy(
                src_ref=a,
                dst_ref=b.at[1],
                send_sem=swap_send.at[n],
                recv_sem=swap_recv.at[n],
                device_id=mate,
                device_id_type=MESH,
            )
        )
        swaps[-1].start()

    def tile_copy(d):
        return pltpu.make_async_remote_copy(
            src_ref=sent,
            dst_ref=tiles_own.at[row],
            send_sem=tile_send.at[d - 1],
            recv_sem=tile_recv.at[d - 1],
            device_id=peer(d),
            device_id_type=MESH,
        )

    def send_tiles(d, carry):
        tile_copy(d).start()
        return carry

    lax.fori_loop(1, n_rows, send_tiles, 0)
    rows = words[...].astype(F32)
    place = lax.broadcasted_iota(jnp.int32, (tokens, wide), 0)
    after = jnp.where(place < tokens - 1, pltpu.roll(rows, tokens - 1, 0), 0.0)
    before = jnp.where(place > 0, pltpu.roll(rows, 1, 0), 0.0)
    trigram[:, :wide] = after.astype(BF)
    trigram[:, wide : 2 * wide] = words[...]
    trigram[:, 2 * wide :] = before.astype(BF)
    spot = lax.broadcasted_iota(jnp.int32, (ATT, 1), 0)
    gain, bias = norms[0:1], norms[1:2]
    loads[0].wait()
    for start in range(0, tokens, ATT):
        r = slice(start, start + ATT)
        second = spot + start >= start_at
        kind = jnp.where(second, extra[tokens + 1 : tokens + 2], extra[tokens : tokens + 1])
        value = dot(trigram[r], conv[...]) + extra[r] + kind
        inputs_out[r] = value
        hidden = layer_norm(dot(value.astype(BF), entry_v[...]), gain[:, :breadth], bias[:, :breadth])
        hidden_v[r] = hidden
        low_v[r] = hidden.astype(BF)
    heads = half // THD
    pending = []
    for p in range(2):
        if p == 0:
            loads[1].wait()
        else:
            swaps[0].wait()
        first_head = core * heads if p == 0 else (1 - core) * heads
        attend_half(
            length,
            first_head,
            low_v,
            project_v.at[p],
            query_v,
            key_v,
            value_t,
            context_v.at[p],
            logs_out,
            sums_out,
            logs_v,
            scores_v,
            weight_v,
            logs_sem,
            pending,
        )
    loads[2].wait()
    swaps[1].wait()
    for c in loads[3:]:
        c.wait()
    blocks = tokens // ROWS_FF

    def hidden_units(p, low):
        for c in range(0, hidden_half, CUT_FF):
            before = dot(low, expand_v[p, :, c : c + CUT_FF])
            inner = 0.5 * before * (1.0 + lax.erf(before * math.sqrt(0.5)))
            inner_v[:, c : c + CUT_FF] = inner.astype(BF)

    def feed_own(n, carry):
        r = pl.ds(pl.multiple_of(n * ROWS_FF, ROWS_FF), ROWS_FF)
        mixed = dot(context_v[0, r], mixer_v[0]) + dot(context_v[1, r], mixer_v[1])
        first = layer_norm(
            mixed + hidden_v[r], gain[:, breadth : 2 * breadth], bias[:, breadth : 2 * breadth]
        )
        hidden_v[r] = first
        low_v[r] = first.astype(BF)
        hidden_units(0, low_v[r])
        hidden_v[r] += dot(inner_v[...], shrink_v[0])
        return carry

    def feed_mate(n, carry):
        r = pl.ds(pl.multiple_of(n * ROWS_FF, ROWS_FF), ROWS_FF)
        hidden_units(1, low_v[r])
        total = dot(inner_v[...], shrink_v[1]) + hidden_v[r]
        second = layer_norm(
            total, gain[:, 2 * breadth : 3 * breadth], bias[:, 2 * breadth : 3 * breadth]
        )
        raw = dot(second.astype(BF), leave_v[...]) + inputs_out[r]
        feature_out[r] = layer_norm(
            raw, gain[:, 3 * breadth : 3 * breadth + HID], bias[:, 3 * breadth : 3 * breadth + HID]
        )
        return carry

    lax.fori_loop(0, blocks, feed_own, 0)

    def take_tiles(d, carry):
        tile_copy(d).wait()
        return carry

    lax.fori_loop(1, n_rows, take_tiles, 0)
    over = pltpu.make_async_remote_copy(
        src_ref=tiles_own,
        dst_ref=tiles_mate,
        send_sem=pass_send,
        recv_sem=pass_recv,
        device_id=mate,
        device_id_type=MESH,
    )
    over.start()
    for c in swaps[2:]:
        c.wait()
    lax.fori_loop(0, blocks, feed_mate, 0)
    over.wait()
    for c in pending:
        c.wait()


def teacher(n_rows, bounds, micro_batch, owners, words, conv, extra, norms, weight, entry, project, mixer, expand, shrink, leave):
    tokens, wide = words.shape
    breadth = entry.shape[1]
    half = project.shape[2]
    hidden_half = expand.shape[1]
    V, D = pltpu.VMEM, pltpu.SemaphoreType.DMA
    slots, lines, lanes = weight.shape
    sent = (slots * lines // 32 + 1, 16, lanes)
    groups = -(-n_rows * slots // 128)
    gathered = jax.ShapeDtypeStruct((n_rows,) + sent, BF)
    return pl.pallas_call(
        teacher_kernel,
        out_shape=(
            jax.ShapeDtypeStruct((tokens, HID), F32),
            jax.ShapeDtypeStruct((tokens, HID), F32),
            jax.ShapeDtypeStruct((2 * half // THD, tokens, tokens), BF),
            jax.ShapeDtypeStruct((2 * half // THD, 1, tokens), F32),
            jax.ShapeDtypeStruct((5 + 2 * groups, 1, 128), jnp.int32),
            gathered,
            gathered,
        ),
        in_specs=[SMEM] * 3 + [VMEM] * 5 + [ANY] * 6,
        out_specs=(VMEM, VMEM, ANY, VMEM, VMEM, ANY, ANY),
        scratch_shapes=[
            V((tokens, 3 * wide), BF),
            V((tokens, breadth), F32),
            V((tokens, breadth), BF),
            V(entry.shape, BF),
            V((2,) + project.shape, BF),
            V((2,) + mixer.shape, BF),
            V((2,) + expand.shape, BF),
            V((2,) + shrink.shape, BF),
            V(leave.shape, BF),
            V((tokens, half), BF),
            V((tokens, half), BF),
            V((half, tokens), BF),
            V((2, tokens, half), BF),
            V((LOG_SLOTS, tokens, ATT), BF),
            V((2, tokens, ATT), F32),
            V((2, tokens, ATT), BF),
            V((ROWS_FF, hidden_half), BF),
            V(sent, BF),
            D((7,)),
            D((LOG_SLOTS,)),
            D((4,)),
            D((4,)),
            D((n_rows - 1,)),
            D((n_rows - 1,)),
            D,
            D,
        ],
        compiler_params=pltpu.CompilerParams(
            collective_id=1, has_side_effects=True, vmem_limit_bytes=62 << 20
        ),
        cost_estimate=pl.CostEstimate(
            flops=33_000_000_000, bytes_accessed=40 << 20, transcendentals=0
        ),
    )(bounds, micro_batch, owners, words, conv, extra, norms, weight, entry, project, mixer, expand, shrink, leave)


def three_parts(value):
    high = value.astype(BF).astype(F32)
    middle = (value - high).astype(BF).astype(F32)
    return high, middle, value - high - middle


def student_kernel(
    side,
    deep,
    where_at,
    bounds,
    micro_batch,
    inputs,
    feature,
    logs,
    sums,
    tiles_own,
    tiles_mate,
    small,
    summed_out,
    rest_out,
    lines_out,
    inputs_v,
    logs_v,
    wide_w,
    pair_w,
    mixer_w,
    expand_w,
    shrink_w,
    leave_w,
    low_v,
    narrow_v,
    first_v,
    query_v,
    key_m,
    value_m,
    key_t,
    value_t,
    context_t,
    contextlow_t,
    blocklow_v,
    hidden_v,
    sum_v,
    dsum_v,
    dcontext_v,
    dcontext_t,
    dvalue_v,
    dkey_v,
    dpair_v,
    scores_v,
    dweight_v,
    weight_v,
    dscores_v,
    g_leave,
    g_mixer,
    g_expand,
    g_shrink,
    small_v,
    tiles_v,
    pool,
    pair_in,
    first_in,
    second,
    second_in,
    third,
    third_in,
    half_own,
    half_in,
    rest_v,
    rest_in,
    rest_sum,
    rest_part,
    rest_all,
    lines_v,
    in_sem,
    sem,
    pair_send,
    pair_recv,
    first_send,
    first_recv,
    second_send,
    second_recv,
    third_send,
    third_recv,
    half_send,
    half_recv,
    swap_send,
    swap_recv,
    part_send,
    part_recv,
    all_send,
    all_recv,
    over_send,
    over_recv,
):
    tokens = inputs.shape[0]
    breadth = small.shape[1] - HID
    breadth = breadth // (2 + NFFN)
    row, core = lax.axis_index("rows"), lax.axis_index("heads")
    n_rows = side * side * deep
    mate = (row, 1 - core)
    barrier = pltpu.get_barrier_semaphore()
    pl.semaphore_signal(barrier, inc=1, device_id=mate, device_id_type=MESH)

    def greet(d, carry):
        peer = (lax.rem(row + d, n_rows), core)
        pl.semaphore_signal(barrier, inc=1, device_id=peer, device_id_type=MESH)
        return carry

    lax.fori_loop(1, n_rows, greet, 0)
    n_blocks = tiles_own.shape[-3]
    loads = [
        (tiles_own, pool.at[:, :, :, pl.ds(0, n_blocks)]),
        (tiles_mate, pool.at[:, :, :, pl.ds(n_blocks, n_blocks)]),
        (inputs, inputs_v),
        (feature.at[:, pl.ds(0, ATT)], dweight_v.at[0]),
        (feature.at[:, pl.ds(ATT, ATT)], dweight_v.at[1]),
    ]
    loads = [pltpu.make_async_copy(p, q, in_sem.at[n]) for n, (p, q) in enumerate(loads)]
    for c in loads:
        c.start()

    def logs_copy(n):
        return pltpu.make_async_copy(logs.at[:, :, pl.ds(n * ATT, ATT)], logs_v.at[n % 2], sem.at[n % 2])

    for n in range(2):
        logs_copy(n).start()
    length, batch = bounds[core, 1], micro_batch[core]
    slots = summed_out.shape[0]
    lines = breadth // 2
    blocks = lines // 16
    for ref in (rest_v, g_leave, g_mixer, g_expand, g_shrink, dvalue_v, dkey_v, small_v):
        ref[...] = jnp.zeros_like(ref)
    plane = side * side

    def of_row(n):
        return n // plane, n // side % side, n % side

    loads[0].wait()
    loads[1].wait()

    def add_digits(n, total):
        zz, yy, xx = of_row(n)
        return total + pool[zz, yy, xx, n_blocks - 1].astype(F32)

    digits = lax.fori_loop(0, n_rows, add_digits, jnp.zeros((16, breadth), F32))
    digits = digits[0:1]
    at_lane = lax.broadcasted_iota(jnp.int32, digits.shape, 1)
    digits = jnp.where(
        at_lane == 2 * batch,
        digits * COUNT_BASE,
        jnp.where(at_lane == 2 * batch + 1, digits, 0.0),
    )
    inverse = 1.0 / jnp.sum(digits, 1, keepdims=True)
    nin = HID // breadth
    nff = SFF // breadth

    def at(j):
        return slice(j * breadth, (j + 1) * breadth)

    at_pair, at_mixer, at_ff = 2 * nin, 2 * nin + 2, 2 * nin + 3
    at_shrink = at_ff + NFFN * nff
    at_leave = at_shrink + NFFN * nff
    def load(i, ref, row, col):
        zz, yy, xx = where_at[0, 0, i], where_at[1, 0, i], where_at[2, 0, i]
        for first_line, there in ((core * lines, where_at[3, 0, i]), ((1 - core) * lines, where_at[4, 0, i])):
            half = pool[zz, yy, xx, pl.ds(there, blocks)].reshape(lines, breadth)
            ref[pl.ds(pl.multiple_of(row * breadth + first_line, lines), lines), at(col)] = half

    for j in range(nin):
        load(j, wide_w, j, 0)
        load(nin + j, wide_w, j, 1)
        load(at_leave + j, leave_w, 0, j)
    load(at_pair, pair_w, 0, 0)
    load(at_pair + 1, pair_w, 0, 1)
    load(at_mixer, mixer_w, 0, 0)
    for b in range(NFFN):
        for j in range(nff):
            load(at_ff + b * nff + j, expand_w.at[b], 0, j)
            load(at_shrink + b * nff + j, shrink_w.at[b], j, 0)

    def gain(n):
        return small[0:1, at(n)]

    def bias(n):
        return small[1:2, at(n)]

    tail = (2 + NFFN) * breadth
    gain_out, bias_out = small[0:1, tail:], small[1:2, tail:]
    lane = lax.broadcasted_iota(jnp.int32, (1, breadth), 1)
    of_head = [(lane // SHD) == h for h in range(SHEADS)]
    loads[2].wait()
    for start in range(0, tokens, ROWS_FF):
        r = slice(start, start + ROWS_FF)
        low = inputs_v[r].astype(BF)
        low_v[r] = low
        both = dot(low, wide_w[...])
        narrow, value = both[:, :breadth], both[:, breadth:]
        narrow_v[r] = narrow
        first = narrow * gain(0) + bias(0)
        first_v[r] = first
        pair = dot(first.astype(BF), pair_w[...])
        query, key = pair[:, :breadth], pair[:, breadth:]
        query_v[r, :breadth] = query.astype(BF)
        place = lax.broadcasted_iota(jnp.int32, (ROWS_FF, 1), 0) + start
        mask = jnp.where(place < length, 0.0, MASKED_SCORE)
        for h in range(SHEADS):
            key_m[h, r, :breadth] = jnp.where(of_head[h], key, 0.0).astype(BF)
            value_m[h, r, :breadth] = jnp.where(of_head[h], value, 0.0).astype(BF)
            of_part = (lane >= 1 + 3 * h) & (lane < 4 + 3 * h)
            less = jnp.where(of_part, -1.0, 0.0)
            key_m[h, r, breadth:] = jnp.where(lane == 0, mask, less).astype(BF)
            value_m[h, r, breadth:] = jnp.broadcast_to(less, (ROWS_FF, breadth)).astype(BF)
        query_v[r, breadth:] = jnp.broadcast_to(jnp.where(lane == 0, 1.0, 0.0), (ROWS_FF, breadth)).astype(BF)
        key_t[:, r] = key.T.astype(BF)
        value_t[:, r] = value.T.astype(BF)
    scale = SHD**-0.5
    scale2 = scale * LOG2E

    def extra_columns(mark, values):
        rows = [jnp.full((1, ATT), mark, F32)]
        for v in values:
            rows.extend(three_parts(v))
        rows.append(jnp.zeros((breadth - len(rows), ATT), F32))
        return jnp.concatenate(rows, 0).T.astype(BF)

    def forward(n, carry):
        r = pl.ds(pl.multiple_of(n * ATT, ATT), ATT)
        query = query_v[r]
        shifts, parts = [], []
        scores_v[0] = dot_nt(key_m[0], query)
        for h in range(SHEADS):
            if h + 1 < SHEADS:
                scores_v[(h + 1) % 2] = dot_nt(key_m[h + 1], query)
            scores, weight = scores_v.at[h % 2], weight_v.at[h % 2]
            top = column_max(scores)
            part = 0.0
            for c in split_rows(scores):
                piece = jnp.exp2((scores[c] - top) * scale2)
                weight[c] = piece.astype(BF)
                part = part + piece
            total = jnp.sum(part, 0, keepdims=True)
            shifts.append(top + jnp.log2(total) * (1.0 / scale2))
            parts.append(dot(value_t[h * SHD : (h + 1) * SHD], weight[...]) * (1.0 / total))
        mixed = jnp.concatenate(parts, 0)
        context_t[:, r] = mixed
        contextlow_t[:, r] = mixed.astype(BF)
        query_v[r, breadth:] = extra_columns(1.0, shifts)
        return carry

    lax.fori_loop(0, tokens // ATT, forward, 0)

    def row_sums(n, d, value):
        small_v[0:1, at(n)] += jnp.sum(d * value, 0, keepdims=True)
        small_v[1:2, at(n)] += jnp.sum(d, 0, keepdims=True)

    def feed(n, loss):
        r = pl.ds(pl.multiple_of(n * ROWS_FF, ROWS_FF), ROWS_FF)
        place = lax.broadcasted_iota(jnp.int32, (ROWS_FF, 1), 0) + n * ROWS_FF
        weight = jnp.where(place < length, inverse, 0.0)
        context = context_t[:, r].T.astype(BF)
        mixed_sum = dot(context, mixer_w[...]) + first_v[r]
        current = mixed_sum * gain(1) + bias(1)
        for b in range(NFFN):
            low = current.astype(BF)
            blocklow_v[b] = low
            hidden = jnp.maximum(dot(low, expand_w[b]), 0.0).astype(BF)
            hidden_v[b] = hidden
            total = dot(hidden, shrink_w[b]) + current
            sum_v[b] = total
            current = total * gain(2 + b) + bias(2 + b)
        joined = dot(current.astype(BF), leave_w[...]) + inputs_v[r]
        differ = joined * gain_out + bias_out - jnp.concatenate([dweight_v[0, r], dweight_v[1, r]], 1)
        loss = loss + jnp.sum(weight * jnp.mean(differ * differ, -1, keepdims=True), 0, keepdims=True)
        outer = differ * (weight * (2.0 / HID))
        small_v[0:1, tail:] += jnp.sum(outer * joined, 0, keepdims=True)
        small_v[1:2, tail:] += jnp.sum(outer, 0, keepdims=True)
        back = (outer * gain_out).astype(BF)
        g_leave[...] += dot(current.T.astype(BF), back)
        d = dot_nt(back, leave_w[...])
        for b in reversed(range(NFFN)):
            row_sums(2 + b, d, sum_v[b])
            d_sum = d * gain(2 + b)
            hidden = hidden_v[b]
            g_shrink[b] += dot(d_sum.T.astype(BF), hidden)
            d_hidden = dot_nt(d_sum.astype(BF), shrink_w[b])
            d_before = jnp.where(hidden > 0, d_hidden, 0.0).astype(BF)
            g_expand[b] += dot(blocklow_v[b].T, d_before)
            d = d_sum + dot_nt(d_before, expand_w[b])
        row_sums(1, d, mixed_sum)
        d_sum = d * gain(1)
        dsum_v[r] = d_sum
        d_mixed = d_sum.astype(BF)
        g_mixer[...] += dot(contextlow_t[:, r], d_mixed)
        d_context = dot_nt(d_mixed, mixer_w[...])
        dcontext_v[r, :breadth] = d_context.astype(BF)
        dcontext_t[:, r] = d_context.astype(BF).astype(F32).T
        return loss

    for c in loads[3:]:
        c.wait()
    loss = lax.fori_loop(0, tokens // ROWS_FF, feed, jnp.zeros((1, 1), F32))
    n_rest = at_mixer
    tiles_v[0] = g_mixer[...].astype(BF)
    for j in range(nin):
        tiles_v[at_leave - n_rest + j] = g_leave[:, at(j)].astype(BF)
    for b in range(NFFN):
        for j in range(nff):
            tiles_v[at_ff - n_rest + b * nff + j] = g_expand[b, :, at(j)].astype(BF)
            tiles_v[at_shrink - n_rest + b * nff + j] = g_shrink[b, :, at(j)].T.astype(BF)
    nothing = tiles_v.shape[0] - 1
    tiles_v[nothing] = jnp.zeros((breadth, breadth), BF)
    z, y, x = row // plane, (row // side) % side, row % side
    mine = pl.multiple_of(core * lines, lines)
    theirs = pl.multiple_of((1 - core) * lines, lines)
    my_half, their_half = core * slots * blocks, (1 - core) * slots * blocks
    straight = core == 0
    a, b_ = jnp.where(straight, x, y), jnp.where(straight, y, x)
    mate_a = b_

    def lay(n, carry):
        per = where_at.shape[2]
        which = where_at[6 + 2 * (n // per), 0, n % per]
        zz, yy, xx = of_row(n // slots)
        tile = tiles_v[which].reshape(2 * blocks, 16, breadth)
        pool[zz, yy, xx, pl.ds(n % slots * blocks, blocks)] = tile[:blocks]
        pool[zz, yy, xx, pl.ds((slots + n % slots) * blocks, blocks)] = tile[blocks:]
        return carry

    lax.fori_loop(0, n_rows * slots, lay, 0)
    pl.semaphore_wait(barrier, n_rows)

    def row_at(xx, yy, zz):
        return zz * plane + yy * side + xx

    def along_a(aa):
        return (jnp.where(straight, row_at(aa, y, z), row_at(x, aa, z)), core)

    def along_b(bb):
        return (jnp.where(straight, row_at(x, bb, z), row_at(bb, y, z)), core)

    def along_z(zz):
        return (row_at(x, y, zz), core)

    def remote(src, dst, send, recv, peer):
        return pltpu.make_async_remote_copy(
            src_ref=src,
            dst_ref=dst,
            send_sem=send,
            recv_sem=recv,
            device_id=peer,
            device_id_type=MESH,
        )

    order = list(range(1, side)) + [0]
    for d in order:
        piece = lax.rem(mate_a + d, side)
        half = pl.ds(their_half, slots * blocks)
        by_y = remote(pool.at[:, piece, :, half], pair_in.at[d], pair_send.at[d], pair_recv.at[d], mate)
        by_x = remote(pool.at[:, :, piece, half], pair_in.at[d], pair_send.at[d], pair_recv.at[d], mate)

        @pl.when(straight)
        def _():
            by_y.start()

        @pl.when(jnp.logical_not(straight))
        def _():
            by_x.start()

    def pair_copy(d):
        return remote(pool.at[:, 0, :, pl.ds(0, slots * blocks)], pair_in.at[d], pair_send.at[d], pair_recv.at[d], mate)

    first_copies, second_copies, third_copies = [], [], []

    def add_pair():
        for d in order:
            pair_copy(d).wait_recv()
            aa = lax.rem(a + d, side)

            def add(i, carry):
                zz, bb = i // side, i % side
                xx, yy = jnp.where(straight, aa, bb), jnp.where(straight, bb, aa)
                own = pool[zz, yy, xx, pl.ds(my_half, slots * blocks)].astype(F32)
                pair_in[d, zz, bb] = (own + pair_in[d, zz, bb].astype(F32)).astype(BF)
                return carry

            lax.fori_loop(0, deep * side, add, 0)
            if d:
                c = remote(pair_in.at[d], first_in.at[d - 1], first_send.at[d - 1], first_recv.at[d - 1], along_a(aa))
                c.start()
                first_copies.append(c)

    def add_first():
        for c in first_copies:
            c.wait_recv()
        for d in order:
            bb = lax.rem(b_ + d, side)

            def add(zz, carry):
                s = pair_in[0, zz, bb].astype(F32)
                for j in range(side - 1):
                    s = s + first_in[j, zz, bb].astype(F32)
                second[d, zz] = s.astype(BF)
                return carry

            lax.fori_loop(0, deep, add, 0)
            if d:
                c = remote(second.at[d], second_in.at[d - 1], second_send.at[d - 1], second_recv.at[d - 1], along_b(bb))
                c.start()
                second_copies.append(c)

    def add_second():
        for c in second_copies:
            c.wait_recv()
        for d in list(range(1, deep)) + [0]:
            zz = lax.rem(z + d, deep)
            s = second[0, zz].astype(F32)
            for j in range(side - 1):
                s = s + second_in[j, zz].astype(F32)
            if d:
                third[d - 1] = s.astype(BF)
                c = remote(third.at[d - 1], third_in.at[d - 1], third_send.at[d - 1], third_recv.at[d - 1], along_z(zz))
                c.start()
                third_copies.append(c)
            else:
                half_own[...] = s.reshape(half_own.shape)

    def add_third():
        for c in third_copies:
            c.wait_recv()
        s = half_own[...]
        for j in range(deep - 1):
            s = s + third_in[j].astype(F32).reshape(half_own.shape)
        half_own[...] = s
        half_copy.start()

    half_copy = remote(half_own, half_in, half_send, half_recv, mate)
    stages = [add_pair, add_first, add_second]

    log_share = jnp.log2(inverse * (1.0 / SHEADS))

    def backward(n, loss):
        r = slice(n * ATT, (n + 1) * ATT)
        place = lax.broadcasted_iota(jnp.int32, (1, ATT), 1) + n * ATT
        inside = place < length
        share = jnp.where(inside, inverse * (1.0 / SHEADS), 0.0)
        share2 = jnp.where(inside, log_share, MASKED_SCORE)
        less = []
        for h in range(SHEADS):
            heads = slice(h * SHD, (h + 1) * SHD)
            along = jnp.sum(context_t[heads, r] * dcontext_t[heads, r], 0, keepdims=True)
            less.append(along - share * sums[h, :, r])
        dcontext_v[r, breadth:] = extra_columns(0.0, less)
        query, d_context = query_v[r], dcontext_v[r]
        logs_copy(n).wait()
        here = logs_v.at[n % 2]

        def products(h):
            scores_v[h % 2] = dot_nt(key_m[h], query)
            dweight_v[h % 2] = dot_nt(value_m[h], d_context)

        products(0)
        parts = []
        gap = 0.0
        for h in range(SHEADS):
            if h + 1 < SHEADS:
                products(h + 1)
            scores, dweight = scores_v.at[h % 2], dweight_v.at[h % 2]
            weight, dscores = weight_v.at[h % 2], dscores_v.at[h % 2]
            for c in split_rows(scores):
                score = scores[c]
                piece = jnp.exp2(score * scale2)
                weight[c] = piece.astype(BF)
                target_log = here[h, c].astype(F32)
                target = jnp.exp2(target_log * LOG2E + share2)
                gap = gap + target * (target_log - score * scale)
                dscores[c] = (piece * dweight[c] - target).astype(BF)
            none = jnp.zeros((ATT, breadth), BF)
            dvalue_v[...] += dot(weight[...], jnp.where(of_head[h], d_context[:, :breadth], none))
            dkey_v[...] += dot(dscores[...], jnp.where(of_head[h], query[:, :breadth], none))
            parts.append(dot(key_t[h * SHD : (h + 1) * SHD], dscores[...]))
        dpair_v[r, at(0)] = (jnp.concatenate(parts, 0) * scale).T.astype(BF)
        if n + 2 < tokens // ATT:
            logs_copy(n + 2).start()
        return loss + jnp.sum(jnp.sum(gap, 0, keepdims=True), 1, keepdims=True)

    for n in range(tokens // ATT):
        loss = backward(n, loss)
        if n < len(stages):
            stages[n]()
    dpair_v[:, at(1)] = (dkey_v[...] * scale).astype(BF)
    d_pair = dpair_v[...]
    d_first = dsum_v[...] + dot_nt(d_pair, pair_w[...])
    row_sums(0, d_first, narrow_v[...])
    g_pair = dot(first_v[...].T.astype(BF), d_pair)
    wide_t = jnp.concatenate([(d_first * gain(0)).T.astype(BF), dvalue_v[...].T.astype(BF)], 0)
    g_wide = dot(wide_t, low_v[...])
    n_lines = small.shape[1] // breadth
    lines_v[...] = jnp.zeros_like(lines_v)
    for j in range(n_lines):
        lines_v[j : j + 1] = small_v[0:1, at(j)]
        lines_v[n_lines + j : n_lines + j + 1] = small_v[1:2, at(j)]
    lines_v[2 * n_lines : 2 * n_lines + 1, 0:1] = loss
    add_third()
    summed = half_own[...]
    lines_v[2 * n_lines + 1 : 2 * n_lines + 2] = jnp.sum(summed * summed, 0, keepdims=True)
    groups = lines_v.shape[0] // 8
    top = 16 * groups
    each = n_rest // 2

    def two_parts(value):
        high = value.astype(BF)
        return high, (value - high.astype(F32)).astype(BF)

    for g in range(groups):
        high, rest = two_parts(lines_v[8 * g : 8 * g + 8])
        rest_v[0, 16 * g : 16 * g + 8] = high
        rest_v[0, 16 * g + 8 : 16 * g + 16] = rest

    def keep(n, value):
        line = top + (n % each) * breadth
        rest_v[n // each, line : line + breadth] = value.astype(BF)

    for j in range(nin):
        keep(j, g_wide[:breadth, at(j)].T)
        keep(nin + j, g_wide[breadth:, at(j)].T)
    keep(at_pair, g_pair[:, at(0)])
    keep(at_pair + 1, g_pair[:, at(1)])
    swap = remote(rest_v.at[1 - core], rest_in, swap_send, swap_recv, mate)
    swap.start()
    swap.wait()
    rest_sum[...] = (rest_v[core].astype(F32) + rest_in[...].astype(F32)).astype(BF)
    for g in range(groups):
        high_at, rest_at = slice(16 * g, 16 * g + 8), slice(16 * g + 8, 16 * g + 16)
        value = rest_v[core, high_at].astype(F32) + rest_v[core, rest_at].astype(F32)
        value = value + rest_in[high_at].astype(F32) + rest_in[rest_at].astype(F32)
        rest_sum[high_at], rest_sum[rest_at] = two_parts(value)
    chunk = rest_part.shape[1]

    def lines_of(n):
        return pl.ds(pl.multiple_of(n * chunk, chunk), chunk)

    def part_copy(d):
        to = lax.rem(row + d, n_rows)
        return remote(rest_sum.at[lines_of(to)], rest_part.at[d - 1], part_send.at[d - 1], part_recv.at[d - 1], (to, core))

    def all_copy(d):
        here = rest_all.at[core, lines_of(row)]
        return remote(here, here, all_send.at[d - 1], all_recv.at[d - 1], (lax.rem(row + d, n_rows), core))

    def each_peer(act):
        def one(d, carry):
            act(d)
            return carry

        lax.fori_loop(1, n_rows, one, 0)

    each_peer(lambda d: part_copy(d).start())
    each_peer(lambda d: part_copy(d).wait())
    total = lax.fori_loop(
        0, n_rows - 1, lambda d, t: t + rest_part[d].astype(F32), rest_sum[lines_of(row)].astype(F32)
    )
    high_of = []
    for g in range(chunk // 16):
        piece = total[16 * g : 16 * g + 16]
        high, rest = two_parts(piece[:8] + piece[8:])
        split = jnp.concatenate([high.astype(F32), rest.astype(F32)], 0)
        high_of.append(jnp.where(row * (chunk // 16) + g < groups, split, piece))
    rest_all[core, lines_of(row)] = jnp.where(core == 0, jnp.concatenate(high_of, 0), total).astype(BF)
    each_peer(lambda d: all_copy(d).start())
    half_copy.wait()
    for k in range(slots):
        summed_out[k, pl.ds(mine, lines)] = half_own[k * lines : (k + 1) * lines]
        summed_out[k, pl.ds(theirs, lines)] = half_in[k * lines : (k + 1) * lines]
    each_peer(lambda d: all_copy(d).wait())
    over = remote(rest_all.at[core], rest_all.at[core], over_send, over_recv, mate)
    over.start()
    for d in order:
        pair_copy(d).wait_send()
    for c in first_copies + second_copies + third_copies:
        c.wait_send()
    over.wait()
    squares = jnp.zeros((1, breadth), F32)
    for n in range(n_rest):
        line = top + (n % each) * breadth
        rest_out[n] = rest_all[n // each, line : line + breadth]
        tile = rest_out[n].astype(F32)
        squares = squares + jnp.sum(tile * tile, 0, keepdims=True)
    for g in range(groups):
        high = rest_all[0, 16 * g : 16 * g + 8].astype(F32)
        lines_out[8 * g : 8 * g + 8] = high + rest_all[0, 16 * g + 8 : 16 * g + 16].astype(F32)
    lines_out[2 * n_lines + 2 : 2 * n_lines + 3] = squares


def student(where_at, bounds, micro_batch, inputs, feature, logs, sums, tiles_own, tiles_mate, small, slots):
    tokens = inputs.shape[0]
    n_rows, w = tiles_own.shape[0], tiles_own.shape[-1]
    deep = 4
    side = math.isqrt(n_rows // deep)
    assert side * side * deep == n_rows
    n_lines = 8 * -(-(2 * small.shape[1] // w + 3) // 8)
    n_rest = 2 * HID // w + 2
    n_tiles = 1 + 2 * NFFN * (SFF // w) + HID // w
    half = w // 2
    in_half = 2 * n_lines + (HID // w + 1) * w
    chunk = 16 * -(-in_half // (16 * n_rows))
    s1, d1 = side - 1, deep - 1
    gathered = (deep, side, side) + tiles_own.shape[1:]
    tiles_own, tiles_mate = tiles_own.reshape(gathered), tiles_mate.reshape(gathered)
    blocks = slots * half // 16
    D = pltpu.SemaphoreType.DMA

    def low(*shape):
        return pltpu.VMEM(shape, BF)

    def full(*shape):
        return pltpu.VMEM(shape, F32)

    return pl.pallas_call(
        functools.partial(student_kernel, side, deep),
        out_shape=(
            jax.ShapeDtypeStruct((slots, w, w), F32),
            jax.ShapeDtypeStruct((n_rest, w, w), BF),
            jax.ShapeDtypeStruct((n_lines, w), F32),
        ),
        in_specs=[SMEM] * 3 + [ANY, ANY, ANY, VMEM, ANY, ANY, VMEM],
        out_specs=(VMEM, VMEM, VMEM),
        scratch_shapes=[
            full(tokens, HID),
            low(2, SHEADS, tokens, ATT),
            low(HID, 2 * w),
            low(w, 2 * w),
            low(w, w),
            low(NFFN, w, SFF),
            low(NFFN, SFF, w),
            low(w, HID),
            low(tokens, HID),
            full(tokens, w),
            full(tokens, w),
            low(tokens, 2 * w),
            low(SHEADS, tokens, 2 * w),
            low(SHEADS, tokens, 2 * w),
            low(w, tokens),
            low(w, tokens),
            full(w, tokens),
            low(w, tokens),
            low(NFFN, ROWS_FF, w),
            low(NFFN, ROWS_FF, SFF),
            full(NFFN, ROWS_FF, w),
            full(tokens, w),
            low(tokens, 2 * w),
            full(w, tokens),
            full(tokens, w),
            full(tokens, w),
            low(tokens, 2 * w),
            full(2, tokens, ATT),
            full(2, tokens, ATT),
            low(2, tokens, ATT),
            low(2, tokens, ATT),
            full(w, HID),
            full(w, w),
            full(NFFN, w, SFF),
            full(NFFN, w, SFF),
            full(8, small.shape[1]),
            low(n_tiles + 1, w, w),
            low(deep, side, side, 2 * tiles_own.shape[-3], 16, w),
            low(side, deep, side, blocks, 16, w),
            low(s1, deep, side, blocks, 16, w),
            low(side, deep, blocks, 16, w),
            low(s1, deep, blocks, 16, w),
            low(d1, blocks, 16, w),
            low(d1, blocks, 16, w),
            full(slots * half, w),
            full(slots * half, w),
            low(2, chunk * n_rows, w),
            low(chunk * n_rows, w),
            low(chunk * n_rows, w),
            low(n_rows - 1, chunk, w),
            low(2, chunk * n_rows, w),
            full(n_lines, w),
            D((5,)),
            D((2,)),
            D((side,)),
            D((side,)),
            D((s1,)),
            D((s1,)),
            D((s1,)),
            D((s1,)),
            D((d1,)),
            D((d1,)),
            D,
            D,
            D,
            D,
            D((n_rows - 1,)),
            D((n_rows - 1,)),
            D((n_rows - 1,)),
            D((n_rows - 1,)),
            D,
            D,
        ],
        compiler_params=pltpu.CompilerParams(
            collective_id=0, has_side_effects=True, vmem_limit_bytes=63 << 20
        ),
        cost_estimate=pl.CostEstimate(
            flops=15_000_000_000, bytes_accessed=16 << 20, transcendentals=0
        ),
    )(where_at, bounds, micro_batch, inputs, feature, logs, sums, tiles_own, tiles_mate, small)


def update_kernel(
    n_tiles, where_at, step, own, summed, rest, lines, weight_in, first_in, second_in, small, small_first, small_second,
    loss_out, norm_out, tiles_out, first_out, second_out, small_out, small_first_out, small_second_out, small_grad_out,
    small_v, weight, first, second, sem,
):
    pairs = ((weight_in, weight), (first_in, first), (second_in, second))
    loads = [pltpu.make_async_copy(a, b, sem.at[n]) for n, (a, b) in enumerate(pairs)]
    for c in loads:
        c.start()
    breadth = summed.shape[2]
    n_lines = small.shape[1] // breadth
    steps = step[0]
    first_fix = 1.0 - lax.fori_loop(0, steps, lambda i, p: p * BETA_FIRST, jnp.float32(1.0))
    second_fix = 1.0 - lax.fori_loop(0, steps, lambda i, p: p * BETA_SECOND, jnp.float32(1.0))

    def adam(w, m, v, g, decay):
        m = BETA_FIRST * m + (1.0 - BETA_FIRST) * g
        v = BETA_SECOND * v + (1.0 - BETA_SECOND) * g * g
        change = m / first_fix / (jnp.sqrt(v / second_fix) + ADAM_EPSILON) + decay * w
        return w - LEARN_RATE * change, m, v

    line = lambda n: lines[n : n + 1]
    squares = line(2 * n_lines + 1) + line(2 * n_lines + 2)
    for n in range(2 * n_lines):
        squares = squares + line(n) * line(n)
    norm = jnp.sqrt(jnp.sum(squares, 1, keepdims=True))
    norm_out[...] = norm
    loss_out[...] = line(2 * n_lines)[:, 0:1]
    factor = CLIP_NORM / jnp.maximum(norm, CLIP_NORM)
    for n in range(n_lines):
        cols = slice(n * breadth, (n + 1) * breadth)
        small_v[0:1, cols] = line(n)
        small_v[1:2, cols] = line(n_lines + n)
    small_grad = small_v[0:2] * factor
    small_grad_out[...] = small_grad
    w, m, v = adam(small[...], small_first[...], small_second[...], small_grad, 0.0)
    small_out[...] = w
    small_first_out[...] = m
    small_second_out[...] = v

    slots, n_rest = summed.shape[0], rest.shape[0]
    for c in loads:
        c.wait()
    for s in range(summed.shape[0]):
        at = own[0] * slots + s
        which = where_at[5 + 2 * (at // 128), 0, at % 128]
        keep = which < n_tiles
        other = rest[jnp.minimum(which, n_rest - 1)].astype(F32)
        total = summed[s] + jnp.where(which < n_rest, other, 0.0)
        w, m, v = adam(weight[s], first[s], second[s], total * factor, WEIGHT_DECAY)
        tiles_out[s] = jnp.where(keep, w, 0.0)
        first_out[s] = jnp.where(keep, m, 0.0)
        second_out[s] = jnp.where(keep, v, 0.0)


def update(n_tiles, where_at, step, own, summed, rest, lines, weight, first, second, small, small_first, small_second):
    one = jax.ShapeDtypeStruct((1, 1), F32)
    tile = jax.ShapeDtypeStruct(weight.shape, F32)
    row = jax.ShapeDtypeStruct(small.shape, F32)
    return pl.pallas_call(
        functools.partial(update_kernel, n_tiles),
        out_shape=(one, one, tile, tile, tile, row, row, row, row),
        in_specs=[SMEM] * 3 + [VMEM] * 3 + [HBM] * 3 + [VMEM] * 3,
        out_specs=(VMEM,) * 9,
        scratch_shapes=[pltpu.VMEM((8, small.shape[1]), F32)]
        + [pltpu.VMEM(weight.shape, F32)] * 3
        + [pltpu.SemaphoreType.DMA((3,))],
        compiler_params=pltpu.CompilerParams(vmem_limit_bytes=63 << 20),
        cost_estimate=pl.CostEstimate(flops=2_000_000, bytes_accessed=2 << 20, transcendentals=0),
    )(where_at, step, own, summed, rest, lines, weight, first, second, small, small_first, small_second)


def on_device(
    token_ids,
    bounds,
    micro_batch,
    owners,
    step_count,
    word_table,
    conv_weight,
    embed_extra,
    teacher_entry,
    teacher_project,
    teacher_mixer,
    teacher_expand,
    teacher_shrink,
    teacher_leave,
    teacher_norms,
    tile_weight,
    tile_first,
    tile_second,
    small_weight,
    small_first,
    small_second,
):
    core = lax.axis_index("heads")
    n_rows = lax.axis_size("rows")
    assert token_ids.shape[0] == lax.axis_size("heads")
    row_ids = lax.dynamic_index_in_dim(token_ids, core, 0, keepdims=False)
    words = word_table.at[row_ids].get(mode="promise_in_bounds")
    inputs, feature, logs, sums, where_at, tiles_own, tiles_mate = teacher(
        n_rows,
        bounds,
        micro_batch,
        owners,
        words,
        conv_weight,
        embed_extra,
        teacher_norms,
        tile_weight,
        teacher_entry,
        teacher_project.transpose(1, 0, 2),
        teacher_mixer,
        teacher_expand,
        teacher_shrink,
        teacher_leave,
    )
    summed, rest, lines = student(
        where_at,
        bounds,
        micro_batch,
        inputs,
        feature,
        logs,
        sums,
        tiles_own,
        tiles_mate,
        small_weight,
        tile_weight.shape[0],
    )
    own = lax.axis_index("rows")[None]
    loss, norm, *rest = update(
        owners.shape[0],
        where_at,
        step_count,
        own,
        summed,
        rest,
        lines,
        tile_weight,
        tile_first,
        tile_second,
        small_weight,
        small_first,
        small_second,
    )
    return (loss[0, 0], norm[0, 0], *rest)


def solution(mesh):
    placed = (
        P("rows", None),
        P("rows", None),
        P("rows"),
        P(),
        P(),
        P(),
        P(),
        P(),
        P(),
        P(None, None, "heads"),
        P("heads", None),
        P(None, "heads"),
        P("heads", None),
        P(),
        P(),
        P("rows", None, None),
        P("rows", None, None),
        P("rows", None, None),
        P(),
        P(),
        P(),
    )
    tiles = P("rows", None, None)
    return jax.shard_map(
        on_device,
        mesh=mesh,
        in_specs=placed,
        out_specs=(P(), P(), tiles, tiles, tiles, P(), P(), P(), P()),
        check_vma=False,
    )
```

```python
import functools
import math

import jax
import jax.numpy as jnp
from jax import lax
from jax.experimental import pallas as pl
from jax.experimental.pallas import tpu as pltpu
from jax.sharding import PartitionSpec as P

HID = 512
THD = 256
SHEADS = 4
SHD = 32
SFF = 512
NFFN = 4
NMB = 2
NORM_EPSILON = 1e-05
CLIP_NORM = 0.05
LEARN_RATE = 0.1
BETA_FIRST = 0.9
BETA_SECOND = 0.999
ADAM_EPSILON = 1e-08
WEIGHT_DECAY = 0.01
MASKED_SCORE = -1e30
LOG2E = math.log2(math.e)
COUNT_BASE = 64

ATT = 256
ROWS_FF = 512
CUT_FF = 512
LOG_SLOTS = 4
DEEP = 4

MESH = pl.DeviceIdType.MESH
BF, F32 = jnp.bfloat16, jnp.float32
VMEM = pl.BlockSpec(memory_space=pltpu.VMEM)
SMEM = pl.BlockSpec(memory_space=pltpu.SMEM)
HBM = pl.BlockSpec(memory_space=pltpu.HBM)
ANY = pl.BlockSpec(memory_space=pl.ANY)


def dot(left, right):
    return jnp.dot(left, right, preferred_element_type=F32)


def dot_nt(left, right):
    return lax.dot_general(left, right, (((1,), (1,)), ((), ())), preferred_element_type=F32)


def layer_norm(values, gain_row, bias_row):
    center = values - jnp.mean(values, -1, keepdims=True)
    spread = jnp.mean(center * center, -1, keepdims=True)
    return center * lax.rsqrt(spread + NORM_EPSILON) * gain_row + bias_row


def sum_over(ref, n):
    s = ref[0]
    for i in range(1, n):
        s = s + ref[i]
    return s


def split_rows(refs, rows=64):
    for start in range(0, refs.shape[-2], rows):
        yield slice(start, start + rows)


def column_max(ref):
    best = None
    for c in split_rows(ref):
        best = ref[c] if best is None else jnp.maximum(best, ref[c])
    return jnp.max(best, 0, keepdims=True)


def attend_half(
    length,
    first_head,
    low_v,
    project_v,
    query_v,
    key_v,
    value_t,
    context_v,
    logs_out,
    sums_out,
    logs_v,
    scores_v,
    weight_v,
    sem,
    pending,
):
    tokens = low_v.shape[0]
    width = project_v.shape[2]
    for start in range(0, tokens, ROWS_FF):
        rows = slice(start, start + ROWS_FF)
        low = low_v[rows]
        query_v[rows] = (dot(low, project_v[0]) * THD**-0.5).astype(BF)
        key_v[rows] = dot(low, project_v[1]).astype(BF)
        value_t[:, rows] = dot(low, project_v[2]).T.astype(BF)
    steps = [(h, q) for h in range(width // THD) for q in range(tokens // ATT)]
    least = tokens // 2

    def scores_of(i):
        h, q = steps[i]
        cols = slice(h * THD, (h + 1) * THD)
        query = query_v[q * ATT : (q + 1) * ATT, cols]
        scores_v[i % 2, :least] = dot_nt(key_v[:least, cols], query)
        valid = lax.broadcasted_iota(jnp.int32, (tokens - least, ATT), 0) + least < length
        scores_v[i % 2, least:] = jnp.where(valid, dot_nt(key_v[least:, cols], query), MASKED_SCORE)

    scores_of(0)
    for i, (h, q) in enumerate(steps):
        if len(pending) == LOG_SLOTS:
            pending.pop(0).wait()
        if i + 1 < len(steps):
            scores_of(i + 1)
        at = i % LOG_SLOTS
        scores, weight, logs = scores_v.at[i % 2], weight_v.at[i % 2], logs_v.at[at]
        top = column_max(scores)
        part = 0.0
        for c in split_rows(scores):
            piece = jnp.exp(scores[c] - top)
            weight[c] = piece.astype(BF)
            part = part + piece
        total = jnp.sum(part, 0, keepdims=True)
        shift = top + jnp.log(total)
        part = 0.0
        for c in split_rows(scores):
            piece = (scores[c] - shift).astype(BF)
            logs[c] = piece
            part = part + jnp.exp(piece.astype(F32))
        sums_out[first_head + h, :, q * ATT : (q + 1) * ATT] = jnp.sum(part, 0, keepdims=True)
        mixed = dot(value_t[h * THD : (h + 1) * THD], weight[...]) * (1.0 / total)
        context_v[q * ATT : (q + 1) * ATT, h * THD : (h + 1) * THD] = mixed.T.astype(BF)
        there = logs_out.at[first_head + h, :, pl.ds(q * ATT, ATT)]
        pending.append(pltpu.make_async_copy(logs, there, sem.at[at]))
        pending[-1].start()
    assert len(steps) % LOG_SLOTS == 0


def teacher_kernel(
    bounds,
    micro_batch,
    owners,
    words,
    conv,
    extra,
    norms,
    weight,
    entry,
    project,
    mixer,
    expand,
    shrink,
    leave,
    inputs_out,
    feature_out,
    logs_out,
    sums_out,
    where_out,
    tiles_own,
    tiles_mate,
    trigram,
    hidden_v,
    low_v,
    entry_v,
    project_v,
    mixer_v,
    expand_v,
    shrink_v,
    leave_v,
    query_v,
    key_v,
    value_t,
    context_v,
    logs_v,
    scores_v,
    weight_v,
    inner_v,
    sent,
    in_sem,
    logs_sem,
    swap_send,
    swap_recv,
    tile_send,
    tile_recv,
    pass_send,
    pass_recv,
):
    tokens, wide = words.shape
    breadth = entry.shape[1]
    half = project.shape[2]
    hidden_half = expand.shape[1]
    n_rows = tiles_own.shape[0]
    row, core = lax.axis_index("rows"), lax.axis_index("heads")
    mate = (row, 1 - core)
    start_at, length = bounds[core, 0], bounds[core, 1]
    slots, _, lanes = weight.shape
    lines = weight.shape[1] // 2
    blocks = lines // 16
    for n in range(slots):
        half_tile = weight[n, pl.ds(core * lines, lines)].astype(BF)
        sent[n * blocks : (n + 1) * blocks] = half_tile.reshape(blocks, 16, lanes)
    lane = lax.broadcasted_iota(jnp.int32, (16, lanes), 1)
    digits = jnp.zeros((16, lanes), F32)
    for m in range(NMB):
        held = jnp.int32(0)
        for n in range(micro_batch.shape[0]):
            held = held + jnp.where(micro_batch[n] == m, bounds[n, 1], 0)
        digits = jnp.where(lane == 2 * m, (held // COUNT_BASE).astype(F32), digits)
        digits = jnp.where(lane == 2 * m + 1, (held % COUNT_BASE).astype(F32), digits)
    sent[slots * blocks] = digits.astype(BF)
    n_tiles, n_rest = owners.shape[0], 2 * HID // lanes + 2
    side = math.isqrt(tiles_own.shape[0] // DEEP)
    bits = side.bit_length() - 1
    spot = lax.broadcasted_iota(jnp.int32, (1, where_out.shape[2]), 1)
    owner_of = jnp.zeros(spot.shape, jnp.int32)
    rank_of = jnp.zeros(spot.shape, jnp.int32)
    for i in range(n_tiles):
        owner_of = jnp.where(spot == i, owners[i], owner_of)
    for i in range(n_tiles):
        rank_of = rank_of + jnp.where((owner_of == owners[i]) & (spot > i), 1, 0)
    where_out[0] = lax.shift_right_logical(owner_of, 2 * bits)
    where_out[1] = lax.shift_right_logical(owner_of, bits) & (side - 1)
    where_out[2] = owner_of & (side - 1)
    where_out[3] = rank_of * blocks
    where_out[4] = rank_of * blocks + slots * blocks + 1
    for g in range(where_out.shape[0] // 2 - 2):
        spots = spot + g * where_out.shape[2]
        owner_here = lax.shift_right_logical(spots, slots.bit_length() - 1)
        rank_here = spots & (slots - 1)
        seen = jnp.zeros(spot.shape, jnp.int32)
        which = jnp.full(spot.shape, n_tiles, jnp.int32)
        for i in range(n_tiles):
            same = owner_here == owners[i]
            which = jnp.where(same & (seen == rank_here), i, which)
            seen = seen + jnp.where(same, 1, 0)
        where_out[5 + 2 * g] = which
        where_out[6 + 2 * g] = jnp.where(which >= n_rest, which - n_rest, n_tiles - n_rest)

    def peer(d):
        return (lax.rem(row + d, n_rows), core)

    local = [(entry, entry_v), (project, project_v.at[0]), (mixer, mixer_v.at[0])]
    local += [(expand, expand_v.at[0]), (shrink, shrink_v.at[0]), (leave, leave_v)]
    local += [(sent, tiles_own.at[row])]
    loads = [pltpu.make_async_copy(a, b, in_sem.at[n]) for n, (a, b) in enumerate(local)]
    for c in loads:
        c.start()
    barrier = pltpu.get_barrier_semaphore()
    pl.semaphore_signal(barrier, inc=1, device_id=mate, device_id_type=MESH)

    def greet(d, carry):
        pl.semaphore_signal(barrier, inc=1, device_id=peer(d), device_id_type=MESH)
        return carry

    lax.fori_loop(1, n_rows, greet, 0)
    pl.semaphore_wait(barrier, n_rows)
    swaps = []
    for n, (a, b) in enumerate(((project, project_v), (mixer, mixer_v), (expand, expand_v), (shrink, shrink_v))):
        swaps.append(
            pltpu.make_async_remote_copy(
                src_ref=a,
                dst_ref=b.at[1],
                send_sem=swap_send.at[n],
                recv_sem=swap_recv.at[n],
                device_id=mate,
                device_id_type=MESH,
            )
        )
        swaps[-1].start()

    def tile_copy(d):
        return pltpu.make_async_remote_copy(
            src_ref=sent,
            dst_ref=tiles_own.at[row],
            send_sem=tile_send.at[d - 1],
            recv_sem=tile_recv.at[d - 1],
            device_id=peer(d),
            device_id_type=MESH,
        )

    def send_tiles(d, carry):
        tile_copy(d).start()
        return carry

    lax.fori_loop(1, n_rows, send_tiles, 0)
    rows = words[...].astype(F32)
    place = lax.broadcasted_iota(jnp.int32, (tokens, wide), 0)
    after = jnp.where(place < tokens - 1, pltpu.roll(rows, tokens - 1, 0), 0.0)
    before = jnp.where(place > 0, pltpu.roll(rows, 1, 0), 0.0)
    trigram[:, :wide] = after.astype(BF)
    trigram[:, wide : 2 * wide] = words[...]
    trigram[:, 2 * wide :] = before.astype(BF)
    spot = lax.broadcasted_iota(jnp.int32, (ATT, 1), 0)
    gain, bias = norms[0:1], norms[1:2]
    loads[0].wait()
    for start in range(0, tokens, ATT):
        r = slice(start, start + ATT)
        second = spot + start >= start_at
        kind = jnp.where(second, extra[tokens + 1 : tokens + 2], extra[tokens : tokens + 1])
        value = dot(trigram[r], conv[...]) + extra[r] + kind
        inputs_out[r] = value
        hidden = layer_norm(dot(value.astype(BF), entry_v[...]), gain[:, :breadth], bias[:, :breadth])
        hidden_v[r] = hidden
        low_v[r] = hidden.astype(BF)
    heads = half // THD
    pending = []
    for p in range(2):
        if p == 0:
            loads[1].wait()
        else:
            swaps[0].wait()
        first_head = core * heads if p == 0 else (1 - core) * heads
        attend_half(
            length,
            first_head,
            low_v,
            project_v.at[p],
            query_v,
            key_v,
            value_t,
            context_v.at[p],
            logs_out,
            sums_out,
            logs_v,
            scores_v,
            weight_v,
            logs_sem,
            pending,
        )
    loads[2].wait()
    swaps[1].wait()
    for c in loads[3:]:
        c.wait()
    blocks = tokens // ROWS_FF

    def hidden_units(p, low):
        for c in range(0, hidden_half, CUT_FF):
            before = dot(low, expand_v[p, :, c : c + CUT_FF])
            inner = 0.5 * before * (1.0 + lax.erf(before * math.sqrt(0.5)))
            inner_v[:, c : c + CUT_FF] = inner.astype(BF)

    def feed_own(n, carry):
        r = pl.ds(pl.multiple_of(n * ROWS_FF, ROWS_FF), ROWS_FF)
        mixed = dot(context_v[0, r], mixer_v[0]) + dot(context_v[1, r], mixer_v[1])
        first = layer_norm(
            mixed + hidden_v[r], gain[:, breadth : 2 * breadth], bias[:, breadth : 2 * breadth]
        )
        hidden_v[r] = first
        low_v[r] = first.astype(BF)
        hidden_units(0, low_v[r])
        hidden_v[r] += dot(inner_v[...], shrink_v[0])
        return carry

    def feed_mate(n, carry):
        r = pl.ds(pl.multiple_of(n * ROWS_FF, ROWS_FF), ROWS_FF)
        hidden_units(1, low_v[r])
        total = dot(inner_v[...], shrink_v[1]) + hidden_v[r]
        second = layer_norm(
            total, gain[:, 2 * breadth : 3 * breadth], bias[:, 2 * breadth : 3 * breadth]
        )
        raw = dot(second.astype(BF), leave_v[...]) + inputs_out[r]
        feature_out[r] = layer_norm(
            raw, gain[:, 3 * breadth : 3 * breadth + HID], bias[:, 3 * breadth : 3 * breadth + HID]
        )
        return carry

    lax.fori_loop(0, blocks, feed_own, 0)

    def take_tiles(d, carry):
        tile_copy(d).wait()
        return carry

    lax.fori_loop(1, n_rows, take_tiles, 0)
    over = pltpu.make_async_remote_copy(
        src_ref=tiles_own,
        dst_ref=tiles_mate,
        send_sem=pass_send,
        recv_sem=pass_recv,
        device_id=mate,
        device_id_type=MESH,
    )
    over.start()
    for c in swaps[2:]:
        c.wait()
    lax.fori_loop(0, blocks, feed_mate, 0)
    over.wait()
    for c in pending:
        c.wait()


def teacher(n_rows, bounds, micro_batch, owners, words, conv, extra, norms, weight, entry, project, mixer, expand, shrink, leave):
    tokens, wide = words.shape
    breadth = entry.shape[1]
    half = project.shape[2]
    hidden_half = expand.shape[1]
    V, D = pltpu.VMEM, pltpu.SemaphoreType.DMA
    slots, lines, lanes = weight.shape
    sent = (slots * lines // 32 + 1, 16, lanes)
    groups = -(-n_rows * slots // 128)
    gathered = jax.ShapeDtypeStruct((n_rows,) + sent, BF)
    return pl.pallas_call(
        teacher_kernel,
        out_shape=(
            jax.ShapeDtypeStruct((tokens, HID), F32),
            jax.ShapeDtypeStruct((tokens, HID), F32),
            jax.ShapeDtypeStruct((2 * half // THD, tokens, tokens), BF),
            jax.ShapeDtypeStruct((2 * half // THD, 1, tokens), F32),
            jax.ShapeDtypeStruct((5 + 2 * groups, 1, 128), jnp.int32),
            gathered,
            gathered,
        ),
        in_specs=[SMEM] * 3 + [VMEM] * 5 + [ANY] * 6,
        out_specs=(VMEM, VMEM, ANY, VMEM, VMEM, ANY, ANY),
        scratch_shapes=[
            V((tokens, 3 * wide), BF),
            V((tokens, breadth), F32),
            V((tokens, breadth), BF),
            V(entry.shape, BF),
            V((2,) + project.shape, BF),
            V((2,) + mixer.shape, BF),
            V((2,) + expand.shape, BF),
            V((2,) + shrink.shape, BF),
            V(leave.shape, BF),
            V((tokens, half), BF),
            V((tokens, half), BF),
            V((half, tokens), BF),
            V((2, tokens, half), BF),
            V((LOG_SLOTS, tokens, ATT), BF),
            V((2, tokens, ATT), F32),
            V((2, tokens, ATT), BF),
            V((ROWS_FF, hidden_half), BF),
            V(sent, BF),
            D((7,)),
            D((LOG_SLOTS,)),
            D((4,)),
            D((4,)),
            D((n_rows - 1,)),
            D((n_rows - 1,)),
            D,
            D,
        ],
        compiler_params=pltpu.CompilerParams(
            collective_id=1, has_side_effects=True, vmem_limit_bytes=62 << 20
        ),
        cost_estimate=pl.CostEstimate(
            flops=33_000_000_000, bytes_accessed=40 << 20, transcendentals=0
        ),
    )(bounds, micro_batch, owners, words, conv, extra, norms, weight, entry, project, mixer, expand, shrink, leave)


def three_parts(value):
    high = value.astype(BF).astype(F32)
    middle = (value - high).astype(BF).astype(F32)
    return high, middle, value - high - middle


def student_kernel(
    side,
    deep,
    where_at,
    bounds,
    micro_batch,
    inputs,
    feature,
    logs,
    sums,
    tiles_own,
    tiles_mate,
    small,
    summed_out,
    rest_out,
    lines_out,
    inputs_v,
    logs_v,
    wide_w,
    pair_w,
    mixer_w,
    expand_w,
    shrink_w,
    leave_w,
    low_v,
    narrow_v,
    first_v,
    query_v,
    key_m,
    value_m,
    key_t,
    value_t,
    context_t,
    contextlow_t,
    blocklow_v,
    hidden_v,
    sum_v,
    dsum_v,
    dcontext_v,
    dcontext_t,
    dvalue_v,
    dkey_v,
    dpair_v,
    scores_v,
    dweight_v,
    weight_v,
    dscores_v,
    g_leave,
    g_mixer,
    g_expand,
    g_shrink,
    small_v,
    tiles_v,
    pool,
    pair_in,
    first_in,
    second,
    second_in,
    third,
    third_in,
    half_own,
    half_in,
    rest_v,
    rest_in,
    rest_sum,
    rest_part,
    rest_all,
    lines_v,
    in_sem,
    sem,
    pair_send,
    pair_recv,
    first_send,
    first_recv,
    second_send,
    second_recv,
    third_send,
    third_recv,
    half_send,
    half_recv,
    swap_send,
    swap_recv,
    part_send,
    part_recv,
    all_send,
    all_recv,
    over_send,
    over_recv,
):
    tokens = inputs.shape[0]
    breadth = small.shape[1] - HID
    breadth = breadth // (2 + NFFN)
    row, core = lax.axis_index("rows"), lax.axis_index("heads")
    n_rows = side * side * deep
    mate = (row, 1 - core)
    barrier = pltpu.get_barrier_semaphore()
    pl.semaphore_signal(barrier, inc=1, device_id=mate, device_id_type=MESH)

    def greet(d, carry):
        peer = (lax.rem(row + d, n_rows), core)
        pl.semaphore_signal(barrier, inc=1, device_id=peer, device_id_type=MESH)
        return carry

    lax.fori_loop(1, n_rows, greet, 0)
    n_blocks = tiles_own.shape[-3]
    loads = [
        (tiles_own, pool.at[:, :, :, pl.ds(0, n_blocks)]),
        (tiles_mate, pool.at[:, :, :, pl.ds(n_blocks, n_blocks)]),
        (inputs, inputs_v),
        (feature.at[:, pl.ds(0, ATT)], dweight_v.at[0]),
        (feature.at[:, pl.ds(ATT, ATT)], dweight_v.at[1]),
    ]
    loads = [pltpu.make_async_copy(p, q, in_sem.at[n]) for n, (p, q) in enumerate(loads)]
    for c in loads:
        c.start()

    def logs_copy(n):
        return pltpu.make_async_copy(logs.at[:, :, pl.ds(n * ATT, ATT)], logs_v.at[n % 2], sem.at[n % 2])

    for n in range(2):
        logs_copy(n).start()
    length, batch = bounds[core, 1], micro_batch[core]
    slots = summed_out.shape[0]
    lines = breadth // 2
    blocks = lines // 16
    for ref in (rest_v, g_leave, g_mixer, g_expand, g_shrink, dvalue_v, dkey_v, small_v):
        ref[...] = jnp.zeros_like(ref)
    plane = side * side

    def of_row(n):
        return n // plane, n // side % side, n % side

    loads[0].wait()
    loads[1].wait()

    def add_digits(n, total):
        zz, yy, xx = of_row(n)
        return total + pool[zz, yy, xx, n_blocks - 1].astype(F32)

    digits = lax.fori_loop(0, n_rows, add_digits, jnp.zeros((16, breadth), F32))
    digits = digits[0:1]
    at_lane = lax.broadcasted_iota(jnp.int32, digits.shape, 1)
    digits = jnp.where(
        at_lane == 2 * batch,
        digits * COUNT_BASE,
        jnp.where(at_lane == 2 * batch + 1, digits, 0.0),
    )
    inverse = 1.0 / jnp.sum(digits, 1, keepdims=True)
    nin = HID // breadth
    nff = SFF // breadth

    def at(j):
        return slice(j * breadth, (j + 1) * breadth)

    at_pair, at_mixer, at_ff = 2 * nin, 2 * nin + 2, 2 * nin + 3
    at_shrink = at_ff + NFFN * nff
    at_leave = at_shrink + NFFN * nff
    def load(i, ref, row, col):
        zz, yy, xx = where_at[0, 0, i], where_at[1, 0, i], where_at[2, 0, i]
        for first_line, there in ((core * lines, where_at[3, 0, i]), ((1 - core) * lines, where_at[4, 0, i])):
            half = pool[zz, yy, xx, pl.ds(there, blocks)].reshape(lines, breadth)
            ref[pl.ds(pl.multiple_of(row * breadth + first_line, lines), lines), at(col)] = half

    for j in range(nin):
        load(j, wide_w, j, 0)
        load(nin + j, wide_w, j, 1)
        load(at_leave + j, leave_w, 0, j)
    load(at_pair, pair_w, 0, 0)
    load(at_pair + 1, pair_w, 0, 1)
    load(at_mixer, mixer_w, 0, 0)
    for b in range(NFFN):
        for j in range(nff):
            load(at_ff + b * nff + j, expand_w.at[b], 0, j)
            load(at_shrink + b * nff + j, shrink_w.at[b], j, 0)

    def gain(n):
        return small[0:1, at(n)]

    def bias(n):
        return small[1:2, at(n)]

    tail = (2 + NFFN) * breadth
    gain_out, bias_out = small[0:1, tail:], small[1:2, tail:]
    lane = lax.broadcasted_iota(jnp.int32, (1, breadth), 1)
    of_head = [(lane // SHD) == h for h in range(SHEADS)]
    loads[2].wait()
    for start in range(0, tokens, ROWS_FF):
        r = slice(start, start + ROWS_FF)
        low = inputs_v[r].astype(BF)
        low_v[r] = low
        both = dot(low, wide_w[...])
        narrow, value = both[:, :breadth], both[:, breadth:]
        narrow_v[r] = narrow
        first = narrow * gain(0) + bias(0)
        first_v[r] = first
        pair = dot(first.astype(BF), pair_w[...])
        query, key = pair[:, :breadth], pair[:, breadth:]
        query_v[r, :breadth] = query.astype(BF)
        place = lax.broadcasted_iota(jnp.int32, (ROWS_FF, 1), 0) + start
        mask = jnp.where(place < length, 0.0, MASKED_SCORE)
        for h in range(SHEADS):
            key_m[h, r, :breadth] = jnp.where(of_head[h], key, 0.0).astype(BF)
            value_m[h, r, :breadth] = jnp.where(of_head[h], value, 0.0).astype(BF)
            of_part = (lane >= 1 + 3 * h) & (lane < 4 + 3 * h)
            less = jnp.where(of_part, -1.0, 0.0)
            key_m[h, r, breadth:] = jnp.where(lane == 0, mask, less).astype(BF)
            value_m[h, r, breadth:] = jnp.broadcast_to(less, (ROWS_FF, breadth)).astype(BF)
        query_v[r, breadth:] = jnp.broadcast_to(jnp.where(lane == 0, 1.0, 0.0), (ROWS_FF, breadth)).astype(BF)
        key_t[:, r] = key.T.astype(BF)
        value_t[:, r] = value.T.astype(BF)
    scale = SHD**-0.5
    scale2 = scale * LOG2E

    def extra_columns(mark, values):
        rows = [jnp.full((1, ATT), mark, F32)]
        for v in values:
            rows.extend(three_parts(v))
        rows.append(jnp.zeros((breadth - len(rows), ATT), F32))
        return jnp.concatenate(rows, 0).T.astype(BF)

    def forward(n, carry):
        r = pl.ds(pl.multiple_of(n * ATT, ATT), ATT)
        query = query_v[r]
        shifts, parts = [], []
        scores_v[0] = dot_nt(key_m[0], query)
        for h in range(SHEADS):
            if h + 1 < SHEADS:
                scores_v[(h + 1) % 2] = dot_nt(key_m[h + 1], query)
            scores, weight = scores_v.at[h % 2], weight_v.at[h % 2]
            top = column_max(scores)
            part = 0.0
            for c in split_rows(scores):
                piece = jnp.exp2((scores[c] - top) * scale2)
                weight[c] = piece.astype(BF)
                part = part + piece
            total = jnp.sum(part, 0, keepdims=True)
            shifts.append(top + jnp.log2(total) * (1.0 / scale2))
            parts.append(dot(value_t[h * SHD : (h + 1) * SHD], weight[...]) * (1.0 / total))
        mixed = jnp.concatenate(parts, 0)
        context_t[:, r] = mixed
        contextlow_t[:, r] = mixed.astype(BF)
        query_v[r, breadth:] = extra_columns(1.0, shifts)
        return carry

    lax.fori_loop(0, tokens // ATT, forward, 0)

    def row_sums(n, d, value):
        small_v[0:1, at(n)] += jnp.sum(d * value, 0, keepdims=True)
        small_v[1:2, at(n)] += jnp.sum(d, 0, keepdims=True)

    part = ROWS_FF // 2

    def feed(n, loss):
        both = range(2)
        rows = [pl.ds(pl.multiple_of(n * ROWS_FF + p * part, part), part) for p in both]
        inside = [slice(p * part, (p + 1) * part) for p in both]
        place = lax.broadcasted_iota(jnp.int32, (part, 1), 0)
        weight = [jnp.where(place + (n * ROWS_FF + p * part) < length, inverse, 0.0) for p in both]
        mixed_sum = [
            dot(context_t[:, rows[p]].T.astype(BF), mixer_w[...]) + first_v[rows[p]] for p in both
        ]
        current = [mixed_sum[p] * gain(1) + bias(1) for p in both]
        for b in range(NFFN):
            for p in both:
                blocklow_v[b, inside[p]] = current[p].astype(BF)
            hidden = [
                jnp.maximum(dot(blocklow_v[b, inside[p]], expand_w[b]), 0.0).astype(BF) for p in both
            ]
            for p in both:
                hidden_v[b, inside[p]] = hidden[p]
            total = [dot(hidden[p], shrink_w[b]) + current[p] for p in both]
            for p in both:
                sum_v[b, inside[p]] = total[p]
            current = [total[p] * gain(2 + b) + bias(2 + b) for p in both]
        joined = [dot(current[p].astype(BF), leave_w[...]) + inputs_v[rows[p]] for p in both]
        d = []
        for p in both:
            feature_rows = jnp.concatenate([dweight_v[0, rows[p]], dweight_v[1, rows[p]]], 1)
            differ = joined[p] * gain_out + bias_out - feature_rows
            square = jnp.mean(differ * differ, -1, keepdims=True)
            loss = loss + jnp.sum(weight[p] * square, 0, keepdims=True)
            outer = differ * (weight[p] * (2.0 / HID))
            small_v[0:1, tail:] += jnp.sum(outer * joined[p], 0, keepdims=True)
            small_v[1:2, tail:] += jnp.sum(outer, 0, keepdims=True)
            back = (outer * gain_out).astype(BF)
            g_leave[...] += dot(current[p].T.astype(BF), back)
            d.append(dot_nt(back, leave_w[...]))
        for b in reversed(range(NFFN)):
            d_sum = []
            for p in both:
                row_sums(2 + b, d[p], sum_v[b, inside[p]])
                d_sum.append(d[p] * gain(2 + b))
            d_hidden = [dot_nt(d_sum[p].astype(BF), shrink_w[b]) for p in both]
            for p in both:
                hidden = hidden_v[b, inside[p]]
                d_before = jnp.where(hidden > 0, d_hidden[p], 0.0).astype(BF)
                d[p] = d_sum[p] + dot_nt(d_before, expand_w[b])
                g_shrink[b] += dot(d_sum[p].T.astype(BF), hidden)
                g_expand[b] += dot(blocklow_v[b, inside[p]].T, d_before)
        for p in both:
            r = rows[p]
            row_sums(1, d[p], mixed_sum[p])
            d_sum = d[p] * gain(1)
            dsum_v[r] = d_sum
            d_mixed = d_sum.astype(BF)
            g_mixer[...] += dot(contextlow_t[:, r], d_mixed)
            d_context = dot_nt(d_mixed, mixer_w[...])
            dcontext_v[r, :breadth] = d_context.astype(BF)
            dcontext_t[:, r] = d_context.astype(BF).astype(F32).T
        return loss

    for c in loads[3:]:
        c.wait()
    loss = lax.fori_loop(0, tokens // ROWS_FF, feed, jnp.zeros((1, 1), F32))
    n_rest = at_mixer
    tiles_v[0] = g_mixer[...].astype(BF)
    for j in range(nin):
        tiles_v[at_leave - n_rest + j] = g_leave[:, at(j)].astype(BF)
    for b in range(NFFN):
        for j in range(nff):
            tiles_v[at_ff - n_rest + b * nff + j] = g_expand[b, :, at(j)].astype(BF)
            tiles_v[at_shrink - n_rest + b * nff + j] = g_shrink[b, :, at(j)].T.astype(BF)
    nothing = tiles_v.shape[0] - 1
    tiles_v[nothing] = jnp.zeros((breadth, breadth), BF)
    z, y, x = row // plane, (row // side) % side, row % side
    mine = pl.multiple_of(core * lines, lines)
    theirs = pl.multiple_of((1 - core) * lines, lines)
    my_half, their_half = core * slots * blocks, (1 - core) * slots * blocks
    straight = core == 0
    a, b_ = jnp.where(straight, x, y), jnp.where(straight, y, x)
    mate_a = b_

    def lay(n, carry):
        per = where_at.shape[2]
        which = where_at[6 + 2 * (n // per), 0, n % per]
        zz, yy, xx = of_row(n // slots)
        tile = tiles_v[which].reshape(2 * blocks, 16, breadth)
        pool[zz, yy, xx, pl.ds(n % slots * blocks, blocks)] = tile[:blocks]
        pool[zz, yy, xx, pl.ds((slots + n % slots) * blocks, blocks)] = tile[blocks:]
        return carry

    lax.fori_loop(0, n_rows * slots, lay, 0)
    pl.semaphore_wait(barrier, n_rows)

    def row_at(xx, yy, zz):
        return zz * plane + yy * side + xx

    def along_a(aa):
        return (jnp.where(straight, row_at(aa, y, z), row_at(x, aa, z)), core)

    def along_b(bb):
        return (jnp.where(straight, row_at(x, bb, z), row_at(bb, y, z)), core)

    def along_z(zz):
        return (row_at(x, y, zz), core)

    def remote(src, dst, send, recv, peer):
        return pltpu.make_async_remote_copy(
            src_ref=src,
            dst_ref=dst,
            send_sem=send,
            recv_sem=recv,
            device_id=peer,
            device_id_type=MESH,
        )

    order = list(range(1, side)) + [0]
    for d in order:
        piece = lax.rem(mate_a + d, side)
        half = pl.ds(their_half, slots * blocks)
        by_y = remote(pool.at[:, piece, :, half], pair_in.at[d], pair_send.at[d], pair_recv.at[d], mate)
        by_x = remote(pool.at[:, :, piece, half], pair_in.at[d], pair_send.at[d], pair_recv.at[d], mate)

        @pl.when(straight)
        def _():
            by_y.start()

        @pl.when(jnp.logical_not(straight))
        def _():
            by_x.start()

    def pair_copy(d):
        return remote(pool.at[:, 0, :, pl.ds(0, slots * blocks)], pair_in.at[d], pair_send.at[d], pair_recv.at[d], mate)

    first_copies, second_copies, third_copies = [], [], []

    def add_pair():
        for d in order:
            pair_copy(d).wait_recv()
            aa = lax.rem(a + d, side)

            def add(i, carry):
                zz, bb = i // side, i % side
                xx, yy = jnp.where(straight, aa, bb), jnp.where(straight, bb, aa)
                own = pool[zz, yy, xx, pl.ds(my_half, slots * blocks)].astype(F32)
                pair_in[d, zz, bb] = (own + pair_in[d, zz, bb].astype(F32)).astype(BF)
                return carry

            lax.fori_loop(0, deep * side, add, 0)
            if d:
                c = remote(pair_in.at[d], first_in.at[d - 1], first_send.at[d - 1], first_recv.at[d - 1], along_a(aa))
                c.start()
                first_copies.append(c)

    def add_first():
        for c in first_copies:
            c.wait_recv()
        for d in order:
            bb = lax.rem(b_ + d, side)

            def add(zz, carry):
                s = pair_in[0, zz, bb].astype(F32)
                for j in range(side - 1):
                    s = s + first_in[j, zz, bb].astype(F32)
                second[d, zz] = s.astype(BF)
                return carry

            lax.fori_loop(0, deep, add, 0)
            if d:
                c = remote(second.at[d], second_in.at[d - 1], second_send.at[d - 1], second_recv.at[d - 1], along_b(bb))
                c.start()
                second_copies.append(c)

    def add_second():
        for c in second_copies:
            c.wait_recv()
        for d in list(range(1, deep)) + [0]:
            zz = lax.rem(z + d, deep)
            s = second[0, zz].astype(F32)
            for j in range(side - 1):
                s = s + second_in[j, zz].astype(F32)
            if d:
                third[d - 1] = s.astype(BF)
                c = remote(third.at[d - 1], third_in.at[d - 1], third_send.at[d - 1], third_recv.at[d - 1], along_z(zz))
                c.start()
                third_copies.append(c)
            else:
                half_own[...] = s.reshape(half_own.shape)

    def add_third():
        for c in third_copies:
            c.wait_recv()
        s = half_own[...]
        for j in range(deep - 1):
            s = s + third_in[j].astype(F32).reshape(half_own.shape)
        half_own[...] = s
        half_copy.start()

    half_copy = remote(half_own, half_in, half_send, half_recv, mate)
    stages = [add_pair, add_first, add_second]

    log_share = jnp.log2(inverse * (1.0 / SHEADS))

    def backward(n, loss):
        r = slice(n * ATT, (n + 1) * ATT)
        place = lax.broadcasted_iota(jnp.int32, (1, ATT), 1) + n * ATT
        inside = place < length
        share = jnp.where(inside, inverse * (1.0 / SHEADS), 0.0)
        share2 = jnp.where(inside, log_share, MASKED_SCORE)
        less = []
        for h in range(SHEADS):
            heads = slice(h * SHD, (h + 1) * SHD)
            along = jnp.sum(context_t[heads, r] * dcontext_t[heads, r], 0, keepdims=True)
            less.append(along - share * sums[h, :, r])
        dcontext_v[r, breadth:] = extra_columns(0.0, less)
        query, d_context = query_v[r], dcontext_v[r]
        logs_copy(n).wait()
        here = logs_v.at[n % 2]

        def products(h):
            scores_v[h % 2] = dot_nt(key_m[h], query)
            dweight_v[h % 2] = dot_nt(value_m[h], d_context)

        products(0)
        parts = []
        gap = 0.0
        for h in range(SHEADS):
            if h + 1 < SHEADS:
                products(h + 1)
            scores, dweight = scores_v.at[h % 2], dweight_v.at[h % 2]
            weight, dscores = weight_v.at[h % 2], dscores_v.at[h % 2]
            for c in split_rows(scores):
                score = scores[c]
                piece = jnp.exp2(score * scale2)
                weight[c] = piece.astype(BF)
                target_log = here[h, c].astype(F32)
                target = jnp.exp2(target_log * LOG2E + share2)
                gap = gap + target * (target_log - score * scale)
                dscores[c] = (piece * dweight[c] - target).astype(BF)
            none = jnp.zeros((ATT, breadth), BF)
            dvalue_v[...] += dot(weight[...], jnp.where(of_head[h], d_context[:, :breadth], none))
            dkey_v[...] += dot(dscores[...], jnp.where(of_head[h], query[:, :breadth], none))
            parts.append(dot(key_t[h * SHD : (h + 1) * SHD], dscores[...]))
        dpair_v[r, at(0)] = (jnp.concatenate(parts, 0) * scale).T.astype(BF)
        if n + 2 < tokens // ATT:
            logs_copy(n + 2).start()
        return loss + jnp.sum(jnp.sum(gap, 0, keepdims=True), 1, keepdims=True)

    for n in range(tokens // ATT):
        loss = backward(n, loss)
        if n < len(stages):
            stages[n]()
    dpair_v[:, at(1)] = (dkey_v[...] * scale).astype(BF)
    d_pair = dpair_v[...]
    d_first = dsum_v[...] + dot_nt(d_pair, pair_w[...])
    row_sums(0, d_first, narrow_v[...])
    g_pair = dot(first_v[...].T.astype(BF), d_pair)
    wide_t = jnp.concatenate([(d_first * gain(0)).T.astype(BF), dvalue_v[...].T.astype(BF)], 0)
    g_wide = dot(wide_t, low_v[...])
    n_lines = small.shape[1] // breadth
    lines_v[...] = jnp.zeros_like(lines_v)
    for j in range(n_lines):
        lines_v[j : j + 1] = small_v[0:1, at(j)]
        lines_v[n_lines + j : n_lines + j + 1] = small_v[1:2, at(j)]
    lines_v[2 * n_lines : 2 * n_lines + 1, 0:1] = loss
    add_third()
    summed = half_own[...]
    lines_v[2 * n_lines + 1 : 2 * n_lines + 2] = jnp.sum(summed * summed, 0, keepdims=True)
    groups = lines_v.shape[0] // 8
    top = 16 * groups
    each = n_rest // 2

    def two_parts(value):
        high = value.astype(BF)
        return high, (value - high.astype(F32)).astype(BF)

    for g in range(groups):
        high, rest = two_parts(lines_v[8 * g : 8 * g + 8])
        rest_v[0, 16 * g : 16 * g + 8] = high
        rest_v[0, 16 * g + 8 : 16 * g + 16] = rest

    def keep(n, value):
        line = top + (n % each) * breadth
        rest_v[n // each, line : line + breadth] = value.astype(BF)

    for j in range(nin):
        keep(j, g_wide[:breadth, at(j)].T)
        keep(nin + j, g_wide[breadth:, at(j)].T)
    keep(at_pair, g_pair[:, at(0)])
    keep(at_pair + 1, g_pair[:, at(1)])
    swap = remote(rest_v.at[1 - core], rest_in, swap_send, swap_recv, mate)
    swap.start()
    swap.wait()
    rest_sum[...] = (rest_v[core].astype(F32) + rest_in[...].astype(F32)).astype(BF)
    for g in range(groups):
        high_at, rest_at = slice(16 * g, 16 * g + 8), slice(16 * g + 8, 16 * g + 16)
        value = rest_v[core, high_at].astype(F32) + rest_v[core, rest_at].astype(F32)
        value = value + rest_in[high_at].astype(F32) + rest_in[rest_at].astype(F32)
        rest_sum[high_at], rest_sum[rest_at] = two_parts(value)
    chunk = rest_part.shape[1]

    def lines_of(n):
        return pl.ds(pl.multiple_of(n * chunk, chunk), chunk)

    def part_copy(d):
        to = lax.rem(row + d, n_rows)
        return remote(rest_sum.at[lines_of(to)], rest_part.at[d - 1], part_send.at[d - 1], part_recv.at[d - 1], (to, core))

    def all_copy(d):
        here = rest_all.at[core, lines_of(row)]
        return remote(here, here, all_send.at[d - 1], all_recv.at[d - 1], (lax.rem(row + d, n_rows), core))

    def each_peer(act):
        def one(d, carry):
            act(d)
            return carry

        lax.fori_loop(1, n_rows, one, 0)

    each_peer(lambda d: part_copy(d).start())
    each_peer(lambda d: part_copy(d).wait())
    total = lax.fori_loop(
        0, n_rows - 1, lambda d, t: t + rest_part[d].astype(F32), rest_sum[lines_of(row)].astype(F32)
    )
    high_of = []
    for g in range(chunk // 16):
        piece = total[16 * g : 16 * g + 16]
        high, rest = two_parts(piece[:8] + piece[8:])
        split = jnp.concatenate([high.astype(F32), rest.astype(F32)], 0)
        high_of.append(jnp.where(row * (chunk // 16) + g < groups, split, piece))
    rest_all[core, lines_of(row)] = jnp.where(core == 0, jnp.concatenate(high_of, 0), total).astype(BF)
    each_peer(lambda d: all_copy(d).start())
    half_copy.wait()
    for k in range(slots):
        summed_out[k, pl.ds(mine, lines)] = half_own[k * lines : (k + 1) * lines]
        summed_out[k, pl.ds(theirs, lines)] = half_in[k * lines : (k + 1) * lines]
    each_peer(lambda d: all_copy(d).wait())
    over = remote(rest_all.at[core], rest_all.at[core], over_send, over_recv, mate)
    over.start()
    for d in order:
        pair_copy(d).wait_send()
    for c in first_copies + second_copies + third_copies:
        c.wait_send()
    over.wait()
    squares = jnp.zeros((1, breadth), F32)
    for n in range(n_rest):
        line = top + (n % each) * breadth
        rest_out[n] = rest_all[n // each, line : line + breadth]
        tile = rest_out[n].astype(F32)
        squares = squares + jnp.sum(tile * tile, 0, keepdims=True)
    for g in range(groups):
        high = rest_all[0, 16 * g : 16 * g + 8].astype(F32)
        lines_out[8 * g : 8 * g + 8] = high + rest_all[0, 16 * g + 8 : 16 * g + 16].astype(F32)
    lines_out[2 * n_lines + 2 : 2 * n_lines + 3] = squares


def student(where_at, bounds, micro_batch, inputs, feature, logs, sums, tiles_own, tiles_mate, small, slots):
    tokens = inputs.shape[0]
    n_rows, w = tiles_own.shape[0], tiles_own.shape[-1]
    deep = 4
    side = math.isqrt(n_rows // deep)
    assert side * side * deep == n_rows
    n_lines = 8 * -(-(2 * small.shape[1] // w + 3) // 8)
    n_rest = 2 * HID // w + 2
    n_tiles = 1 + 2 * NFFN * (SFF // w) + HID // w
    half = w // 2
    in_half = 2 * n_lines + (HID // w + 1) * w
    chunk = 16 * -(-in_half // (16 * n_rows))
    s1, d1 = side - 1, deep - 1
    gathered = (deep, side, side) + tiles_own.shape[1:]
    tiles_own, tiles_mate = tiles_own.reshape(gathered), tiles_mate.reshape(gathered)
    blocks = slots * half // 16
    D = pltpu.SemaphoreType.DMA

    def low(*shape):
        return pltpu.VMEM(shape, BF)

    def full(*shape):
        return pltpu.VMEM(shape, F32)

    return pl.pallas_call(
        functools.partial(student_kernel, side, deep),
        out_shape=(
            jax.ShapeDtypeStruct((slots, w, w), F32),
            jax.ShapeDtypeStruct((n_rest, w, w), BF),
            jax.ShapeDtypeStruct((n_lines, w), F32),
        ),
        in_specs=[SMEM] * 3 + [ANY, ANY, ANY, VMEM, ANY, ANY, VMEM],
        out_specs=(VMEM, VMEM, VMEM),
        scratch_shapes=[
            full(tokens, HID),
            low(2, SHEADS, tokens, ATT),
            low(HID, 2 * w),
            low(w, 2 * w),
            low(w, w),
            low(NFFN, w, SFF),
            low(NFFN, SFF, w),
            low(w, HID),
            low(tokens, HID),
            full(tokens, w),
            full(tokens, w),
            low(tokens, 2 * w),
            low(SHEADS, tokens, 2 * w),
            low(SHEADS, tokens, 2 * w),
            low(w, tokens),
            low(w, tokens),
            full(w, tokens),
            low(w, tokens),
            low(NFFN, ROWS_FF, w),
            low(NFFN, ROWS_FF, SFF),
            full(NFFN, ROWS_FF, w),
            full(tokens, w),
            low(tokens, 2 * w),
            full(w, tokens),
            full(tokens, w),
            full(tokens, w),
            low(tokens, 2 * w),
            full(2, tokens, ATT),
            full(2, tokens, ATT),
            low(2, tokens, ATT),
            low(2, tokens, ATT),
            full(w, HID),
            full(w, w),
            full(NFFN, w, SFF),
            full(NFFN, w, SFF),
            full(8, small.shape[1]),
            low(n_tiles + 1, w, w),
            low(deep, side, side, 2 * tiles_own.shape[-3], 16, w),
            low(side, deep, side, blocks, 16, w),
            low(s1, deep, side, blocks, 16, w),
            low(side, deep, blocks, 16, w),
            low(s1, deep, blocks, 16, w),
            low(d1, blocks, 16, w),
            low(d1, blocks, 16, w),
            full(slots * half, w),
            full(slots * half, w),
            low(2, chunk * n_rows, w),
            low(chunk * n_rows, w),
            low(chunk * n_rows, w),
            low(n_rows - 1, chunk, w),
            low(2, chunk * n_rows, w),
            full(n_lines, w),
            D((5,)),
            D((2,)),
            D((side,)),
            D((side,)),
            D((s1,)),
            D((s1,)),
            D((s1,)),
            D((s1,)),
            D((d1,)),
            D((d1,)),
            D,
            D,
            D,
            D,
            D((n_rows - 1,)),
            D((n_rows - 1,)),
            D((n_rows - 1,)),
            D((n_rows - 1,)),
            D,
            D,
        ],
        compiler_params=pltpu.CompilerParams(
            collective_id=0, has_side_effects=True, vmem_limit_bytes=63 << 20
        ),
        cost_estimate=pl.CostEstimate(
            flops=15_000_000_000, bytes_accessed=16 << 20, transcendentals=0
        ),
    )(where_at, bounds, micro_batch, inputs, feature, logs, sums, tiles_own, tiles_mate, small)


def update_kernel(
    n_tiles, where_at, step, own, summed, rest, lines, weight_in, first_in, second_in, small, small_first, small_second,
    loss_out, norm_out, tiles_out, first_out, second_out, small_out, small_first_out, small_second_out, small_grad_out,
    small_v, weight, first, second, sem,
):
    pairs = ((weight_in, weight), (first_in, first), (second_in, second))
    loads = [pltpu.make_async_copy(a, b, sem.at[n]) for n, (a, b) in enumerate(pairs)]
    for c in loads:
        c.start()
    breadth = summed.shape[2]
    n_lines = small.shape[1] // breadth
    steps = step[0]
    first_fix = 1.0 - lax.fori_loop(0, steps, lambda i, p: p * BETA_FIRST, jnp.float32(1.0))
    second_fix = 1.0 - lax.fori_loop(0, steps, lambda i, p: p * BETA_SECOND, jnp.float32(1.0))

    def adam(w, m, v, g, decay):
        m = BETA_FIRST * m + (1.0 - BETA_FIRST) * g
        v = BETA_SECOND * v + (1.0 - BETA_SECOND) * g * g
        change = m / first_fix / (jnp.sqrt(v / second_fix) + ADAM_EPSILON) + decay * w
        return w - LEARN_RATE * change, m, v

    line = lambda n: lines[n : n + 1]
    squares = line(2 * n_lines + 1) + line(2 * n_lines + 2)
    for n in range(2 * n_lines):
        squares = squares + line(n) * line(n)
    norm = jnp.sqrt(jnp.sum(squares, 1, keepdims=True))
    norm_out[...] = norm
    loss_out[...] = line(2 * n_lines)[:, 0:1]
    factor = CLIP_NORM / jnp.maximum(norm, CLIP_NORM)
    for n in range(n_lines):
        cols = slice(n * breadth, (n + 1) * breadth)
        small_v[0:1, cols] = line(n)
        small_v[1:2, cols] = line(n_lines + n)
    small_grad = small_v[0:2] * factor
    small_grad_out[...] = small_grad
    w, m, v = adam(small[...], small_first[...], small_second[...], small_grad, 0.0)
    small_out[...] = w
    small_first_out[...] = m
    small_second_out[...] = v

    slots, n_rest = summed.shape[0], rest.shape[0]
    for c in loads:
        c.wait()
    for s in range(summed.shape[0]):
        at = own[0] * slots + s
        which = where_at[5 + 2 * (at // 128), 0, at % 128]
        keep = which < n_tiles
        other = rest[jnp.minimum(which, n_rest - 1)].astype(F32)
        total = summed[s] + jnp.where(which < n_rest, other, 0.0)
        w, m, v = adam(weight[s], first[s], second[s], total * factor, WEIGHT_DECAY)
        tiles_out[s] = jnp.where(keep, w, 0.0)
        first_out[s] = jnp.where(keep, m, 0.0)
        second_out[s] = jnp.where(keep, v, 0.0)


def update(n_tiles, where_at, step, own, summed, rest, lines, weight, first, second, small, small_first, small_second):
    one = jax.ShapeDtypeStruct((1, 1), F32)
    tile = jax.ShapeDtypeStruct(weight.shape, F32)
    row = jax.ShapeDtypeStruct(small.shape, F32)
    return pl.pallas_call(
        functools.partial(update_kernel, n_tiles),
        out_shape=(one, one, tile, tile, tile, row, row, row, row),
        in_specs=[SMEM] * 3 + [VMEM] * 3 + [HBM] * 3 + [VMEM] * 3,
        out_specs=(VMEM,) * 9,
        scratch_shapes=[pltpu.VMEM((8, small.shape[1]), F32)]
        + [pltpu.VMEM(weight.shape, F32)] * 3
        + [pltpu.SemaphoreType.DMA((3,))],
        compiler_params=pltpu.CompilerParams(vmem_limit_bytes=63 << 20),
        cost_estimate=pl.CostEstimate(flops=2_000_000, bytes_accessed=2 << 20, transcendentals=0),
    )(where_at, step, own, summed, rest, lines, weight, first, second, small, small_first, small_second)


def on_device(
    token_ids,
    bounds,
    micro_batch,
    owners,
    step_count,
    word_table,
    conv_weight,
    embed_extra,
    teacher_entry,
    teacher_project,
    teacher_mixer,
    teacher_expand,
    teacher_shrink,
    teacher_leave,
    teacher_norms,
    tile_weight,
    tile_first,
    tile_second,
    small_weight,
    small_first,
    small_second,
):
    core = lax.axis_index("heads")
    n_rows = lax.axis_size("rows")
    assert token_ids.shape[0] == lax.axis_size("heads")
    row_ids = lax.dynamic_index_in_dim(token_ids, core, 0, keepdims=False)
    words = word_table.at[row_ids].get(mode="promise_in_bounds")
    inputs, feature, logs, sums, where_at, tiles_own, tiles_mate = teacher(
        n_rows,
        bounds,
        micro_batch,
        owners,
        words,
        conv_weight,
        embed_extra,
        teacher_norms,
        tile_weight,
        teacher_entry,
        teacher_project.transpose(1, 0, 2),
        teacher_mixer,
        teacher_expand,
        teacher_shrink,
        teacher_leave,
    )
    summed, rest, lines = student(
        where_at,
        bounds,
        micro_batch,
        inputs,
        feature,
        logs,
        sums,
        tiles_own,
        tiles_mate,
        small_weight,
        tile_weight.shape[0],
    )
    own = lax.axis_index("rows")[None]
    loss, norm, *rest = update(
        owners.shape[0],
        where_at,
        step_count,
        own,
        summed,
        rest,
        lines,
        tile_weight,
        tile_first,
        tile_second,
        small_weight,
        small_first,
        small_second,
    )
    return (loss[0, 0], norm[0, 0], *rest)


def solution(mesh):
    placed = (
        P("rows", None),
        P("rows", None),
        P("rows"),
        P(),
        P(),
        P(),
        P(),
        P(),
        P(),
        P(None, None, "heads"),
        P("heads", None),
        P(None, "heads"),
        P("heads", None),
        P(),
        P(),
        P("rows", None, None),
        P("rows", None, None),
        P("rows", None, None),
        P(),
        P(),
        P(),
    )
    tiles = P("rows", None, None)
    return jax.shard_map(
        on_device,
        mesh=mesh,
        in_specs=placed,
        out_specs=(P(), P(), tiles, tiles, tiles, P(), P(), P(), P()),
        check_vma=False,
    )
```

```python
import functools
import math

import jax
import jax.numpy as jnp
from jax import lax
from jax.experimental import pallas as pl
from jax.experimental.pallas import tpu as pltpu
from jax.sharding import PartitionSpec as P

HID = 512
THD = 256
SHEADS = 4
SHD = 32
SFF = 512
NFFN = 4
NMB = 2
NORM_EPSILON = 1e-05
CLIP_NORM = 0.05
LEARN_RATE = 0.1
BETA_FIRST = 0.9
BETA_SECOND = 0.999
ADAM_EPSILON = 1e-08
WEIGHT_DECAY = 0.01
MASKED_SCORE = -1e30
LOG2E = math.log2(math.e)
COUNT_BASE = 64

ATT = 256
ROWS_FF = 512
CUT_FF = 512
LOG_SLOTS = 4
DEEP = 4

MESH = pl.DeviceIdType.MESH
BF, F32 = jnp.bfloat16, jnp.float32
VMEM = pl.BlockSpec(memory_space=pltpu.VMEM)
SMEM = pl.BlockSpec(memory_space=pltpu.SMEM)
HBM = pl.BlockSpec(memory_space=pltpu.HBM)
ANY = pl.BlockSpec(memory_space=pl.ANY)


def dot(left, right):
    return jnp.dot(left, right, preferred_element_type=F32)


def dot_nt(left, right):
    return lax.dot_general(left, right, (((1,), (1,)), ((), ())), preferred_element_type=F32)


def layer_norm(values, gain_row, bias_row):
    center = values - jnp.mean(values, -1, keepdims=True)
    spread = jnp.mean(center * center, -1, keepdims=True)
    return center * lax.rsqrt(spread + NORM_EPSILON) * gain_row + bias_row


def sum_over(ref, n):
    s = ref[0]
    for i in range(1, n):
        s = s + ref[i]
    return s


def split_rows(refs, rows=64):
    for start in range(0, refs.shape[-2], rows):
        yield slice(start, start + rows)


def column_max(ref):
    best = None
    for c in split_rows(ref):
        best = ref[c] if best is None else jnp.maximum(best, ref[c])
    return jnp.max(best, 0, keepdims=True)


def attend_half(
    length,
    first_head,
    low_v,
    project_v,
    query_v,
    key_v,
    value_t,
    context_v,
    logs_out,
    sums_out,
    logs_v,
    scores_v,
    weight_v,
    sem,
    pending,
):
    tokens = low_v.shape[0]
    width = project_v.shape[2]
    for start in range(0, tokens, ROWS_FF):
        rows = slice(start, start + ROWS_FF)
        low = low_v[rows]
        query_v[rows] = (dot(low, project_v[0]) * THD**-0.5).astype(BF)
        key_v[rows] = dot(low, project_v[1]).astype(BF)
        value_t[:, rows] = dot(low, project_v[2]).T.astype(BF)
    steps = [(h, q) for h in range(width // THD) for q in range(tokens // ATT)]
    least = tokens // 2

    def scores_of(i):
        h, q = steps[i]
        cols = slice(h * THD, (h + 1) * THD)
        query = query_v[q * ATT : (q + 1) * ATT, cols]
        scores_v[i % 2, :least] = dot_nt(key_v[:least, cols], query)
        valid = lax.broadcasted_iota(jnp.int32, (tokens - least, ATT), 0) + least < length
        scores_v[i % 2, least:] = jnp.where(valid, dot_nt(key_v[least:, cols], query), MASKED_SCORE)

    scores_of(0)
    for i, (h, q) in enumerate(steps):
        if len(pending) == LOG_SLOTS:
            pending.pop(0).wait()
        if i + 1 < len(steps):
            scores_of(i + 1)
        at = i % LOG_SLOTS
        scores, weight, logs = scores_v.at[i % 2], weight_v.at[i % 2], logs_v.at[at]
        top = column_max(scores)
        part = 0.0
        for c in split_rows(scores):
            piece = jnp.exp(scores[c] - top)
            weight[c] = piece.astype(BF)
            part = part + piece
        total = jnp.sum(part, 0, keepdims=True)
        shift = top + jnp.log(total)
        part = 0.0
        for c in split_rows(scores):
            piece = (scores[c] - shift).astype(BF)
            logs[c] = piece
            part = part + jnp.exp(piece.astype(F32))
        sums_out[first_head + h, :, q * ATT : (q + 1) * ATT] = jnp.sum(part, 0, keepdims=True)
        mixed = dot(value_t[h * THD : (h + 1) * THD], weight[...]) * (1.0 / total)
        context_v[q * ATT : (q + 1) * ATT, h * THD : (h + 1) * THD] = mixed.T.astype(BF)
        there = logs_out.at[first_head + h, :, pl.ds(q * ATT, ATT)]
        pending.append(pltpu.make_async_copy(logs, there, sem.at[at]))
        pending[-1].start()
    assert len(steps) % LOG_SLOTS == 0


def teacher_kernel(
    bounds,
    micro_batch,
    owners,
    words,
    conv,
    extra,
    norms,
    weight,
    entry,
    project,
    mixer,
    expand,
    shrink,
    leave,
    inputs_out,
    feature_out,
    logs_out,
    sums_out,
    where_out,
    tiles_own,
    tiles_mate,
    trigram,
    hidden_v,
    low_v,
    entry_v,
    project_v,
    mixer_v,
    expand_v,
    shrink_v,
    leave_v,
    query_v,
    key_v,
    value_t,
    context_v,
    logs_v,
    scores_v,
    weight_v,
    inner_v,
    sent,
    in_sem,
    logs_sem,
    swap_send,
    swap_recv,
    tile_send,
    tile_recv,
    pass_send,
    pass_recv,
):
    tokens, wide = words.shape
    breadth = entry.shape[1]
    half = project.shape[2]
    hidden_half = expand.shape[1]
    n_rows = tiles_own.shape[0]
    row, core = lax.axis_index("rows"), lax.axis_index("heads")
    mate = (row, 1 - core)
    start_at, length = bounds[core, 0], bounds[core, 1]
    slots, _, lanes = weight.shape
    lines = weight.shape[1] // 2
    blocks = lines // 16
    for n in range(slots):
        half_tile = weight[n, pl.ds(core * lines, lines)].astype(BF)
        sent[n * blocks : (n + 1) * blocks] = half_tile.reshape(blocks, 16, lanes)
    lane = lax.broadcasted_iota(jnp.int32, (16, lanes), 1)
    digits = jnp.zeros((16, lanes), F32)
    for m in range(NMB):
        held = jnp.int32(0)
        for n in range(micro_batch.shape[0]):
            held = held + jnp.where(micro_batch[n] == m, bounds[n, 1], 0)
        digits = jnp.where(lane == 2 * m, (held // COUNT_BASE).astype(F32), digits)
        digits = jnp.where(lane == 2 * m + 1, (held % COUNT_BASE).astype(F32), digits)
    sent[slots * blocks] = digits.astype(BF)
    n_tiles, n_rest = owners.shape[0], 2 * HID // lanes + 2
    side = math.isqrt(tiles_own.shape[0] // DEEP)
    bits = side.bit_length() - 1
    spot = lax.broadcasted_iota(jnp.int32, (1, where_out.shape[2]), 1)
    owner_of = jnp.zeros(spot.shape, jnp.int32)
    rank_of = jnp.zeros(spot.shape, jnp.int32)
    for i in range(n_tiles):
        owner_of = jnp.where(spot == i, owners[i], owner_of)
    for i in range(n_tiles):
        rank_of = rank_of + jnp.where((owner_of == owners[i]) & (spot > i), 1, 0)
    where_out[0] = lax.shift_right_logical(owner_of, 2 * bits)
    where_out[1] = lax.shift_right_logical(owner_of, bits) & (side - 1)
    where_out[2] = owner_of & (side - 1)
    where_out[3] = rank_of * blocks
    where_out[4] = rank_of * blocks + slots * blocks + 1
    for g in range(where_out.shape[0] // 2 - 2):
        spots = spot + g * where_out.shape[2]
        owner_here = lax.shift_right_logical(spots, slots.bit_length() - 1)
        rank_here = spots & (slots - 1)
        seen = jnp.zeros(spot.shape, jnp.int32)
        which = jnp.full(spot.shape, n_tiles, jnp.int32)
        for i in range(n_tiles):
            same = owner_here == owners[i]
            which = jnp.where(same & (seen == rank_here), i, which)
            seen = seen + jnp.where(same, 1, 0)
        where_out[5 + 2 * g] = which
        where_out[6 + 2 * g] = jnp.where(which >= n_rest, which - n_rest, n_tiles - n_rest)

    def peer(d):
        return (lax.rem(row + d, n_rows), core)

    local = [(entry, entry_v), (project, project_v.at[0]), (mixer, mixer_v.at[0])]
    local += [(expand, expand_v.at[0]), (shrink, shrink_v.at[0]), (leave, leave_v)]
    local += [(sent, tiles_own.at[row])]
    loads = [pltpu.make_async_copy(a, b, in_sem.at[n]) for n, (a, b) in enumerate(local)]
    for c in loads:
        c.start()
    barrier = pltpu.get_barrier_semaphore()
    pl.semaphore_signal(barrier, inc=1, device_id=mate, device_id_type=MESH)

    def greet(d, carry):
        pl.semaphore_signal(barrier, inc=1, device_id=peer(d), device_id_type=MESH)
        return carry

    lax.fori_loop(1, n_rows, greet, 0)
    pl.semaphore_wait(barrier, n_rows)
    swaps = []
    for n, (a, b) in enumerate(((project, project_v), (mixer, mixer_v), (expand, expand_v), (shrink, shrink_v))):
        swaps.append(
            pltpu.make_async_remote_copy(
                src_ref=a,
                dst_ref=b.at[1],
                send_sem=swap_send.at[n],
                recv_sem=swap_recv.at[n],
                device_id=mate,
                device_id_type=MESH,
            )
        )
        swaps[-1].start()

    def tile_copy(d):
        return pltpu.make_async_remote_copy(
            src_ref=sent,
            dst_ref=tiles_own.at[row],
            send_sem=tile_send.at[d - 1],
            recv_sem=tile_recv.at[d - 1],
            device_id=peer(d),
            device_id_type=MESH,
        )

    def send_tiles(d, carry):
        tile_copy(d).start()
        return carry

    lax.fori_loop(1, n_rows, send_tiles, 0)
    rows = words[...].astype(F32)
    place = lax.broadcasted_iota(jnp.int32, (tokens, wide), 0)
    after = jnp.where(place < tokens - 1, pltpu.roll(rows, tokens - 1, 0), 0.0)
    before = jnp.where(place > 0, pltpu.roll(rows, 1, 0), 0.0)
    trigram[:, :wide] = after.astype(BF)
    trigram[:, wide : 2 * wide] = words[...]
    trigram[:, 2 * wide :] = before.astype(BF)
    spot = lax.broadcasted_iota(jnp.int32, (ATT, 1), 0)
    gain, bias = norms[0:1], norms[1:2]
    loads[0].wait()
    for start in range(0, tokens, ATT):
        r = slice(start, start + ATT)
        second = spot + start >= start_at
        kind = jnp.where(second, extra[tokens + 1 : tokens + 2], extra[tokens : tokens + 1])
        value = dot(trigram[r], conv[...]) + extra[r] + kind
        inputs_out[r] = value
        hidden = layer_norm(dot(value.astype(BF), entry_v[...]), gain[:, :breadth], bias[:, :breadth])
        hidden_v[r] = hidden
        low_v[r] = hidden.astype(BF)
    heads = half // THD
    pending = []
    for p in range(2):
        if p == 0:
            loads[1].wait()
        else:
            swaps[0].wait()
        first_head = core * heads if p == 0 else (1 - core) * heads
        attend_half(
            length,
            first_head,
            low_v,
            project_v.at[p],
            query_v,
            key_v,
            value_t,
            context_v.at[p],
            logs_out,
            sums_out,
            logs_v,
            scores_v,
            weight_v,
            logs_sem,
            pending,
        )
    loads[2].wait()
    swaps[1].wait()
    for c in loads[3:]:
        c.wait()
    blocks = tokens // ROWS_FF

    def hidden_units(p, low):
        for c in range(0, hidden_half, CUT_FF):
            before = dot(low, expand_v[p, :, c : c + CUT_FF])
            inner = 0.5 * before * (1.0 + lax.erf(before * math.sqrt(0.5)))
            inner_v[:, c : c + CUT_FF] = inner.astype(BF)

    def feed_own(n):
        r = slice(n * ROWS_FF, (n + 1) * ROWS_FF)
        mixed = dot(context_v[0, r], mixer_v[0]) + dot(context_v[1, r], mixer_v[1])
        first = layer_norm(
            mixed + hidden_v[r], gain[:, breadth : 2 * breadth], bias[:, breadth : 2 * breadth]
        )
        hidden_v[r] = first
        low_v[r] = first.astype(BF)
        hidden_units(0, low_v[r])
        hidden_v[r] += dot(inner_v[...], shrink_v[0])

    def feed_mate(n):
        r = slice(n * ROWS_FF, (n + 1) * ROWS_FF)
        hidden_units(1, low_v[r])
        total = dot(inner_v[...], shrink_v[1]) + hidden_v[r]
        second = layer_norm(
            total, gain[:, 2 * breadth : 3 * breadth], bias[:, 2 * breadth : 3 * breadth]
        )
        raw = dot(second.astype(BF), leave_v[...]) + inputs_out[r]
        feature_out[r] = layer_norm(
            raw, gain[:, 3 * breadth : 3 * breadth + HID], bias[:, 3 * breadth : 3 * breadth + HID]
        )

    for n in range(blocks):
        feed_own(n)

    def take_tiles(d, carry):
        tile_copy(d).wait()
        return carry

    lax.fori_loop(1, n_rows, take_tiles, 0)
    over = pltpu.make_async_remote_copy(
        src_ref=tiles_own,
        dst_ref=tiles_mate,
        send_sem=pass_send,
        recv_sem=pass_recv,
        device_id=mate,
        device_id_type=MESH,
    )
    over.start()
    for c in swaps[2:]:
        c.wait()
    for n in range(blocks):
        feed_mate(n)
    over.wait()
    for c in pending:
        c.wait()


def teacher(n_rows, bounds, micro_batch, owners, words, conv, extra, norms, weight, entry, project, mixer, expand, shrink, leave):
    tokens, wide = words.shape
    breadth = entry.shape[1]
    half = project.shape[2]
    hidden_half = expand.shape[1]
    V, D = pltpu.VMEM, pltpu.SemaphoreType.DMA
    slots, lines, lanes = weight.shape
    sent = (slots * lines // 32 + 1, 16, lanes)
    groups = -(-n_rows * slots // 128)
    gathered = jax.ShapeDtypeStruct((n_rows,) + sent, BF)
    return pl.pallas_call(
        teacher_kernel,
        out_shape=(
            jax.ShapeDtypeStruct((tokens, HID), F32),
            jax.ShapeDtypeStruct((tokens, HID), F32),
            jax.ShapeDtypeStruct((2 * half // THD, tokens, tokens), BF),
            jax.ShapeDtypeStruct((2 * half // THD, 1, tokens), F32),
            jax.ShapeDtypeStruct((5 + 2 * groups, 1, 128), jnp.int32),
            gathered,
            gathered,
        ),
        in_specs=[SMEM] * 3 + [VMEM] * 5 + [ANY] * 6,
        out_specs=(VMEM, VMEM, ANY, VMEM, VMEM, ANY, ANY),
        scratch_shapes=[
            V((tokens, 3 * wide), BF),
            V((tokens, breadth), F32),
            V((tokens, breadth), BF),
            V(entry.shape, BF),
            V((2,) + project.shape, BF),
            V((2,) + mixer.shape, BF),
            V((2,) + expand.shape, BF),
            V((2,) + shrink.shape, BF),
            V(leave.shape, BF),
            V((tokens, half), BF),
            V((tokens, half), BF),
            V((half, tokens), BF),
            V((2, tokens, half), BF),
            V((LOG_SLOTS, tokens, ATT), BF),
            V((2, tokens, ATT), F32),
            V((2, tokens, ATT), BF),
            V((ROWS_FF, hidden_half), BF),
            V(sent, BF),
            D((7,)),
            D((LOG_SLOTS,)),
            D((4,)),
            D((4,)),
            D((n_rows - 1,)),
            D((n_rows - 1,)),
            D,
            D,
        ],
        compiler_params=pltpu.CompilerParams(
            collective_id=1, has_side_effects=True, vmem_limit_bytes=62 << 20
        ),
        cost_estimate=pl.CostEstimate(
            flops=33_000_000_000, bytes_accessed=40 << 20, transcendentals=0
        ),
    )(bounds, micro_batch, owners, words, conv, extra, norms, weight, entry, project, mixer, expand, shrink, leave)


def three_parts(value):
    high = value.astype(BF).astype(F32)
    middle = (value - high).astype(BF).astype(F32)
    return high, middle, value - high - middle


def student_kernel(
    side,
    deep,
    where_at,
    bounds,
    micro_batch,
    inputs,
    feature,
    logs,
    sums,
    tiles_own,
    tiles_mate,
    small,
    summed_out,
    rest_out,
    lines_out,
    inputs_v,
    logs_v,
    wide_w,
    pair_w,
    mixer_w,
    expand_w,
    shrink_w,
    leave_w,
    low_v,
    narrow_v,
    first_v,
    query_v,
    key_m,
    value_m,
    key_t,
    value_t,
    context_t,
    contextlow_t,
    blocklow_v,
    hidden_v,
    sum_v,
    dsum_v,
    dcontext_v,
    dcontext_t,
    dvalue_v,
    dkey_v,
    dpair_v,
    scores_v,
    dweight_v,
    weight_v,
    dscores_v,
    g_leave,
    g_mixer,
    g_expand,
    g_shrink,
    small_v,
    tiles_v,
    pool,
    pair_in,
    first_in,
    second,
    second_in,
    third,
    third_in,
    half_own,
    half_in,
    rest_v,
    rest_in,
    rest_sum,
    rest_part,
    rest_all,
    lines_v,
    in_sem,
    sem,
    pair_send,
    pair_recv,
    first_send,
    first_recv,
    second_send,
    second_recv,
    third_send,
    third_recv,
    half_send,
    half_recv,
    swap_send,
    swap_recv,
    part_send,
    part_recv,
    all_send,
    all_recv,
    over_send,
    over_recv,
):
    tokens = inputs.shape[0]
    breadth = small.shape[1] - HID
    breadth = breadth // (2 + NFFN)
    row, core = lax.axis_index("rows"), lax.axis_index("heads")
    n_rows = side * side * deep
    mate = (row, 1 - core)
    barrier = pltpu.get_barrier_semaphore()
    pl.semaphore_signal(barrier, inc=1, device_id=mate, device_id_type=MESH)

    def greet(d, carry):
        peer = (lax.rem(row + d, n_rows), core)
        pl.semaphore_signal(barrier, inc=1, device_id=peer, device_id_type=MESH)
        return carry

    lax.fori_loop(1, n_rows, greet, 0)
    n_blocks = tiles_own.shape[-3]
    loads = [
        (tiles_own, pool.at[:, :, :, pl.ds(0, n_blocks)]),
        (tiles_mate, pool.at[:, :, :, pl.ds(n_blocks, n_blocks)]),
        (inputs, inputs_v),
        (feature.at[:, pl.ds(0, ATT)], dweight_v.at[0]),
        (feature.at[:, pl.ds(ATT, ATT)], dweight_v.at[1]),
    ]
    loads = [pltpu.make_async_copy(p, q, in_sem.at[n]) for n, (p, q) in enumerate(loads)]
    for c in loads:
        c.start()

    def logs_copy(n):
        return pltpu.make_async_copy(logs.at[:, :, pl.ds(n * ATT, ATT)], logs_v.at[n % 2], sem.at[n % 2])

    for n in range(2):
        logs_copy(n).start()
    length, batch = bounds[core, 1], micro_batch[core]
    slots = summed_out.shape[0]
    lines = breadth // 2
    blocks = lines // 16
    for ref in (rest_v, g_leave, g_mixer, g_expand, g_shrink, dvalue_v, dkey_v, small_v):
        ref[...] = jnp.zeros_like(ref)
    plane = side * side

    def of_row(n):
        return n // plane, n // side % side, n % side

    loads[0].wait()
    loads[1].wait()

    def add_digits(n, total):
        zz, yy, xx = of_row(n)
        return total + pool[zz, yy, xx, n_blocks - 1].astype(F32)

    digits = lax.fori_loop(0, n_rows, add_digits, jnp.zeros((16, breadth), F32))
    digits = digits[0:1]
    at_lane = lax.broadcasted_iota(jnp.int32, digits.shape, 1)
    digits = jnp.where(
        at_lane == 2 * batch,
        digits * COUNT_BASE,
        jnp.where(at_lane == 2 * batch + 1, digits, 0.0),
    )
    inverse = 1.0 / jnp.sum(digits, 1, keepdims=True)
    nin = HID // breadth
    nff = SFF // breadth

    def at(j):
        return slice(j * breadth, (j + 1) * breadth)

    at_pair, at_mixer, at_ff = 2 * nin, 2 * nin + 2, 2 * nin + 3
    at_shrink = at_ff + NFFN * nff
    at_leave = at_shrink + NFFN * nff
    def load(i, ref, row, col):
        zz, yy, xx = where_at[0, 0, i], where_at[1, 0, i], where_at[2, 0, i]
        for first_line, there in ((core * lines, where_at[3, 0, i]), ((1 - core) * lines, where_at[4, 0, i])):
            half = pool[zz, yy, xx, pl.ds(there, blocks)].reshape(lines, breadth)
            ref[pl.ds(pl.multiple_of(row * breadth + first_line, lines), lines), at(col)] = half

    for j in range(nin):
        load(j, wide_w, j, 0)
        load(nin + j, wide_w, j, 1)
        load(at_leave + j, leave_w, 0, j)
    load(at_pair, pair_w, 0, 0)
    load(at_pair + 1, pair_w, 0, 1)
    load(at_mixer, mixer_w, 0, 0)
    for b in range(NFFN):
        for j in range(nff):
            load(at_ff + b * nff + j, expand_w.at[b], 0, j)
            load(at_shrink + b * nff + j, shrink_w.at[b], j, 0)

    def gain(n):
        return small[0:1, at(n)]

    def bias(n):
        return small[1:2, at(n)]

    tail = (2 + NFFN) * breadth
    gain_out, bias_out = small[0:1, tail:], small[1:2, tail:]
    lane = lax.broadcasted_iota(jnp.int32, (1, breadth), 1)
    of_head = [(lane // SHD) == h for h in range(SHEADS)]
    loads[2].wait()
    for start in range(0, tokens, ROWS_FF):
        r = slice(start, start + ROWS_FF)
        low = inputs_v[r].astype(BF)
        low_v[r] = low
        both = dot(low, wide_w[...])
        narrow, value = both[:, :breadth], both[:, breadth:]
        narrow_v[r] = narrow
        first = narrow * gain(0) + bias(0)
        first_v[r] = first
        pair = dot(first.astype(BF), pair_w[...])
        query, key = pair[:, :breadth], pair[:, breadth:]
        query_v[r, :breadth] = query.astype(BF)
        place = lax.broadcasted_iota(jnp.int32, (ROWS_FF, 1), 0) + start
        mask = jnp.where(place < length, 0.0, MASKED_SCORE)
        for h in range(SHEADS):
            key_m[h, r, :breadth] = jnp.where(of_head[h], key, 0.0).astype(BF)
            value_m[h, r, :breadth] = jnp.where(of_head[h], value, 0.0).astype(BF)
            of_part = (lane >= 1 + 3 * h) & (lane < 4 + 3 * h)
            less = jnp.where(of_part, -1.0, 0.0)
            key_m[h, r, breadth:] = jnp.where(lane == 0, mask, less).astype(BF)
            value_m[h, r, breadth:] = jnp.broadcast_to(less, (ROWS_FF, breadth)).astype(BF)
        query_v[r, breadth:] = jnp.broadcast_to(jnp.where(lane == 0, 1.0, 0.0), (ROWS_FF, breadth)).astype(BF)
        key_t[:, r] = key.T.astype(BF)
        value_t[:, r] = value.T.astype(BF)
    scale = SHD**-0.5
    scale2 = scale * LOG2E

    def extra_columns(mark, values):
        rows = [jnp.full((1, ATT), mark, F32)]
        for v in values:
            rows.extend(three_parts(v))
        rows.append(jnp.zeros((breadth - len(rows), ATT), F32))
        return jnp.concatenate(rows, 0).T.astype(BF)

    def forward(n, carry):
        r = pl.ds(pl.multiple_of(n * ATT, ATT), ATT)
        query = query_v[r]
        shifts, parts = [], []
        scores_v[0] = dot_nt(key_m[0], query)
        for h in range(SHEADS):
            if h + 1 < SHEADS:
                scores_v[(h + 1) % 2] = dot_nt(key_m[h + 1], query)
            scores, weight = scores_v.at[h % 2], weight_v.at[h % 2]
            top = column_max(scores)
            part = 0.0
            for c in split_rows(scores):
                piece = jnp.exp2((scores[c] - top) * scale2)
                weight[c] = piece.astype(BF)
                part = part + piece
            total = jnp.sum(part, 0, keepdims=True)
            shifts.append(top + jnp.log2(total) * (1.0 / scale2))
            parts.append(dot(value_t[h * SHD : (h + 1) * SHD], weight[...]) * (1.0 / total))
        mixed = jnp.concatenate(parts, 0)
        context_t[:, r] = mixed
        contextlow_t[:, r] = mixed.astype(BF)
        query_v[r, breadth:] = extra_columns(1.0, shifts)
        return carry

    lax.fori_loop(0, tokens // ATT, forward, 0)

    def row_sums(n, d, value):
        small_v[0:1, at(n)] += jnp.sum(d * value, 0, keepdims=True)
        small_v[1:2, at(n)] += jnp.sum(d, 0, keepdims=True)

    part = ROWS_FF // 2

    def feed(n, loss):
        both = range(2)
        rows = [pl.ds(pl.multiple_of(n * ROWS_FF + p * part, part), part) for p in both]
        inside = [slice(p * part, (p + 1) * part) for p in both]
        place = lax.broadcasted_iota(jnp.int32, (part, 1), 0)
        weight = [jnp.where(place + (n * ROWS_FF + p * part) < length, inverse, 0.0) for p in both]
        mixed_sum = [
            dot(context_t[:, rows[p]].T.astype(BF), mixer_w[...]) + first_v[rows[p]] for p in both
        ]
        current = [mixed_sum[p] * gain(1) + bias(1) for p in both]
        for b in range(NFFN):
            for p in both:
                blocklow_v[b, inside[p]] = current[p].astype(BF)
            hidden = [
                jnp.maximum(dot(blocklow_v[b, inside[p]], expand_w[b]), 0.0).astype(BF) for p in both
            ]
            for p in both:
                hidden_v[b, inside[p]] = hidden[p]
            total = [dot(hidden[p], shrink_w[b]) + current[p] for p in both]
            for p in both:
                sum_v[b, inside[p]] = total[p]
            current = [total[p] * gain(2 + b) + bias(2 + b) for p in both]
        joined = [dot(current[p].astype(BF), leave_w[...]) + inputs_v[rows[p]] for p in both]
        d = []
        for p in both:
            feature_rows = jnp.concatenate([dweight_v[0, rows[p]], dweight_v[1, rows[p]]], 1)
            differ = joined[p] * gain_out + bias_out - feature_rows
            square = jnp.mean(differ * differ, -1, keepdims=True)
            loss = loss + jnp.sum(weight[p] * square, 0, keepdims=True)
            outer = differ * (weight[p] * (2.0 / HID))
            small_v[0:1, tail:] += jnp.sum(outer * joined[p], 0, keepdims=True)
            small_v[1:2, tail:] += jnp.sum(outer, 0, keepdims=True)
            back = (outer * gain_out).astype(BF)
            g_leave[...] += dot(current[p].T.astype(BF), back)
            d.append(dot_nt(back, leave_w[...]))
        for b in reversed(range(NFFN)):
            d_sum = []
            for p in both:
                row_sums(2 + b, d[p], sum_v[b, inside[p]])
                d_sum.append(d[p] * gain(2 + b))
            d_hidden = [dot_nt(d_sum[p].astype(BF), shrink_w[b]) for p in both]
            for p in both:
                hidden = hidden_v[b, inside[p]]
                d_before = jnp.where(hidden > 0, d_hidden[p], 0.0).astype(BF)
                d[p] = d_sum[p] + dot_nt(d_before, expand_w[b])
                g_shrink[b] += dot(d_sum[p].T.astype(BF), hidden)
                g_expand[b] += dot(blocklow_v[b, inside[p]].T, d_before)
        for p in both:
            r = rows[p]
            row_sums(1, d[p], mixed_sum[p])
            d_sum = d[p] * gain(1)
            dsum_v[r] = d_sum
            d_mixed = d_sum.astype(BF)
            g_mixer[...] += dot(contextlow_t[:, r], d_mixed)
            d_context = dot_nt(d_mixed, mixer_w[...])
            dcontext_v[r, :breadth] = d_context.astype(BF)
            dcontext_t[:, r] = d_context.astype(BF).astype(F32).T
        return loss

    for c in loads[3:]:
        c.wait()
    loss = lax.fori_loop(0, tokens // ROWS_FF, feed, jnp.zeros((1, 1), F32))
    n_rest = at_mixer
    tiles_v[0] = g_mixer[...].astype(BF)
    for j in range(nin):
        tiles_v[at_leave - n_rest + j] = g_leave[:, at(j)].astype(BF)
    for b in range(NFFN):
        for j in range(nff):
            tiles_v[at_ff - n_rest + b * nff + j] = g_expand[b, :, at(j)].astype(BF)
            tiles_v[at_shrink - n_rest + b * nff + j] = g_shrink[b, :, at(j)].T.astype(BF)
    nothing = tiles_v.shape[0] - 1
    tiles_v[nothing] = jnp.zeros((breadth, breadth), BF)
    z, y, x = row // plane, (row // side) % side, row % side
    mine = pl.multiple_of(core * lines, lines)
    theirs = pl.multiple_of((1 - core) * lines, lines)
    my_half, their_half = core * slots * blocks, (1 - core) * slots * blocks
    straight = core == 0
    a, b_ = jnp.where(straight, x, y), jnp.where(straight, y, x)
    mate_a = b_

    def lay(n, carry):
        per = where_at.shape[2]
        which = where_at[6 + 2 * (n // per), 0, n % per]
        zz, yy, xx = of_row(n // slots)
        tile = tiles_v[which].reshape(2 * blocks, 16, breadth)
        pool[zz, yy, xx, pl.ds(n % slots * blocks, blocks)] = tile[:blocks]
        pool[zz, yy, xx, pl.ds((slots + n % slots) * blocks, blocks)] = tile[blocks:]
        return carry

    lax.fori_loop(0, n_rows * slots, lay, 0)
    pl.semaphore_wait(barrier, n_rows)

    def row_at(xx, yy, zz):
        return zz * plane + yy * side + xx

    def along_a(aa):
        return (jnp.where(straight, row_at(aa, y, z), row_at(x, aa, z)), core)

    def along_b(bb):
        return (jnp.where(straight, row_at(x, bb, z), row_at(bb, y, z)), core)

    def along_z(zz):
        return (row_at(x, y, zz), core)

    def remote(src, dst, send, recv, peer):
        return pltpu.make_async_remote_copy(
            src_ref=src,
            dst_ref=dst,
            send_sem=send,
            recv_sem=recv,
            device_id=peer,
            device_id_type=MESH,
        )

    order = list(range(1, side)) + [0]
    for d in order:
        piece = lax.rem(mate_a + d, side)
        half = pl.ds(their_half, slots * blocks)
        by_y = remote(pool.at[:, piece, :, half], pair_in.at[d], pair_send.at[d], pair_recv.at[d], mate)
        by_x = remote(pool.at[:, :, piece, half], pair_in.at[d], pair_send.at[d], pair_recv.at[d], mate)

        @pl.when(straight)
        def _():
            by_y.start()

        @pl.when(jnp.logical_not(straight))
        def _():
            by_x.start()

    def pair_copy(d):
        return remote(pool.at[:, 0, :, pl.ds(0, slots * blocks)], pair_in.at[d], pair_send.at[d], pair_recv.at[d], mate)

    first_copies, second_copies, third_copies = [], [], []

    def add_pair():
        for d in order:
            pair_copy(d).wait_recv()
            aa = lax.rem(a + d, side)

            def add(i, carry):
                zz, bb = i // side, i % side
                xx, yy = jnp.where(straight, aa, bb), jnp.where(straight, bb, aa)
                own = pool[zz, yy, xx, pl.ds(my_half, slots * blocks)].astype(F32)
                pair_in[d, zz, bb] = (own + pair_in[d, zz, bb].astype(F32)).astype(BF)
                return carry

            lax.fori_loop(0, deep * side, add, 0)
            if d:
                c = remote(pair_in.at[d], first_in.at[d - 1], first_send.at[d - 1], first_recv.at[d - 1], along_a(aa))
                c.start()
                first_copies.append(c)

    def add_first():
        for c in first_copies:
            c.wait_recv()
        for d in order:
            bb = lax.rem(b_ + d, side)

            def add(zz, carry):
                s = pair_in[0, zz, bb].astype(F32)
                for j in range(side - 1):
                    s = s + first_in[j, zz, bb].astype(F32)
                second[d, zz] = s.astype(BF)
                return carry

            lax.fori_loop(0, deep, add, 0)
            if d:
                c = remote(second.at[d], second_in.at[d - 1], second_send.at[d - 1], second_recv.at[d - 1], along_b(bb))
                c.start()
                second_copies.append(c)

    def add_second():
        for c in second_copies:
            c.wait_recv()
        for d in list(range(1, deep)) + [0]:
            zz = lax.rem(z + d, deep)
            s = second[0, zz].astype(F32)
            for j in range(side - 1):
                s = s + second_in[j, zz].astype(F32)
            if d:
                third[d - 1] = s.astype(BF)
                c = remote(third.at[d - 1], third_in.at[d - 1], third_send.at[d - 1], third_recv.at[d - 1], along_z(zz))
                c.start()
                third_copies.append(c)
            else:
                half_own[...] = s.reshape(half_own.shape)

    def add_third():
        for c in third_copies:
            c.wait_recv()
        s = half_own[...]
        for j in range(deep - 1):
            s = s + third_in[j].astype(F32).reshape(half_own.shape)
        half_own[...] = s
        half_copy.start()

    half_copy = remote(half_own, half_in, half_send, half_recv, mate)
    stages = [add_pair, add_first, add_second]

    log_share = jnp.log2(inverse * (1.0 / SHEADS))

    def backward(n, loss):
        r = slice(n * ATT, (n + 1) * ATT)
        place = lax.broadcasted_iota(jnp.int32, (1, ATT), 1) + n * ATT
        inside = place < length
        share = jnp.where(inside, inverse * (1.0 / SHEADS), 0.0)
        share2 = jnp.where(inside, log_share, MASKED_SCORE)
        less = []
        for h in range(SHEADS):
            heads = slice(h * SHD, (h + 1) * SHD)
            along = jnp.sum(context_t[heads, r] * dcontext_t[heads, r], 0, keepdims=True)
            less.append(along - share * sums[h, :, r])
        dcontext_v[r, breadth:] = extra_columns(0.0, less)
        query, d_context = query_v[r], dcontext_v[r]
        logs_copy(n).wait()
        here = logs_v.at[n % 2]

        def products(h):
            scores_v[h % 2] = dot_nt(key_m[h], query)
            dweight_v[h % 2] = dot_nt(value_m[h], d_context)

        products(0)
        parts = []
        gap = 0.0
        for h in range(SHEADS):
            if h + 1 < SHEADS:
                products(h + 1)
            scores, dweight = scores_v.at[h % 2], dweight_v.at[h % 2]
            weight, dscores = weight_v.at[h % 2], dscores_v.at[h % 2]
            for c in split_rows(scores):
                score = scores[c]
                piece = jnp.exp2(score * scale2)
                weight[c] = piece.astype(BF)
                target_log = here[h, c].astype(F32)
                target = jnp.exp2(target_log * LOG2E + share2)
                gap = gap + target * (target_log - score * scale)
                dscores[c] = (piece * dweight[c] - target).astype(BF)
            none = jnp.zeros((ATT, breadth), BF)
            dvalue_v[...] += dot(weight[...], jnp.where(of_head[h], d_context[:, :breadth], none))
            dkey_v[...] += dot(dscores[...], jnp.where(of_head[h], query[:, :breadth], none))
            parts.append(dot(key_t[h * SHD : (h + 1) * SHD], dscores[...]))
        dpair_v[r, at(0)] = (jnp.concatenate(parts, 0) * scale).T.astype(BF)
        if n + 2 < tokens // ATT:
            logs_copy(n + 2).start()
        return loss + jnp.sum(jnp.sum(gap, 0, keepdims=True), 1, keepdims=True)

    for n in range(tokens // ATT):
        loss = backward(n, loss)
        if n < len(stages):
            stages[n]()
    dpair_v[:, at(1)] = (dkey_v[...] * scale).astype(BF)
    d_pair = dpair_v[...]
    d_first = dsum_v[...] + dot_nt(d_pair, pair_w[...])
    row_sums(0, d_first, narrow_v[...])
    g_pair = dot(first_v[...].T.astype(BF), d_pair)
    wide_t = jnp.concatenate([(d_first * gain(0)).T.astype(BF), dvalue_v[...].T.astype(BF)], 0)
    g_wide = dot(wide_t, low_v[...])
    n_lines = small.shape[1] // breadth
    lines_v[...] = jnp.zeros_like(lines_v)
    for j in range(n_lines):
        lines_v[j : j + 1] = small_v[0:1, at(j)]
        lines_v[n_lines + j : n_lines + j + 1] = small_v[1:2, at(j)]
    lines_v[2 * n_lines : 2 * n_lines + 1, 0:1] = loss
    add_third()
    summed = half_own[...]
    lines_v[2 * n_lines + 1 : 2 * n_lines + 2] = jnp.sum(summed * summed, 0, keepdims=True)
    groups = lines_v.shape[0] // 8
    top = 16 * groups
    each = n_rest // 2

    def two_parts(value):
        high = value.astype(BF)
        return high, (value - high.astype(F32)).astype(BF)

    for g in range(groups):
        high, rest = two_parts(lines_v[8 * g : 8 * g + 8])
        rest_v[0, 16 * g : 16 * g + 8] = high
        rest_v[0, 16 * g + 8 : 16 * g + 16] = rest

    def keep(n, value):
        line = top + (n % each) * breadth
        rest_v[n // each, line : line + breadth] = value.astype(BF)

    for j in range(nin):
        keep(j, g_wide[:breadth, at(j)].T)
        keep(nin + j, g_wide[breadth:, at(j)].T)
    keep(at_pair, g_pair[:, at(0)])
    keep(at_pair + 1, g_pair[:, at(1)])
    swap = remote(rest_v.at[1 - core], rest_in, swap_send, swap_recv, mate)
    swap.start()
    swap.wait()
    rest_sum[...] = (rest_v[core].astype(F32) + rest_in[...].astype(F32)).astype(BF)
    for g in range(groups):
        high_at, rest_at = slice(16 * g, 16 * g + 8), slice(16 * g + 8, 16 * g + 16)
        value = rest_v[core, high_at].astype(F32) + rest_v[core, rest_at].astype(F32)
        value = value + rest_in[high_at].astype(F32) + rest_in[rest_at].astype(F32)
        rest_sum[high_at], rest_sum[rest_at] = two_parts(value)
    chunk = rest_part.shape[1]

    def lines_of(n):
        return pl.ds(pl.multiple_of(n * chunk, chunk), chunk)

    def part_copy(d):
        to = lax.rem(row + d, n_rows)
        return remote(rest_sum.at[lines_of(to)], rest_part.at[d - 1], part_send.at[d - 1], part_recv.at[d - 1], (to, core))

    def all_copy(d):
        here = rest_all.at[core, lines_of(row)]
        return remote(here, here, all_send.at[d - 1], all_recv.at[d - 1], (lax.rem(row + d, n_rows), core))

    def each_peer(act):
        def one(d, carry):
            act(d)
            return carry

        lax.fori_loop(1, n_rows, one, 0)

    each_peer(lambda d: part_copy(d).start())
    each_peer(lambda d: part_copy(d).wait())
    total = lax.fori_loop(
        0, n_rows - 1, lambda d, t: t + rest_part[d].astype(F32), rest_sum[lines_of(row)].astype(F32)
    )
    high_of = []
    for g in range(chunk // 16):
        piece = total[16 * g : 16 * g + 16]
        high, rest = two_parts(piece[:8] + piece[8:])
        split = jnp.concatenate([high.astype(F32), rest.astype(F32)], 0)
        high_of.append(jnp.where(row * (chunk // 16) + g < groups, split, piece))
    rest_all[core, lines_of(row)] = jnp.where(core == 0, jnp.concatenate(high_of, 0), total).astype(BF)
    each_peer(lambda d: all_copy(d).start())
    half_copy.wait()
    for k in range(slots):
        summed_out[k, pl.ds(mine, lines)] = half_own[k * lines : (k + 1) * lines]
        summed_out[k, pl.ds(theirs, lines)] = half_in[k * lines : (k + 1) * lines]
    each_peer(lambda d: all_copy(d).wait())
    over = remote(rest_all.at[core], rest_all.at[core], over_send, over_recv, mate)
    over.start()
    for d in order:
        pair_copy(d).wait_send()
    for c in first_copies + second_copies + third_copies:
        c.wait_send()
    over.wait()
    squares = jnp.zeros((1, breadth), F32)
    for n in range(n_rest):
        line = top + (n % each) * breadth
        rest_out[n] = rest_all[n // each, line : line + breadth]
        tile = rest_out[n].astype(F32)
        squares = squares + jnp.sum(tile * tile, 0, keepdims=True)
    for g in range(groups):
        high = rest_all[0, 16 * g : 16 * g + 8].astype(F32)
        lines_out[8 * g : 8 * g + 8] = high + rest_all[0, 16 * g + 8 : 16 * g + 16].astype(F32)
    lines_out[2 * n_lines + 2 : 2 * n_lines + 3] = squares


def student(where_at, bounds, micro_batch, inputs, feature, logs, sums, tiles_own, tiles_mate, small, slots):
    tokens = inputs.shape[0]
    n_rows, w = tiles_own.shape[0], tiles_own.shape[-1]
    deep = 4
    side = math.isqrt(n_rows // deep)
    assert side * side * deep == n_rows
    n_lines = 8 * -(-(2 * small.shape[1] // w + 3) // 8)
    n_rest = 2 * HID // w + 2
    n_tiles = 1 + 2 * NFFN * (SFF // w) + HID // w
    half = w // 2
    in_half = 2 * n_lines + (HID // w + 1) * w
    chunk = 16 * -(-in_half // (16 * n_rows))
    s1, d1 = side - 1, deep - 1
    gathered = (deep, side, side) + tiles_own.shape[1:]
    tiles_own, tiles_mate = tiles_own.reshape(gathered), tiles_mate.reshape(gathered)
    blocks = slots * half // 16
    D = pltpu.SemaphoreType.DMA

    def low(*shape):
        return pltpu.VMEM(shape, BF)

    def full(*shape):
        return pltpu.VMEM(shape, F32)

    return pl.pallas_call(
        functools.partial(student_kernel, side, deep),
        out_shape=(
            jax.ShapeDtypeStruct((slots, w, w), F32),
            jax.ShapeDtypeStruct((n_rest, w, w), BF),
            jax.ShapeDtypeStruct((n_lines, w), F32),
        ),
        in_specs=[SMEM] * 3 + [ANY, ANY, ANY, VMEM, ANY, ANY, VMEM],
        out_specs=(VMEM, VMEM, VMEM),
        scratch_shapes=[
            full(tokens, HID),
            low(2, SHEADS, tokens, ATT),
            low(HID, 2 * w),
            low(w, 2 * w),
            low(w, w),
            low(NFFN, w, SFF),
            low(NFFN, SFF, w),
            low(w, HID),
            low(tokens, HID),
            full(tokens, w),
            full(tokens, w),
            low(tokens, 2 * w),
            low(SHEADS, tokens, 2 * w),
            low(SHEADS, tokens, 2 * w),
            low(w, tokens),
            low(w, tokens),
            full(w, tokens),
            low(w, tokens),
            low(NFFN, ROWS_FF, w),
            low(NFFN, ROWS_FF, SFF),
            full(NFFN, ROWS_FF, w),
            full(tokens, w),
            low(tokens, 2 * w),
            full(w, tokens),
            full(tokens, w),
            full(tokens, w),
            low(tokens, 2 * w),
            full(2, tokens, ATT),
            full(2, tokens, ATT),
            low(2, tokens, ATT),
            low(2, tokens, ATT),
            full(w, HID),
            full(w, w),
            full(NFFN, w, SFF),
            full(NFFN, w, SFF),
            full(8, small.shape[1]),
            low(n_tiles + 1, w, w),
            low(deep, side, side, 2 * tiles_own.shape[-3], 16, w),
            low(side, deep, side, blocks, 16, w),
            low(s1, deep, side, blocks, 16, w),
            low(side, deep, blocks, 16, w),
            low(s1, deep, blocks, 16, w),
            low(d1, blocks, 16, w),
            low(d1, blocks, 16, w),
            full(slots * half, w),
            full(slots * half, w),
            low(2, chunk * n_rows, w),
            low(chunk * n_rows, w),
            low(chunk * n_rows, w),
            low(n_rows - 1, chunk, w),
            low(2, chunk * n_rows, w),
            full(n_lines, w),
            D((5,)),
            D((2,)),
            D((side,)),
            D((side,)),
            D((s1,)),
            D((s1,)),
            D((s1,)),
            D((s1,)),
            D((d1,)),
            D((d1,)),
            D,
            D,
            D,
            D,
            D((n_rows - 1,)),
            D((n_rows - 1,)),
            D((n_rows - 1,)),
            D((n_rows - 1,)),
            D,
            D,
        ],
        compiler_params=pltpu.CompilerParams(
            collective_id=0, has_side_effects=True, vmem_limit_bytes=63 << 20
        ),
        cost_estimate=pl.CostEstimate(
            flops=15_000_000_000, bytes_accessed=16 << 20, transcendentals=0
        ),
    )(where_at, bounds, micro_batch, inputs, feature, logs, sums, tiles_own, tiles_mate, small)


def update_kernel(
    n_tiles, where_at, step, own, summed, rest, lines, weight_in, first_in, second_in, small, small_first, small_second,
    loss_out, norm_out, tiles_out, first_out, second_out, small_out, small_first_out, small_second_out, small_grad_out,
    small_v, weight, first, second, sem,
):
    pairs = ((weight_in, weight), (first_in, first), (second_in, second))
    loads = [pltpu.make_async_copy(a, b, sem.at[n]) for n, (a, b) in enumerate(pairs)]
    for c in loads:
        c.start()
    breadth = summed.shape[2]
    n_lines = small.shape[1] // breadth
    steps = step[0]
    first_fix = 1.0 - lax.fori_loop(0, steps, lambda i, p: p * BETA_FIRST, jnp.float32(1.0))
    second_fix = 1.0 - lax.fori_loop(0, steps, lambda i, p: p * BETA_SECOND, jnp.float32(1.0))

    def adam(w, m, v, g, decay):
        m = BETA_FIRST * m + (1.0 - BETA_FIRST) * g
        v = BETA_SECOND * v + (1.0 - BETA_SECOND) * g * g
        change = m / first_fix / (jnp.sqrt(v / second_fix) + ADAM_EPSILON) + decay * w
        return w - LEARN_RATE * change, m, v

    line = lambda n: lines[n : n + 1]
    squares = line(2 * n_lines + 1) + line(2 * n_lines + 2)
    for n in range(2 * n_lines):
        squares = squares + line(n) * line(n)
    norm = jnp.sqrt(jnp.sum(squares, 1, keepdims=True))
    norm_out[...] = norm
    loss_out[...] = line(2 * n_lines)[:, 0:1]
    factor = CLIP_NORM / jnp.maximum(norm, CLIP_NORM)
    for n in range(n_lines):
        cols = slice(n * breadth, (n + 1) * breadth)
        small_v[0:1, cols] = line(n)
        small_v[1:2, cols] = line(n_lines + n)
    small_grad = small_v[0:2] * factor
    small_grad_out[...] = small_grad
    w, m, v = adam(small[...], small_first[...], small_second[...], small_grad, 0.0)
    small_out[...] = w
    small_first_out[...] = m
    small_second_out[...] = v

    slots, n_rest = summed.shape[0], rest.shape[0]
    for c in loads:
        c.wait()
    for s in range(summed.shape[0]):
        at = own[0] * slots + s
        which = where_at[5 + 2 * (at // 128), 0, at % 128]
        keep = which < n_tiles
        other = rest[jnp.minimum(which, n_rest - 1)].astype(F32)
        total = summed[s] + jnp.where(which < n_rest, other, 0.0)
        w, m, v = adam(weight[s], first[s], second[s], total * factor, WEIGHT_DECAY)
        tiles_out[s] = jnp.where(keep, w, 0.0)
        first_out[s] = jnp.where(keep, m, 0.0)
        second_out[s] = jnp.where(keep, v, 0.0)


def update(n_tiles, where_at, step, own, summed, rest, lines, weight, first, second, small, small_first, small_second):
    one = jax.ShapeDtypeStruct((1, 1), F32)
    tile = jax.ShapeDtypeStruct(weight.shape, F32)
    row = jax.ShapeDtypeStruct(small.shape, F32)
    return pl.pallas_call(
        functools.partial(update_kernel, n_tiles),
        out_shape=(one, one, tile, tile, tile, row, row, row, row),
        in_specs=[SMEM] * 3 + [VMEM] * 3 + [HBM] * 3 + [VMEM] * 3,
        out_specs=(VMEM,) * 9,
        scratch_shapes=[pltpu.VMEM((8, small.shape[1]), F32)]
        + [pltpu.VMEM(weight.shape, F32)] * 3
        + [pltpu.SemaphoreType.DMA((3,))],
        compiler_params=pltpu.CompilerParams(vmem_limit_bytes=63 << 20),
        cost_estimate=pl.CostEstimate(flops=2_000_000, bytes_accessed=2 << 20, transcendentals=0),
    )(where_at, step, own, summed, rest, lines, weight, first, second, small, small_first, small_second)


def on_device(
    token_ids,
    bounds,
    micro_batch,
    owners,
    step_count,
    word_table,
    conv_weight,
    embed_extra,
    teacher_entry,
    teacher_project,
    teacher_mixer,
    teacher_expand,
    teacher_shrink,
    teacher_leave,
    teacher_norms,
    tile_weight,
    tile_first,
    tile_second,
    small_weight,
    small_first,
    small_second,
):
    core = lax.axis_index("heads")
    n_rows = lax.axis_size("rows")
    assert token_ids.shape[0] == lax.axis_size("heads")
    row_ids = lax.dynamic_index_in_dim(token_ids, core, 0, keepdims=False)
    words = word_table.at[row_ids].get(mode="promise_in_bounds")
    inputs, feature, logs, sums, where_at, tiles_own, tiles_mate = teacher(
        n_rows,
        bounds,
        micro_batch,
        owners,
        words,
        conv_weight,
        embed_extra,
        teacher_norms,
        tile_weight,
        teacher_entry,
        teacher_project.transpose(1, 0, 2),
        teacher_mixer,
        teacher_expand,
        teacher_shrink,
        teacher_leave,
    )
    summed, rest, lines = student(
        where_at,
        bounds,
        micro_batch,
        inputs,
        feature,
        logs,
        sums,
        tiles_own,
        tiles_mate,
        small_weight,
        tile_weight.shape[0],
    )
    own = lax.axis_index("rows")[None]
    loss, norm, *rest = update(
        owners.shape[0],
        where_at,
        step_count,
        own,
        summed,
        rest,
        lines,
        tile_weight,
        tile_first,
        tile_second,
        small_weight,
        small_first,
        small_second,
    )
    return (loss[0, 0], norm[0, 0], *rest)


def solution(mesh):
    placed = (
        P("rows", None),
        P("rows", None),
        P("rows"),
        P(),
        P(),
        P(),
        P(),
        P(),
        P(),
        P(None, None, "heads"),
        P("heads", None),
        P(None, "heads"),
        P("heads", None),
        P(),
        P(),
        P("rows", None, None),
        P("rows", None, None),
        P("rows", None, None),
        P(),
        P(),
        P(),
    )
    tiles = P("rows", None, None)
    return jax.shard_map(
        on_device,
        mesh=mesh,
        in_specs=placed,
        out_specs=(P(), P(), tiles, tiles, tiles, P(), P(), P(), P()),
        check_vma=False,
    )
```
